32 devices in a mesh: dp: 8 (over y, x, core), tensor: 4 (over z).
Axes of the slice: x: 2, y: 2, z: 4, core: 2. Of those that a mesh axis runs over, the one named last changes fastest.
Arguments:
- tokens: bfloat16 [2048, 4096], P(('dp', 'tensor')), may hold values from -110 to 110
- norm_gain: bfloat16 [4096], replicated, may hold values from 0.099609375 to 1.8984375
- query_weight: bfloat16 [4096, 4096], P('dp', 'tensor'), may hold values from -1 to 1
- kv_weight: bfloat16 [4096, 1024], P('dp', 'tensor'), may hold values from -1 to 1
- out_weight: bfloat16 [4096, 4096], P('tensor', 'dp'), may hold values from -0.09375 to 0.09375
- grad_out: bfloat16 [2048, 4096], P(('dp', 'tensor')), may hold values from -6 to 6
- doc_lengths: int32 [8, 4], P('dp'), may hold values from 1 to 128, 256 in all within a row
Outputs:
- input_grad: bfloat16 [2048, 4096], P(('dp', 'tensor'))
- query_weight_grad: float32 [4096, 4096], P('dp', 'tensor')
- kv_weight_grad: float32 [4096, 1024], P('dp', 'tensor')
The draws below stay inside these ranges and needn't reach their ends.
Inputs may be any that keep to these rules, and one draw needn't show every extreme that they name: `doc_lengths`: each row sums to 256.
All inputs are finite; a program needn't handle non-finite values.
Results may differ from the reference program's by a relative error of at most 0.025.
Values may be sent and summed in bfloat16 or wider, within the bound.
No kernel may reach another device: no remote copies, remote signals or barrier semaphores. Data moves between devices by JAX's collectives and lax.ppermute only.
A program may use at most 64 MiB of HBM per device.

```python
import math
import jax
import jax.numpy as jnp
import numpy as np
from jax import lax

D = 4096
H = 32
KVH = 4
HD = 128
SEQ = 256
NDOC = 4
REPLICAS = 8
TOKENS = 2048
N_DP = 8
N_TENSOR = 4


def draw_tokens(key, part):
    noise = jax.random.truncated_normal(jax.random.fold_in(key, 1), -4.0, 4.0, (TOKENS, D), jnp.float32)
    pairing = jax.random.permutation(jax.random.fold_in(key, 2), N_DP)
    replica = jnp.arange(TOKENS) // SEQ
    column_block = jnp.arange(D) // (D // N_DP)
    spiked = jnp.where(pairing[replica][:, None] == column_block[None, :], 3.0, 1.0)
    rough = noise * spiked
    return rough.astype(jnp.bfloat16)


def drawn_weight(key, column_count):
    return jax.random.truncated_normal(jax.random.fold_in(key, 22), -3.0, 3.0, (D, column_count), jnp.float32) / math.sqrt(D)


def draw_query_weight(key, part):
    return drawn_weight(jax.random.fold_in(key, 31), H * HD).astype(jnp.bfloat16)


def draw_kv_weight(key, part):
    return drawn_weight(jax.random.fold_in(key, 32), 2 * KVH * HD).astype(jnp.bfloat16)


def level_of(rng, extent, shards, low, high):
    level = 1.0
    for dim, blocks in shards:
        heights = jax.random.uniform(jax.random.fold_in(jax.random.fold_in(rng, 6), dim), (blocks,), jnp.float32, low / len(shards), high / len(shards))
        level = level * jnp.repeat(jnp.exp(heights), extent[dim] // blocks).reshape((-1,) + (1,) * (len(extent) - 1 - dim))
    return level


def profile(number_of, total, most, skew):
    loads = [(1 << 20) // math.isqrt(standing ** skew) + 1 for standing in range(2, number_of + 1)]
    spare, counts = total - most - (number_of - 1), [1] * (number_of - 1)
    while spare > 0:
        movable = [i for i in range(number_of - 1) if counts[i] < most]
        mass, budget = sum([loads[i] for i in movable]), spare
        for i in movable:
            extra = min(most - counts[i], max(1, budget * loads[i] // mass), spare)
            counts[i] = counts[i] + extra
            spare = spare - extra
    return np.array([most] + counts)


def ragged_sizes(stream_key, count, total, limit, lean):
    if count == 2:
        one = jax.random.randint(stream_key, (), max(1, total - limit), min(limit, total - 1) + 1)
        return jnp.stack([one, total - one])
    sizes = jnp.asarray(profile(count, total, limit, lean), jnp.int32)
    twos = (count - 1) // 2
    source_of, taker = sizes[1:1 + 2 * twos:2], sizes[2:2 + 2 * twos:2]
    slack = jnp.minimum(source_of - 1, limit - taker)
    shifted = jax.random.randint(jax.random.fold_in(stream_key, 1), (twos,), 0, 1 << 20) % (slack + 1)
    sizes = sizes.at[1:1 + 2 * twos:2].set(source_of - shifted).at[2:2 + 2 * twos:2].set(taker + shifted)
    return sizes[jax.random.permutation(jax.random.fold_in(stream_key, 2), count)]


def scatter_about(key, shape, scale, bound, shards=(), kind=jnp.bfloat16):
    factor_of = level_of(key, shape, shards, -0.22, 0.18) if shards else 1.0
    values = jax.random.normal(key, shape, jnp.float32) * scale * factor_of
    return jnp.minimum(jnp.maximum(values, -bound), bound).astype(kind)


def setup_inputs(seed: int = 0) -> dict:
    arg_keys = jax.random.split(jax.random.key(seed), 8)
    tokens = draw_tokens(jax.random.fold_in(arg_keys[7], 71), 0)
    norm_gain = jnp.clip(1.0 + 0.18 * jax.random.normal(arg_keys[1], (D,), jnp.float32), 0.099609375, 1.8984375).astype(jnp.bfloat16)
    query_weight = draw_query_weight(jax.random.fold_in(arg_keys[7], 71), 0)
    kv_weight = draw_kv_weight(jax.random.fold_in(arg_keys[7], 71), 0)
    out_weight = scatter_about(arg_keys[4], (H * HD, D), (H * HD) ** -0.5, 0.09375, ((0, 4), (1, 8)))
    grad_out = scatter_about(arg_keys[5], (TOKENS, D), 1.0, 6.0, ((0, 32),))
    doc_lengths = jax.vmap(lambda own: ragged_sizes(own, NDOC, SEQ, SEQ // 2, 0))(jax.random.split(arg_keys[6], REPLICAS)).reshape((REPLICAS, NDOC)).astype(jnp.int32)
    return {"tokens": tokens, "norm_gain": norm_gain, "query_weight": query_weight, "kv_weight": kv_weight, "out_weight": out_weight, "grad_out": grad_out, "doc_lengths": doc_lengths}


epsilon = 1e-05

def rounded(value):
    return lax.optimization_barrier(value.astype(jnp.bfloat16)).astype(jnp.float32)

def document_mask(lengths, length_total):
    ends = jnp.cumsum(lengths.astype(jnp.int32)).astype(jnp.int32)
    positions = jnp.arange(length_total, dtype=jnp.int32)
    labels = lax.optimization_barrier(jnp.sum((ends[None, :] <= positions[:, None]).astype(jnp.int32), axis=1))
    return (labels[:, None] == labels[None, :]) & (positions[None, :] <= positions[:, None])

def reference(tokens, norm_gain, query_weight, kv_weight, out_weight, grad_out, doc_lengths):
    group = H // KVH
    query_cols = H * HD // N_TENSOR
    kv_cols = 2 * HD * KVH // N_TENSOR
    gain32 = norm_gain.astype(jnp.float32)
    query_blocks = query_weight.astype(jnp.float32).reshape(D, N_TENSOR, query_cols)
    kv_blocks = kv_weight.astype(jnp.float32).reshape(D, N_TENSOR, kv_cols)

    def replica(carry, inputs):
        row_block, grad_block, lengths = inputs
        values32 = row_block.astype(jnp.float32)
        root_mean = jnp.sqrt(lax.optimization_barrier(jnp.mean(values32 * values32, axis=-1)) + epsilon)
        unit = values32 / root_mean[:, None]
        normed = (unit * gain32).astype(jnp.bfloat16)
        queries = jnp.dot(normed, query_weight, preferred_element_type=jnp.float32).astype(jnp.bfloat16)
        keyvals = jnp.dot(normed, kv_weight, preferred_element_type=jnp.float32).astype(jnp.bfloat16)
        keyvals = keyvals.astype(jnp.float32).reshape(SEQ, KVH, 2, HD)
        key_rows = keyvals[:, :, 0]
        value_rows = keyvals[:, :, 1]
        grouped = queries.astype(jnp.float32).reshape(SEQ, KVH, group, HD)
        allowed = document_mask(lengths, SEQ)
        scores = jnp.einsum('qkgd,tkd->kgqt', grouped, key_rows) / math.sqrt(HD)
        scores = jnp.where(allowed, scores, -1e+30)
        peak = lax.optimization_barrier(jnp.max(scores, axis=-1, keepdims=True))
        expo = jnp.exp(scores - peak)
        probs = expo / lax.optimization_barrier(jnp.sum(expo, axis=-1, keepdims=True))
        probs_low = rounded(probs)
        out_grad = jnp.dot(grad_block, out_weight.T, preferred_element_type=jnp.float32)
        out_heads = rounded(out_grad).reshape(SEQ, KVH, group, HD)
        prob_grad = jnp.einsum('qkgd,tkd->kgqt', out_heads, value_rows)
        inner = lax.optimization_barrier(jnp.sum(probs * prob_grad, axis=-1, keepdims=True))
        score_grad = rounded(probs * (prob_grad - inner) / math.sqrt(HD))
        query_grad = jnp.einsum('kgqt,tkd->qkgd', score_grad, key_rows).astype(jnp.bfloat16).reshape(SEQ, H * HD)
        key_grad = jnp.einsum('kgqt,qkgd->tkd', score_grad, grouped)
        value_grad = jnp.einsum('kgqt,qkgd->tkd', probs_low, out_heads)
        kv_grad = jnp.stack([key_grad, value_grad], axis=2).astype(jnp.bfloat16).reshape(SEQ, KVH * 2 * HD)
        query_parts = jnp.einsum('snc,dnc->nsd', query_grad.astype(jnp.float32).reshape(SEQ, N_TENSOR, query_cols), query_blocks)
        kv_parts = jnp.einsum('snc,dnc->nsd', kv_grad.astype(jnp.float32).reshape(SEQ, N_TENSOR, kv_cols), kv_blocks)
        normed_grad = lax.optimization_barrier(jnp.sum(rounded(query_parts + kv_parts), axis=0))
        scaled = normed_grad * gain32
        input_grad = (grad_block.astype(jnp.float32) + (scaled - unit * lax.optimization_barrier(jnp.mean(scaled * unit, axis=-1, keepdims=True))) / root_mean[:, None]).astype(jnp.bfloat16)
        query_wgrad = jnp.dot(normed.T, query_grad, preferred_element_type=jnp.float32)
        kv_wgrad = jnp.dot(normed.T, kv_grad, preferred_element_type=jnp.float32)
        return ((carry[0] + rounded(query_wgrad), carry[1] + rounded(kv_wgrad)), input_grad)
    start_sums = (jnp.zeros((D, H * HD), jnp.float32), jnp.zeros((D, 2 * KVH * HD), jnp.float32))
    sums, input_grads = lax.scan(replica, start_sums, (tokens.reshape(N_DP, SEQ, D), grad_out.reshape(N_DP, SEQ, D), doc_lengths))
    return (input_grads.reshape(TOKENS, D), sums[0] / N_DP, sums[1] / N_DP)
```

```python
import math

import jax
import jax.numpy as jnp
from jax import lax
from jax.sharding import PartitionSpec as P

KVH = 4
HD = 128

epsilon = 1e-05


def swap(value, axis, mask):
    pairs = [(source, source ^ mask) for source in range(lax.axis_size(axis))]
    return lax.ppermute(value, axis, pairs)


def gather_chips(value):
    chips = lax.axis_size("dp") // 2
    if chips != 4:
        return [value] + [swap(value, "dp", 2 * k) for k in range(1, chips)]
    half = value.shape[0] // 2
    near_x = swap(value, "dp", 2)
    near_y = swap(value, "dp", 4)
    far_top = swap(near_x[:half], "dp", 4)
    far_bottom = swap(near_y[half:], "dp", 2)
    return [value, near_x, near_y, jnp.concatenate([far_top, far_bottom], axis=0)]


def scatter_chips(blocks):
    chips = lax.axis_size("dp") // 2
    total = blocks[0].astype(jnp.float32)
    if chips != 4:
        for k in range(1, chips):
            total = total + swap(blocks[k], "dp", 2 * k).astype(jnp.float32)
        return total
    half = blocks[0].shape[0] // 2
    far_top = swap(blocks[3][:half], "dp", 4)
    far_bottom = swap(blocks[3][half:], "dp", 2)
    x_bottom = swap(blocks[1][half:], "dp", 2)
    y_top = swap(blocks[2][:half], "dp", 4)
    x_top = swap(blocks[1][:half] + far_top, "dp", 2)
    y_bottom = swap(blocks[2][half:] + far_bottom, "dp", 4)
    top = x_top.astype(jnp.float32) + y_top.astype(jnp.float32)
    bottom = x_bottom.astype(jnp.float32) + y_bottom.astype(jnp.float32)
    return total + jnp.concatenate([top, bottom], axis=0)


def gather_tensor(value):
    size = lax.axis_size("tensor")
    if size != 4:
        return [value] + [swap(value, "tensor", k) for k in range(1, size)]
    index = lax.axis_index("tensor")
    two = swap(value, "tensor", 2)
    one = swap(value, "tensor", 1)
    inner = lax.ppermute(value, "tensor", [(1, 2), (2, 1)])
    outer = lax.ppermute(two, "tensor", [(2, 3), (1, 0)])
    return [value, one, two, jnp.where((index == 1) | (index == 2), inner, outer)]


def scatter_tensor(blocks):
    size = lax.axis_size("tensor")
    total = blocks[0].astype(jnp.float32)
    if size != 4:
        for k in range(1, size):
            total = total + swap(blocks[k], "tensor", k).astype(jnp.float32)
        return total
    outer = lax.ppermute(blocks[3], "tensor", [(0, 1), (3, 2)])
    one = swap(blocks[1], "tensor", 1)
    inner = lax.ppermute(blocks[3], "tensor", [(1, 2), (2, 1)])
    two = swap(blocks[2] + outer, "tensor", 2)
    return total + one.astype(jnp.float32) + inner.astype(jnp.float32) + two.astype(jnp.float32)


def local(tokens, norm_gain, query_weight, kv_weight, out_weight, grad_out, doc_lengths):
    tensor_size = lax.axis_size("tensor")
    data_size = lax.axis_size("dp")
    tensor_index = lax.axis_index("tensor")
    data_index = lax.axis_index("dp")
    core, chip = data_index & 1, data_index >> 1
    chips = data_size // 2
    sharers = tensor_size // KVH
    levels = sharers.bit_length() - 1
    rows, width = tokens.shape
    block = width // data_size
    length = rows * tensor_size
    query_width = query_weight.shape[1]
    out_width = out_weight.shape[0]
    contract_last = (((1,), (1,)), ((), ()))

    def columns(value, which):
        starts = [((chip ^ k) * 2 + which) * block for k in range(chips)]
        return jnp.concatenate(
            [lax.dynamic_slice(value, (0, start), (value.shape[0], block)) for start in starts], axis=1
        )

    def share(value):
        handed = swap(columns(value, 1 - core), "dp", 1)
        return jnp.concatenate([columns(value, core), handed], axis=0)

    def all_rows(value):
        return jnp.stack(gather_tensor(share(value)), axis=0).reshape(2 * length, width // 2)

    def join(product):
        split = product.reshape(tensor_size, 2, rows, product.shape[1])
        handed = swap(split[:, 1].astype(jnp.bfloat16), "dp", 1)
        return (split[:, 0] + handed.astype(jnp.float32)).astype(jnp.bfloat16).reshape(length, -1)

    out_blocks = gather_chips(out_weight)
    joint_blocks = gather_chips(jnp.concatenate([query_weight, kv_weight], axis=1))

    grad_rows = all_rows(grad_out)
    values32 = tokens.astype(jnp.float32)
    root_mean = jnp.sqrt(jnp.mean(values32 * values32, axis=-1) + epsilon)
    unit = values32 / root_mean[:, None]
    gain32 = norm_gain.astype(jnp.float32)
    normed = all_rows((unit * gain32).astype(jnp.bfloat16))

    out_grad = join(
        lax.dot_general(
            grad_rows,
            jnp.concatenate(out_blocks, axis=1),
            contract_last,
            preferred_element_type=jnp.float32,
        )
    )
    joint_weight = jnp.concatenate(joint_blocks, axis=0)
    projected = join(jnp.dot(normed, joint_weight, preferred_element_type=jnp.float32))
    queries = projected[:, :query_width]
    keyvals = projected[:, query_width:]
    for bit_index in range(levels):
        partner = swap(keyvals, "tensor", 2**bit_index)
        upper = tensor_index >> bit_index & 1 == 1
        keyvals = jnp.concatenate(
            [jnp.where(upper, partner, keyvals), jnp.where(upper, keyvals, partner)], axis=1
        )
    key_rows = keyvals[:, :HD]
    value_rows = keyvals[:, HD:]

    order = jnp.arange(length, dtype=jnp.int32)
    positions = ((order // rows) ^ tensor_index) * rows + order % rows
    ends = jnp.cumsum(doc_lengths[0])
    labels = jnp.sum((ends[None, :] <= positions[:, None]).astype(jnp.int32), axis=1)
    allowed = (labels[:, None] == labels[None, :]) & (positions[None, :] <= positions[:, None])

    local_heads = query_width // HD
    query_heads = queries.reshape(length, local_heads, HD)
    out_heads = out_grad.reshape(length, local_heads, HD)
    scores = jnp.einsum(
        "qhd,td->hqt", query_heads, key_rows, preferred_element_type=jnp.float32
    ) / math.sqrt(HD)
    scores = jnp.where(allowed[None, :, :], scores, -1e30)
    peak = jnp.max(scores, axis=-1, keepdims=True)
    expo = jnp.exp(scores - peak)
    probs = expo / jnp.sum(expo, axis=-1, keepdims=True)
    probs_low = probs.astype(jnp.bfloat16)
    prob_grad = jnp.einsum("qhd,td->hqt", out_heads, value_rows, preferred_element_type=jnp.float32)
    inner = jnp.sum(probs * prob_grad, axis=-1, keepdims=True)
    score_grad = (probs * (prob_grad - inner) / math.sqrt(HD)).astype(jnp.bfloat16)
    query_grad = jnp.einsum("hqt,td->qhd", score_grad, key_rows, preferred_element_type=jnp.float32)
    query_grad = query_grad.astype(jnp.bfloat16).reshape(length, local_heads * HD)
    key_part = jnp.einsum(
        "hqt,qhd->td", score_grad, query_heads, preferred_element_type=jnp.float32
    )
    value_part = jnp.einsum("hqt,qhd->td", probs_low, out_heads, preferred_element_type=jnp.float32)
    kv_partial = jnp.concatenate([key_part, value_part], axis=1)
    for bit_index in reversed(range(levels)):
        half_cols = kv_partial.shape[1] // 2
        upper = tensor_index >> bit_index & 1 == 1
        lower_cols = kv_partial[:, :half_cols]
        higher_cols = kv_partial[:, half_cols:]
        kept = jnp.where(upper, higher_cols, lower_cols)
        handed = jnp.where(upper, lower_cols, higher_cols)
        kv_partial = kept + swap(handed.astype(jnp.bfloat16), "tensor", 2**bit_index).astype(
            jnp.float32
        )
    combined = jnp.concatenate([query_grad, kv_partial.astype(jnp.bfloat16)], axis=1)
    joint_width = combined.shape[1]
    other = swap(combined, "dp", 1)
    both = jnp.stack(
        [
            combined.reshape(tensor_size, rows, joint_width),
            other.reshape(tensor_size, rows, joint_width),
        ],
        axis=1,
    ).reshape(2 * length, joint_width)

    weight_terms = lax.dot_general(
        normed, both, (((0,), (0,)), ((), ())), preferred_element_type=jnp.float32
    ).astype(jnp.bfloat16)
    weight_grads = (
        scatter_chips([weight_terms[k * block : (k + 1) * block] for k in range(chips)]) / data_size
    )

    row_terms = lax.dot_general(
        both, joint_weight, contract_last, preferred_element_type=jnp.float32
    ).astype(jnp.bfloat16)
    normed_part = scatter_tensor(
        [row_terms[k * 2 * rows : (k + 1) * 2 * rows] for k in range(tensor_size)]
    )
    handed = swap(normed_part[rows:].astype(jnp.bfloat16), "dp", 1).astype(jnp.float32)
    relative = jnp.concatenate([normed_part[:rows], handed], axis=1)
    normed_grad = jnp.concatenate(
        [
            lax.dynamic_slice(
                relative,
                (0, (((b & 1) ^ core) * chips + ((b >> 1) ^ chip)) * block),
                (rows, block),
            )
            for b in range(data_size)
        ],
        axis=1,
    )
    scaled = normed_grad * gain32
    correction = unit * jnp.mean(scaled * unit, axis=-1, keepdims=True)
    input_grad = (grad_out.astype(jnp.float32) + (scaled - correction) / root_mean[:, None]).astype(
        jnp.bfloat16
    )
    return (input_grad, weight_grads[:, :query_width], weight_grads[:, query_width:])


def solution(mesh):
    placed = (
        P(("dp", "tensor"), None),
        P(),
        P("dp", "tensor"),
        P("dp", "tensor"),
        P("tensor", "dp"),
        P(("dp", "tensor"), None),
        P("dp", None),
    )
    return jax.shard_map(
        local,
        mesh=mesh,
        in_specs=placed,
        out_specs=(P(("dp", "tensor"), None), P("dp", "tensor"), P("dp", "tensor")),
        check_vma=False,
    )
```

```python
import math

import jax
import jax.numpy as jnp
from jax import lax
from jax.sharding import PartitionSpec as P

KVH = 4
HD = 128

epsilon = 1e-05


def swap(value, axis, mask):
    pairs = [(source, source ^ mask) for source in range(lax.axis_size(axis))]
    return lax.ppermute(value, axis, pairs)


def in_step(*streams):
    results = [None] * len(streams)
    waiting = {number: next(stream) for number, stream in enumerate(streams)}
    while waiting:
        ready = lax.optimization_barrier(tuple(waiting.values()))
        following = {}
        for number, values in zip(list(waiting), ready):
            try:
                following[number] = streams[number].send(values)
            except StopIteration as end:
                results[number] = end.value
        waiting = following
    return results


def gather_chips(value, then=()):
    chips = lax.axis_size("dp") // 2
    if chips != 4:
        blocks = [value] + [swap(value, "dp", 2 * k) for k in range(1, chips)]
        blocks, then = yield (blocks, then)
        return blocks, then
    half = value.shape[0] // 2
    near_x = swap(value, "dp", 2)
    near_y = swap(value, "dp", 4)
    value, near_x, near_y, then = yield (value, near_x, near_y, then)
    far_top = swap(near_x[:half], "dp", 4)
    far_bottom = swap(near_y[half:], "dp", 2)
    far_top, far_bottom, then = yield (far_top, far_bottom, then)
    return [value, near_x, near_y, jnp.concatenate([far_top, far_bottom], axis=0)], then


def scatter_chips(blocks):
    chips = lax.axis_size("dp") // 2
    if chips != 4:
        parts = [blocks[0]] + [swap(blocks[k], "dp", 2 * k) for k in range(1, chips)]
        parts = yield parts
        return sum(part.astype(jnp.float32) for part in parts)
    half = blocks[0].shape[0] // 2
    far_top = swap(blocks[3][:half], "dp", 4)
    far_bottom = swap(blocks[3][half:], "dp", 2)
    far_top, far_bottom = yield (far_top, far_bottom)
    near_x = swap(
        jnp.concatenate([blocks[1][:half] + far_top, blocks[1][half:]], axis=0), "dp", 2
    )
    near_y = swap(
        jnp.concatenate([blocks[2][:half], blocks[2][half:] + far_bottom], axis=0), "dp", 4
    )
    near_x, near_y = yield (near_x, near_y)
    return blocks[0].astype(jnp.float32) + near_x.astype(jnp.float32) + near_y.astype(jnp.float32)


def gather_tensor(value, then=()):
    size = lax.axis_size("tensor")
    if size != 4:
        blocks = [value] + [swap(value, "tensor", k) for k in range(1, size)]
        blocks, then = yield (blocks, then)
        return blocks, then
    index = lax.axis_index("tensor")
    two = swap(value, "tensor", 2)
    one = swap(value, "tensor", 1)
    value, one, two, then = yield (value, one, two, then)
    inner = lax.ppermute(value, "tensor", [(1, 2), (2, 1)])
    outer = lax.ppermute(two, "tensor", [(2, 3), (1, 0)])
    inner, outer, then = yield (inner, outer, then)
    return [value, one, two, jnp.where((index == 1) | (index == 2), inner, outer)], then


def scatter_tensor(blocks):
    size = lax.axis_size("tensor")
    if size != 4:
        parts = [blocks[0]] + [swap(blocks[k], "tensor", k) for k in range(1, size)]
        parts = yield parts
        return sum(part.astype(jnp.float32) for part in parts)
    outer = lax.ppermute(blocks[3], "tensor", [(0, 1), (3, 2)])
    inner = lax.ppermute(blocks[3], "tensor", [(1, 2), (2, 1)])
    outer, inner = yield (outer, inner)
    one = swap(blocks[1], "tensor", 1)
    two = swap(blocks[2] + outer, "tensor", 2)
    one, two = yield (one, two)
    return sum(part.astype(jnp.float32) for part in (blocks[0], one, inner, two))


def both(gather, first, second):
    first, second = yield from gather(first, second)
    second, _ = yield from gather(second)
    return first, second


def local(tokens, norm_gain, query_weight, kv_weight, out_weight, grad_out, doc_lengths):
    tensor_size = lax.axis_size("tensor")
    data_size = lax.axis_size("dp")
    tensor_index = lax.axis_index("tensor")
    data_index = lax.axis_index("dp")
    core, chip = data_index & 1, data_index >> 1
    chips = data_size // 2
    sharers = tensor_size // KVH
    levels = sharers.bit_length() - 1
    rows, width = tokens.shape
    block = width // data_size
    length = rows * tensor_size
    query_width = query_weight.shape[1]
    out_width = out_weight.shape[0]
    contract_last = (((1,), (1,)), ((), ()))

    def columns(value, which):
        starts = [((chip ^ k) * 2 + which) * block for k in range(chips)]
        return jnp.concatenate(
            [lax.dynamic_slice(value, (0, start), (value.shape[0], block)) for start in starts], axis=1
        )

    def share(value):
        handed = swap(columns(value, 1 - core), "dp", 1)
        return jnp.concatenate([columns(value, core), handed], axis=0)

    def all_rows(blocks):
        return jnp.stack(blocks, axis=0).reshape(2 * length, width // 2)

    def join(product):
        split = product.reshape(tensor_size, 2, rows, product.shape[1])
        handed = swap(split[:, 1].astype(jnp.bfloat16), "dp", 1)
        return (split[:, 0] + handed.astype(jnp.float32)).astype(jnp.bfloat16).reshape(length, -1)

    values32 = tokens.astype(jnp.float32)
    root_mean = jnp.sqrt(jnp.mean(values32 * values32, axis=-1) + epsilon)
    unit = values32 / root_mean[:, None]
    gain32 = norm_gain.astype(jnp.float32)
    normed_local = (unit * gain32).astype(jnp.bfloat16)
    (out_blocks, joint_blocks), (grad_blocks, normed_blocks) = in_step(
        both(gather_chips, out_weight, jnp.concatenate([query_weight, kv_weight], axis=1)),
        both(gather_tensor, share(grad_out), share(normed_local)),
    )
    grad_rows = all_rows(grad_blocks)
    normed = all_rows(normed_blocks)

    out_grad = join(
        lax.dot_general(
            grad_rows,
            jnp.concatenate(out_blocks, axis=1),
            contract_last,
            preferred_element_type=jnp.float32,
        )
    )
    joint_weight = jnp.concatenate(joint_blocks, axis=0)
    projected = join(jnp.dot(normed, joint_weight, preferred_element_type=jnp.float32))
    queries = projected[:, :query_width]
    keyvals = projected[:, query_width:]
    for bit_index in range(levels):
        partner = swap(keyvals, "tensor", 2**bit_index)
        upper = tensor_index >> bit_index & 1 == 1
        keyvals = jnp.concatenate(
            [jnp.where(upper, partner, keyvals), jnp.where(upper, keyvals, partner)], axis=1
        )
    key_rows = keyvals[:, :HD]
    value_rows = keyvals[:, HD:]

    order = jnp.arange(length, dtype=jnp.int32)
    positions = ((order // rows) ^ tensor_index) * rows + order % rows
    ends = jnp.cumsum(doc_lengths[0])
    labels = jnp.sum((ends[None, :] <= positions[:, None]).astype(jnp.int32), axis=1)
    allowed = (labels[:, None] == labels[None, :]) & (positions[None, :] <= positions[:, None])

    local_heads = query_width // HD
    query_heads = queries.reshape(length, local_heads, HD)
    out_heads = out_grad.reshape(length, local_heads, HD)
    scores = jnp.einsum(
        "qhd,td->hqt", query_heads, key_rows, preferred_element_type=jnp.float32
    ) / math.sqrt(HD)
    scores = jnp.where(allowed[None, :, :], scores, -1e30)
    peak = jnp.max(scores, axis=-1, keepdims=True)
    expo = jnp.exp(scores - peak)
    probs = expo / jnp.sum(expo, axis=-1, keepdims=True)
    probs_low = probs.astype(jnp.bfloat16)
    prob_grad = jnp.einsum("qhd,td->hqt", out_heads, value_rows, preferred_element_type=jnp.float32)
    inner = jnp.sum(probs * prob_grad, axis=-1, keepdims=True)
    score_grad = (probs * (prob_grad - inner) / math.sqrt(HD)).astype(jnp.bfloat16)
    query_grad = jnp.einsum("hqt,td->qhd", score_grad, key_rows, preferred_element_type=jnp.float32)
    query_grad = query_grad.astype(jnp.bfloat16).reshape(length, local_heads * HD)
    key_part = jnp.einsum(
        "hqt,qhd->td", score_grad, query_heads, preferred_element_type=jnp.float32
    )
    value_part = jnp.einsum("hqt,qhd->td", probs_low, out_heads, preferred_element_type=jnp.float32)
    kv_partial = jnp.concatenate([key_part, value_part], axis=1)
    for bit_index in reversed(range(levels)):
        half_cols = kv_partial.shape[1] // 2
        upper = tensor_index >> bit_index & 1 == 1
        lower_cols = kv_partial[:, :half_cols]
        higher_cols = kv_partial[:, half_cols:]
        kept = jnp.where(upper, higher_cols, lower_cols)
        handed = jnp.where(upper, lower_cols, higher_cols)
        kv_partial = kept + swap(handed.astype(jnp.bfloat16), "tensor", 2**bit_index).astype(
            jnp.float32
        )
    combined = jnp.concatenate([query_grad, kv_partial.astype(jnp.bfloat16)], axis=1)
    joint_width = combined.shape[1]
    other = swap(combined, "dp", 1)
    pair = jnp.stack(
        [
            combined.reshape(tensor_size, rows, joint_width),
            other.reshape(tensor_size, rows, joint_width),
        ],
        axis=1,
    ).reshape(2 * length, joint_width)

    weight_terms = lax.dot_general(
        normed, pair, (((0,), (0,)), ((), ())), preferred_element_type=jnp.float32
    ).astype(jnp.bfloat16)
    row_terms = lax.dot_general(
        pair, joint_weight, contract_last, preferred_element_type=jnp.float32
    ).astype(jnp.bfloat16)
    weight_sums, normed_part = in_step(
        scatter_chips([weight_terms[k * block : (k + 1) * block] for k in range(chips)]),
        scatter_tensor([row_terms[k * 2 * rows : (k + 1) * 2 * rows] for k in range(tensor_size)]),
    )
    weight_grads = weight_sums / data_size
    handed = swap(normed_part[rows:].astype(jnp.bfloat16), "dp", 1).astype(jnp.float32)
    relative = jnp.concatenate([normed_part[:rows], handed], axis=1)
    normed_grad = jnp.concatenate(
        [
            lax.dynamic_slice(
                relative,
                (0, (((b & 1) ^ core) * chips + ((b >> 1) ^ chip)) * block),
                (rows, block),
            )
            for b in range(data_size)
        ],
        axis=1,
    )
    scaled = normed_grad * gain32
    correction = unit * jnp.mean(scaled * unit, axis=-1, keepdims=True)
    input_grad = (grad_out.astype(jnp.float32) + (scaled - correction) / root_mean[:, None]).astype(
        jnp.bfloat16
    )
    return (input_grad, weight_grads[:, :query_width], weight_grads[:, query_width:])


def solution(mesh):
    placed = (
        P(("dp", "tensor"), None),
        P(),
        P("dp", "tensor"),
        P("dp", "tensor"),
        P("tensor", "dp"),
        P(("dp", "tensor"), None),
        P("dp", None),
    )
    return jax.shard_map(
        local,
        mesh=mesh,
        in_specs=placed,
        out_specs=(P(("dp", "tensor"), None), P("dp", "tensor"), P("dp", "tensor")),
        check_vma=False,
    )
```

```python
import math

import jax
import jax.numpy as jnp
from jax import lax
from jax.sharding import PartitionSpec as P

KVH = 4
HD = 128

epsilon = 1e-05


def swap(value, axis, mask):
    pairs = [(source, source ^ mask) for source in range(lax.axis_size(axis))]
    return lax.ppermute(value, axis, pairs)


def in_step(*streams):
    results = [None] * len(streams)
    waiting = {number: next(stream) for number, stream in enumerate(streams)}
    while waiting:
        ready = lax.optimization_barrier(tuple(waiting.values()))
        following = {}
        for number, values in zip(list(waiting), ready):
            try:
                following[number] = streams[number].send(values)
            except StopIteration as end:
                results[number] = end.value
        waiting = following
    return results


def gather_chips(value, axis):
    size = lax.axis_size("dp")
    groups = [list(range(core, size, 2)) for core in range(2)]
    return lax.all_gather(value, "dp", axis=axis, tiled=True, axis_index_groups=groups)


def scatter_chips(blocks):
    chips = lax.axis_size("dp") // 2
    if chips != 4:
        parts = [blocks[0]] + [swap(blocks[k], "dp", 2 * k) for k in range(1, chips)]
        parts = yield parts
        return sum(part.astype(jnp.float32) for part in parts)
    half = blocks[0].shape[0] // 2
    far_top = swap(blocks[3][:half], "dp", 4)
    far_bottom = swap(blocks[3][half:], "dp", 2)
    far_top, far_bottom = yield (far_top, far_bottom)
    near_x = swap(
        jnp.concatenate([blocks[1][:half] + far_top, blocks[1][half:]], axis=0), "dp", 2
    )
    near_y = swap(
        jnp.concatenate([blocks[2][:half], blocks[2][half:] + far_bottom], axis=0), "dp", 4
    )
    near_x, near_y = yield (near_x, near_y)
    return blocks[0].astype(jnp.float32) + near_x.astype(jnp.float32) + near_y.astype(jnp.float32)


def gather_tensor(value, then=()):
    size = lax.axis_size("tensor")
    if size != 4:
        blocks = [value] + [swap(value, "tensor", k) for k in range(1, size)]
        blocks, then = yield (blocks, then)
        return blocks, then
    index = lax.axis_index("tensor")
    two = swap(value, "tensor", 2)
    one = swap(value, "tensor", 1)
    value, one, two, then = yield (value, one, two, then)
    inner = lax.ppermute(value, "tensor", [(1, 2), (2, 1)])
    outer = lax.ppermute(two, "tensor", [(2, 3), (1, 0)])
    inner, outer, then = yield (inner, outer, then)
    return [value, one, two, jnp.where((index == 1) | (index == 2), inner, outer)], then


def scatter_tensor(blocks):
    size = lax.axis_size("tensor")
    if size != 4:
        parts = [blocks[0]] + [swap(blocks[k], "tensor", k) for k in range(1, size)]
        parts = yield parts
        return sum(part.astype(jnp.float32) for part in parts)
    outer = lax.ppermute(blocks[3], "tensor", [(0, 1), (3, 2)])
    inner = lax.ppermute(blocks[3], "tensor", [(1, 2), (2, 1)])
    outer, inner = yield (outer, inner)
    one = swap(blocks[1], "tensor", 1)
    two = swap(blocks[2] + outer, "tensor", 2)
    one, two = yield (one, two)
    return sum(part.astype(jnp.float32) for part in (blocks[0], one, inner, two))


def both(gather, first, second):
    first, second = yield from gather(first, second)
    second, _ = yield from gather(second)
    return first, second


def local(tokens, norm_gain, query_weight, kv_weight, out_weight, grad_out, doc_lengths):
    tensor_size = lax.axis_size("tensor")
    data_size = lax.axis_size("dp")
    tensor_index = lax.axis_index("tensor")
    data_index = lax.axis_index("dp")
    core, chip = data_index & 1, data_index >> 1
    chips = data_size // 2
    sharers = tensor_size // KVH
    levels = sharers.bit_length() - 1
    rows, width = tokens.shape
    block = width // data_size
    length = rows * tensor_size
    query_width = query_weight.shape[1]
    out_width = out_weight.shape[0]
    contract_last = (((1,), (1,)), ((), ()))

    def columns(value, which):
        split = value.reshape(rows, chips, 2, block)
        return lax.dynamic_index_in_dim(split, which, 2, keepdims=False).reshape(rows, width // 2)

    def share(value):
        handed = swap(columns(value, 1 - core), "dp", 1)
        return jnp.concatenate([columns(value, core), handed], axis=0)

    def all_rows(blocks):
        return jnp.stack(blocks, axis=0).reshape(2 * length, width // 2)

    def join(product):
        split = product.reshape(tensor_size, 2, rows, product.shape[1])
        handed = swap(split[:, 1].astype(jnp.bfloat16), "dp", 1)
        return (split[:, 0] + handed.astype(jnp.float32)).astype(jnp.bfloat16).reshape(length, -1)

    values32 = tokens.astype(jnp.float32)
    root_mean = jnp.sqrt(jnp.mean(values32 * values32, axis=-1) + epsilon)
    unit = values32 / root_mean[:, None]
    gain32 = norm_gain.astype(jnp.float32)
    normed_local = (unit * gain32).astype(jnp.bfloat16)
    out_half = gather_chips(out_weight, 1)
    joint_weight = gather_chips(jnp.concatenate([query_weight, kv_weight], axis=1), 0)
    ((grad_blocks, normed_blocks),) = in_step(
        both(gather_tensor, share(grad_out), share(normed_local))
    )
    grad_rows = all_rows(grad_blocks)
    normed = all_rows(normed_blocks)

    out_grad = join(
        lax.dot_general(
            grad_rows,
            out_half,
            contract_last,
            preferred_element_type=jnp.float32,
        )
    )
    projected = join(jnp.dot(normed, joint_weight, preferred_element_type=jnp.float32))
    queries = projected[:, :query_width]
    keyvals = projected[:, query_width:]
    for bit_index in range(levels):
        partner = swap(keyvals, "tensor", 2**bit_index)
        upper = tensor_index >> bit_index & 1 == 1
        keyvals = jnp.concatenate(
            [jnp.where(upper, partner, keyvals), jnp.where(upper, keyvals, partner)], axis=1
        )
    key_rows = keyvals[:, :HD]
    value_rows = keyvals[:, HD:]

    order = jnp.arange(length, dtype=jnp.int32)
    positions = ((order // rows) ^ tensor_index) * rows + order % rows
    ends = jnp.cumsum(doc_lengths[0])
    labels = jnp.sum((ends[None, :] <= positions[:, None]).astype(jnp.int32), axis=1)
    allowed = (labels[:, None] == labels[None, :]) & (positions[None, :] <= positions[:, None])

    local_heads = query_width // HD
    query_heads = queries.reshape(length, local_heads, HD)
    out_heads = out_grad.reshape(length, local_heads, HD)
    scores = jnp.einsum(
        "qhd,td->hqt", query_heads, key_rows, preferred_element_type=jnp.float32
    ) / math.sqrt(HD)
    scores = jnp.where(allowed[None, :, :], scores, -1e30)
    peak = jnp.max(scores, axis=-1, keepdims=True)
    expo = jnp.exp(scores - peak)
    probs = expo / jnp.sum(expo, axis=-1, keepdims=True)
    probs_low = probs.astype(jnp.bfloat16)
    prob_grad = jnp.einsum("qhd,td->hqt", out_heads, value_rows, preferred_element_type=jnp.float32)
    inner = jnp.sum(probs * prob_grad, axis=-1, keepdims=True)
    score_grad = (probs * (prob_grad - inner) / math.sqrt(HD)).astype(jnp.bfloat16)
    query_grad = jnp.einsum("hqt,td->qhd", score_grad, key_rows, preferred_element_type=jnp.float32)
    query_grad = query_grad.astype(jnp.bfloat16).reshape(length, local_heads * HD)
    key_part = jnp.einsum(
        "hqt,qhd->td", score_grad, query_heads, preferred_element_type=jnp.float32
    )
    value_part = jnp.einsum("hqt,qhd->td", probs_low, out_heads, preferred_element_type=jnp.float32)
    kv_partial = jnp.concatenate([key_part, value_part], axis=1)
    for bit_index in reversed(range(levels)):
        half_cols = kv_partial.shape[1] // 2
        upper = tensor_index >> bit_index & 1 == 1
        lower_cols = kv_partial[:, :half_cols]
        higher_cols = kv_partial[:, half_cols:]
        kept = jnp.where(upper, higher_cols, lower_cols)
        handed = jnp.where(upper, lower_cols, higher_cols)
        kv_partial = kept + swap(handed.astype(jnp.bfloat16), "tensor", 2**bit_index).astype(
            jnp.float32
        )
    combined = jnp.concatenate([query_grad, kv_partial.astype(jnp.bfloat16)], axis=1)
    joint_width = combined.shape[1]
    other = swap(combined, "dp", 1)
    pair = jnp.stack(
        [
            combined.reshape(tensor_size, rows, joint_width),
            other.reshape(tensor_size, rows, joint_width),
        ],
        axis=1,
    ).reshape(2 * length, joint_width)

    weight_terms = lax.dot_general(
        normed, pair, (((0,), (0,)), ((), ())), preferred_element_type=jnp.float32
    ).astype(jnp.bfloat16)
    row_terms = lax.dot_general(
        pair, joint_weight, contract_last, preferred_element_type=jnp.float32
    ).astype(jnp.bfloat16)
    weight_sums, normed_part = in_step(
        scatter_chips(
            [
                lax.dynamic_slice(weight_terms, ((chip ^ k) * block, 0), (block, joint_width))
                for k in range(chips)
            ]
        ),
        scatter_tensor([row_terms[k * 2 * rows : (k + 1) * 2 * rows] for k in range(tensor_size)]),
    )
    weight_grads = weight_sums / data_size
    handed = swap(normed_part[rows:].astype(jnp.bfloat16), "dp", 1).astype(jnp.float32)
    own_half = normed_part[:rows].reshape(rows, chips, 1, block)
    other_half = handed.reshape(rows, chips, 1, block)
    normed_grad = jnp.where(
        core == 0,
        jnp.concatenate([own_half, other_half], axis=2),
        jnp.concatenate([other_half, own_half], axis=2),
    ).reshape(rows, width)
    scaled = normed_grad * gain32
    correction = unit * jnp.mean(scaled * unit, axis=-1, keepdims=True)
    input_grad = (grad_out.astype(jnp.float32) + (scaled - correction) / root_mean[:, None]).astype(
        jnp.bfloat16
    )
    return (input_grad, weight_grads[:, :query_width], weight_grads[:, query_width:])


def solution(mesh):
    placed = (
        P(("dp", "tensor"), None),
        P(),
        P("dp", "tensor"),
        P("dp", "tensor"),
        P("tensor", "dp"),
        P(("dp", "tensor"), None),
        P("dp", None),
    )
    return jax.shard_map(
        local,
        mesh=mesh,
        in_specs=placed,
        out_specs=(P(("dp", "tensor"), None), P("dp", "tensor"), P("dp", "tensor")),
        check_vma=False,
    )
```

```python
import functools
import math

import jax
import jax.numpy as jnp
from jax import lax
from jax.experimental import pallas as pl
from jax.experimental.pallas import tpu as pltpu
from jax.sharding import PartitionSpec as P

KVH = 4
HD = 128

epsilon = 1e-05
CONTRACT_LAST = (((1,), (1,)), ((), ()))
CONTRACT_FIRST = (((0,), (0,)), ((), ()))
WHOLE = pl.BlockSpec(memory_space=pltpu.VMEM)
SCALARS = pl.BlockSpec(memory_space=pltpu.SMEM)


def call(kernel, outs, operands, scalars=(), scratch=(), flops=0, megabytes=32):
    moved = sum(math.prod(a.shape) * a.dtype.itemsize for a in (*operands, *outs))
    return pl.pallas_call(
        kernel,
        out_shape=outs,
        in_specs=[SCALARS] * len(scalars) + [WHOLE] * len(operands),
        out_specs=[WHOLE] * len(outs),
        scratch_shapes=scratch,
        compiler_params=pltpu.CompilerParams(vmem_limit_bytes=megabytes * 2**20),
        cost_estimate=pl.CostEstimate(flops=flops, bytes_accessed=moved, transcendentals=0),
    )(*scalars, *operands)


def shaped(shape, dtype=jnp.bfloat16):
    return jax.ShapeDtypeStruct(shape, dtype)


def dot(left, right, contract=(((1,), (0,)), ((), ()))):
    return lax.dot_general(left, right, contract, preferred_element_type=jnp.float32)


def swap(value, axis, mask):
    pairs = [(source, source ^ mask) for source in range(lax.axis_size(axis))]
    return lax.ppermute(value, axis, pairs)


def in_step(*streams):
    results = [None] * len(streams)
    waiting = {}
    for number, stream in enumerate(streams):
        try:
            waiting[number] = next(stream)
        except StopIteration as end:
            results[number] = end.value
    while waiting:
        ready = lax.optimization_barrier(tuple(waiting.values()))
        following = {}
        for number, values in zip(list(waiting), ready):
            try:
                following[number] = streams[number].send(values)
            except StopIteration as end:
                results[number] = end.value
        waiting = following
    return results


def gather_chips(value, axis, then=()):
    chips = lax.axis_size("dp") // 2
    if chips != 4:
        blocks = [value] + [swap(value, "dp", 2 * k) for k in range(1, chips)]
        blocks, then = yield (blocks, then)
        return blocks, then
    near_x = swap(value, "dp", 2)
    near_y = swap(value, "dp", 4)
    value, near_x, near_y, then = yield (value, near_x, near_y, then)
    far_top = swap(jnp.split(near_x, 2, axis)[0], "dp", 4)
    far_bottom = swap(jnp.split(near_y, 2, axis)[1], "dp", 2)
    far_top, far_bottom, then = yield (far_top, far_bottom, then)
    return [value, near_x, near_y, far_top, far_bottom], then


def scatter_chips(blocks):
    chips = lax.axis_size("dp") // 2
    if chips != 4:
        return [blocks[0]] + [swap(blocks[k], "dp", 2 * k) for k in range(1, chips)]
        yield
    half = blocks[0].shape[0] // 2
    far_top = swap(blocks[3][:half], "dp", 4)
    far_bottom = swap(blocks[3][half:], "dp", 2)
    far_top, far_bottom = yield (far_top, far_bottom)
    near_x = swap(
        jnp.concatenate([blocks[1][:half] + far_top, blocks[1][half:]], axis=0), "dp", 2
    )
    near_y = swap(
        jnp.concatenate([blocks[2][:half], blocks[2][half:] + far_bottom], axis=0), "dp", 4
    )
    return [blocks[0], near_x, near_y]


def gather_tensor(value, then=()):
    size = lax.axis_size("tensor")
    if size != 4:
        blocks = [value] + [swap(value, "tensor", k) for k in range(1, size)]
        blocks, then = yield (blocks, then)
        return blocks, then
    two = swap(value, "tensor", 2)
    one = swap(value, "tensor", 1)
    value, one, two, then = yield (value, one, two, then)
    inner = lax.ppermute(value, "tensor", [(1, 2), (2, 1)])
    outer = lax.ppermute(two, "tensor", [(2, 3), (1, 0)])
    inner, outer, then = yield (inner, outer, then)
    return [value, one, two, inner, outer], then


def scatter_tensor(blocks):
    size = lax.axis_size("tensor")
    if size != 4:
        return [blocks[0]] + [swap(blocks[k], "tensor", k) for k in range(1, size)]
        yield
    outer = lax.ppermute(blocks[3], "tensor", [(0, 1), (3, 2)])
    inner = lax.ppermute(blocks[3], "tensor", [(1, 2), (2, 1)])
    outer, inner = yield (outer, inner)
    two = swap(blocks[2] + outer, "tensor", 2)
    one = swap(blocks[1], "tensor", 1)
    return [blocks[0], one, inner, two]


def weights_stream(out_weight, joint):
    first, joint = yield from gather_chips(out_weight, 1, joint)
    second, _ = yield from gather_chips(joint, 0)
    return first, second


def rows_stream(first, second):
    first, second = yield from gather_tensor(first, second)
    second, _ = yield from gather_tensor(second)
    return first, second


def column_start(place, k, which, block):
    return pl.multiple_of(((place[0] ^ k) * 2 + which) * block, 128)


def divide(place, source, keep, send, block):
    core = place[1]
    for k in range(keep.shape[1] // block):
        columns = slice(k * block, (k + 1) * block)
        keep[:, columns] = source[:, pl.ds(column_start(place, k, core, block), block)]
        send[:, columns] = source[:, pl.ds(column_start(place, k, 1 - core, block), block)]


def divide_kernel(block, place, source, keep, send):
    divide(place, source, keep, send, block)


def norm_kernel(block, place, tokens, gain, keep, send, normed):
    values = tokens[...].astype(jnp.float32)
    root_mean = jnp.sqrt(jnp.mean(values * values, axis=-1, keepdims=True) + epsilon)
    normed[...] = (values / root_mean * gain[...].astype(jnp.float32)).astype(jnp.bfloat16)
    divide(place, normed, keep, send, block)


def project_kernel(pieces, weights, size, transposed, place, *refs):
    row_refs, weight_refs = refs[:pieces], refs[pieces : pieces + weights]
    keep, send, pair = refs[pieces + weights :]
    rows = row_refs[0].shape[0] // 2
    length = rows * size
    for k in range(size):
        value = row_refs[k][...]
        if pieces > size and k == size - 1:
            middle = jnp.logical_or(place[2] == 1, place[2] == 2)
            value = jnp.where(middle, value, row_refs[k + 1][...])
        pair[k * rows : (k + 1) * rows] = value[:rows]
        pair[length + k * rows : length + (k + 1) * rows] = value[rows:]
    width = keep.shape[1]
    tile = 256 if width % 256 == 0 else width

    def step(columns):
        start, total = 0, None
        for weight in weight_refs:
            depth = weight.shape[1 if transposed else 0]
            left = pair[:, start : start + depth]
            if transposed:
                term = dot(left, weight[columns, :], CONTRACT_LAST)
            else:
                term = dot(left, weight[:, columns])
            total = term if total is None else total + term
            start += depth
        keep[:, columns] = total[:length]
        send[:, columns] = total[length:].astype(jnp.bfloat16)

    if tile == width:
        step(slice(0, width))
    else:

        @pl.loop(0, width // tile)
        def _(number):
            step(pl.ds(pl.multiple_of(number * tile, tile), tile))


def project(place, pieces, weights, transposed, size):
    rows = pieces[0].shape[0] // 2 * size
    half = pieces[0].shape[1]
    width = weights[0].shape[0 if transposed else 1]
    return call(
        functools.partial(project_kernel, len(pieces), len(weights), size, transposed),
        [
            shaped((rows, width), jnp.float32),
            shaped((rows, width)),
            shaped((2 * rows, half)),
        ],
        [*pieces, *weights],
        [place],
        flops=4 * rows * half * width,
    )


def attention_kernel(rows, heads, place, lengths, out_own, out_sent, own, sent, grads, partial):
    length = out_own.shape[0]
    width = heads * HD
    scale = 1 / math.sqrt(HD)
    tensor_index = place[2]

    def positions_of(dimension):
        order = lax.broadcasted_iota(jnp.int32, (length, length), dimension)
        return ((order // rows) ^ tensor_index) * rows + order % rows

    def labels_of(positions):
        labels, end = jnp.zeros((length, length), jnp.int32), 0
        for document in range(lengths.shape[1]):
            end = end + lengths[0, document]
            labels = labels + (end <= positions).astype(jnp.int32)
        return labels

    key_positions, query_positions = positions_of(0), positions_of(1)
    allowed = jnp.logical_and(
        labels_of(key_positions) == labels_of(query_positions), key_positions <= query_positions
    )

    def joined(first, second, columns):
        return (first[:, columns] + second[:, columns].astype(jnp.float32)).astype(jnp.bfloat16)

    keys = joined(own, sent, slice(width, width + HD))
    values = joined(own, sent, slice(width + HD, width + 2 * HD))
    key_total = value_total = None
    for head in range(heads):
        columns = slice(head * HD, (head + 1) * HD)
        queries = joined(own, sent, columns)
        out_grad = joined(out_own, out_sent, columns)
        scores = jnp.where(allowed, dot(keys, queries, CONTRACT_LAST) * scale, -1e30)
        expo = jnp.exp(scores - jnp.max(scores, axis=0, keepdims=True))
        probs = expo * (1 / jnp.sum(expo, axis=0, keepdims=True))
        prob_grad = dot(values, out_grad, CONTRACT_LAST)
        inner = jnp.sum(probs * prob_grad, axis=0, keepdims=True)
        score_grad = (probs * (prob_grad - inner) * scale).astype(jnp.bfloat16)
        grads[:, columns] = dot(score_grad, keys, CONTRACT_FIRST).astype(jnp.bfloat16)
        key_term = dot(score_grad, queries)
        value_term = dot(probs.astype(jnp.bfloat16), out_grad)
        key_total = key_term if head == 0 else key_total + key_term
        value_total = value_term if head == 0 else value_total + value_term
    if partial is None:
        grads[:, width : width + HD] = key_total.astype(jnp.bfloat16)
        grads[:, width + HD :] = value_total.astype(jnp.bfloat16)
    else:
        partial[:, :HD] = key_total
        partial[:, HD:] = value_total


def attention(place, lengths, out_own, out_sent, own, sent, rows, split):
    length, width = out_own.shape
    outs = [shaped((length, width if split else width + 2 * HD))]
    if split:
        outs.append(shaped((length, 2 * HD), jnp.float32))

    def kernel(*refs):
        attention_kernel(rows, width // HD, *(refs if split else (*refs, None)))

    return call(
        kernel,
        outs,
        [out_own, out_sent, own, sent],
        [place, lengths],
        flops=10 * length * length * width,
    )


def weight_kernel(first, block, pair, own, other, *outs):
    length = own.shape[0]
    tile = min(block, 256)
    for number, out in enumerate(outs):
        for part in range(block // tile):
            start = (first + number) * block + part * tile
            out[part * tile : (part + 1) * tile] = (
                dot(pair[:length, start : start + tile], own[...], CONTRACT_FIRST)
                + dot(pair[length:, start : start + tile], other[...], CONTRACT_FIRST)
            ).astype(jnp.bfloat16)


def weight_terms(pair, own, other, first, count, block):
    return call(
        functools.partial(weight_kernel, first, block),
        [shaped((block, own.shape[1]))] * count,
        [pair, own, other],
        flops=2 * pair.shape[0] * block * count * own.shape[1],
    )


def row_kernel(weights, own, other, *refs):
    weight_refs, outs = refs[:weights], refs[weights:]
    length = own.shape[0]
    rows = length // len(outs)
    start = 0
    for weight in weight_refs:
        tile = min(weight.shape[0], 256)
        for part in range(weight.shape[0] // tile):
            right = weight[part * tile : (part + 1) * tile, :]
            for offset, left in ((0, own), (rows, other)):
                term = dot(left[...], right, CONTRACT_LAST).astype(jnp.bfloat16)
                for k, out in enumerate(outs):
                    out[offset : offset + rows, start : start + tile] = term[
                        k * rows : (k + 1) * rows
                    ]
            start += tile


def row_terms(own, other, weights, size):
    length, width = own.shape
    half = sum(weight.shape[0] for weight in weights)
    return call(
        functools.partial(row_kernel, len(weights)),
        [shaped((2 * length // size, half))] * size,
        [own, other, *weights],
        flops=4 * length * width * half,
    )


def finish_kernel(count, share, *refs):
    total = refs[0][...].astype(jnp.float32)
    for part in refs[1:count]:
        total = total + part[...].astype(jnp.float32)
    total = total * share
    query_out, kv_out = refs[count:]
    width = query_out.shape[1]
    query_out[...] = total[:, :width]
    kv_out[...] = total[:, width:]


def finish(parts, query_width, share):
    block, width = parts[0].shape
    step = min(block, 128)

    def spec(columns):
        return pl.BlockSpec((step, columns), lambda i: (i, 0))

    return pl.pallas_call(
        functools.partial(finish_kernel, len(parts), share),
        grid=(block // step,),
        out_shape=[
            shaped((block, query_width), jnp.float32),
            shaped((block, width - query_width), jnp.float32),
        ],
        in_specs=[spec(width)] * len(parts),
        out_specs=[spec(query_width), spec(width - query_width)],
        compiler_params=pltpu.CompilerParams(vmem_limit_bytes=32 * 2**20),
        cost_estimate=pl.CostEstimate(
            flops=0, bytes_accessed=(2 * len(parts) + 4) * block * width, transcendentals=0
        ),
    )(*parts)


def input_kernel(count, block, place, tokens, gain, grad_out, handed, *refs):
    parts, out, gathered = refs[:count], refs[count], refs[count + 1]
    rows = tokens.shape[0]
    core = place[1]
    total = parts[0][:rows].astype(jnp.float32)
    for part in parts[1:]:
        total = total + part[:rows].astype(jnp.float32)
    for k in range(total.shape[1] // block):
        columns = slice(k * block, (k + 1) * block)
        gathered[:, pl.ds(column_start(place, k, core, block), block)] = total[:, columns]
        gathered[:, pl.ds(column_start(place, k, 1 - core, block), block)] = handed[
            :, columns
        ].astype(jnp.float32)
    values = tokens[...].astype(jnp.float32)
    root_mean = jnp.sqrt(jnp.mean(values * values, axis=-1, keepdims=True) + epsilon)
    unit = values / root_mean
    scaled = gathered[...] * gain[...].astype(jnp.float32)
    correction = unit * jnp.mean(scaled * unit, axis=-1, keepdims=True)
    out[...] = (grad_out[...].astype(jnp.float32) + (scaled - correction) / root_mean).astype(
        jnp.bfloat16
    )


def local(tokens, norm_gain, query_weight, kv_weight, out_weight, grad_out, doc_lengths):
    tensor_size = lax.axis_size("tensor")
    data_size = lax.axis_size("dp")
    tensor_index = lax.axis_index("tensor")
    data_index = lax.axis_index("dp")
    chips = data_size // 2
    place = jnp.stack([data_index >> 1, data_index & 1, tensor_index]).astype(jnp.int32)
    sharers = tensor_size // KVH
    levels = sharers.bit_length() - 1
    rows, width = tokens.shape
    block = width // data_size
    query_width = query_weight.shape[1]
    gain = norm_gain.reshape(1, width)
    halves = [shaped((rows, width // 2))] * 2

    keep, send = call(functools.partial(divide_kernel, block), halves, [grad_out], [place])
    grad_pair = jnp.concatenate([keep, swap(send, "dp", 1)], axis=0)
    tokens, gain, grad_pair = lax.optimization_barrier((tokens, gain, grad_pair))
    keep, send = call(
        functools.partial(norm_kernel, block),
        halves,
        [tokens, gain],
        [place],
        [pltpu.VMEM((rows, width), jnp.bfloat16)],
    )
    normed_pair = jnp.concatenate([keep, swap(send, "dp", 1)], axis=0)
    joint = jnp.concatenate([query_weight, kv_weight], axis=1)
    (out_blocks, joint_blocks), (grad_blocks, normed_blocks) = in_step(
        weights_stream(out_weight, joint), rows_stream(grad_pair, normed_pair)
    )

    out_own, out_sent, _ = project(place, grad_blocks, out_blocks, True, tensor_size)
    out_sent = swap(out_sent, "dp", 1)
    own, sent, normed = project(place, normed_blocks, joint_blocks, False, tensor_size)
    sent = swap(sent, "dp", 1)
    if levels:
        joined = (own + sent.astype(jnp.float32)).astype(jnp.bfloat16)
        keyvals = joined[:, query_width:]
        for bit_index in range(levels):
            partner = swap(keyvals, "tensor", 2**bit_index)
            upper = tensor_index >> bit_index & 1 == 1
            keyvals = jnp.concatenate(
                [jnp.where(upper, partner, keyvals), jnp.where(upper, keyvals, partner)], axis=1
            )
        own = jnp.concatenate([joined[:, :query_width], keyvals], axis=1).astype(jnp.float32)
        sent = jnp.zeros(own.shape, jnp.bfloat16)
    combined, *partial = attention(
        place, doc_lengths, out_own, out_sent, own, sent, rows, levels > 0
    )
    if levels:
        kv_partial = partial[0]
        for bit_index in reversed(range(levels)):
            half_cols = kv_partial.shape[1] // 2
            upper = tensor_index >> bit_index & 1 == 1
            lower_cols = kv_partial[:, :half_cols]
            higher_cols = kv_partial[:, half_cols:]
            kept = jnp.where(upper, higher_cols, lower_cols)
            handed = jnp.where(upper, lower_cols, higher_cols)
            kv_partial = kept + swap(handed.astype(jnp.bfloat16), "tensor", 2**bit_index).astype(
                jnp.float32
            )
        combined = jnp.concatenate([combined, kv_partial.astype(jnp.bfloat16)], axis=1)
    other = swap(combined, "dp", 1)

    far = weight_terms(normed, combined, other, chips - 1, 1, block)
    near = weight_terms(normed, combined, other, 0, chips - 1, block)
    weight_parts, row_parts = in_step(
        scatter_chips([*near, *far]),
        scatter_tensor(row_terms(combined, other, joint_blocks, tensor_size)),
    )
    handed = sum(part[rows:].astype(jnp.float32) for part in row_parts).astype(jnp.bfloat16)
    (input_grad,) = call(
        functools.partial(input_kernel, len(row_parts), block),
        [shaped((rows, width))],
        [tokens, gain, grad_out, swap(handed, "dp", 1), *row_parts],
        [place],
        [pltpu.VMEM((rows, width), jnp.float32)],
    )
    query_grad, kv_grad = finish(weight_parts, query_width, 1 / data_size)
    return (input_grad, query_grad, kv_grad)


def solution(mesh):
    placed = (
        P(("dp", "tensor"), None),
        P(),
        P("dp", "tensor"),
        P("dp", "tensor"),
        P("tensor", "dp"),
        P(("dp", "tensor"), None),
        P("dp", None),
    )
    return jax.shard_map(
        local,
        mesh=mesh,
        in_specs=placed,
        out_specs=(P(("dp", "tensor"), None), P("dp", "tensor"), P("dp", "tensor")),
        check_vma=False,
    )
```

```python
import functools
import math

import jax
import jax.numpy as jnp
from jax import lax
from jax.experimental import pallas as pl
from jax.experimental.pallas import tpu as pltpu
from jax.sharding import PartitionSpec as P

KVH = 4
HD = 128

epsilon = 1e-05
CONTRACT_LAST = (((1,), (1,)), ((), ()))
CONTRACT_FIRST = (((0,), (0,)), ((), ()))
WHOLE = pl.BlockSpec(memory_space=pltpu.VMEM)
SCALARS = pl.BlockSpec(memory_space=pltpu.SMEM)


def call(kernel, outs, operands, scalars=(), scratch=(), flops=0, megabytes=32):
    moved = sum(math.prod(a.shape) * a.dtype.itemsize for a in (*operands, *outs))
    return pl.pallas_call(
        kernel,
        out_shape=outs,
        in_specs=[SCALARS] * len(scalars) + [WHOLE] * len(operands),
        out_specs=[WHOLE] * len(outs),
        scratch_shapes=scratch,
        compiler_params=pltpu.CompilerParams(vmem_limit_bytes=megabytes * 2**20),
        cost_estimate=pl.CostEstimate(flops=flops, bytes_accessed=moved, transcendentals=0),
    )(*scalars, *operands)


def shaped(shape, dtype=jnp.bfloat16):
    return jax.ShapeDtypeStruct(shape, dtype)


def dot(left, right, contract=(((1,), (0,)), ((), ()))):
    return lax.dot_general(left, right, contract, preferred_element_type=jnp.float32)


def swap(value, axis, mask):
    pairs = [(source, source ^ mask) for source in range(lax.axis_size(axis))]
    return lax.ppermute(value, axis, pairs)


def tied(*values):
    return lax.optimization_barrier(values)


def gather_outward(value):
    size = lax.axis_size("dp")
    groups = [list(range(core, size, 2)) for core in range(2)]
    return lax.all_gather(value, "dp", axis=1, tiled=True, axis_index_groups=groups)


def everyone(value, axis, unit):
    size = lax.axis_size(axis) // unit
    return [value] + [swap(value, axis, unit * k) for k in range(1, size)]


def inner_pair(value):
    return lax.ppermute(value, "tensor", [(1, 2), (2, 1)])


def outer_pair(value, outward=True):
    pairs = [(2, 3), (1, 0)] if outward else [(3, 2), (0, 1)]
    return lax.ppermute(value, "tensor", pairs)


def staged_gathers(grad, normed_later, joint, project_out):
    half = joint.shape[0] // 2
    two_g, one_g = swap(grad, "tensor", 2), swap(grad, "tensor", 1)
    near_x, near_y = swap(joint, "dp", 2), swap(joint, "dp", 4)
    normed = normed_later()
    grad, two_g, one_g, near_x, near_y, normed = tied(grad, two_g, one_g, near_x, near_y, normed)
    outer_g, inner_g = outer_pair(two_g), inner_pair(grad)
    two_n, one_n = swap(normed, "tensor", 2), swap(normed, "tensor", 1)
    far_top = swap(near_x[:half], "dp", 4)
    outer_g, inner_g, two_n, one_n, far_top, normed, near_y = tied(
        outer_g, inner_g, two_n, one_n, far_top, normed, near_y
    )
    outer_n, inner_n = outer_pair(two_n), inner_pair(normed)
    far_bottom = swap(near_y[half:], "dp", 2)
    out_own, out_sent = project_out([grad, one_g, two_g, inner_g, outer_g])
    outer_n, inner_n, far_bottom, out_own, out_sent = tied(
        outer_n, inner_n, far_bottom, out_own, out_sent
    )
    return (
        [normed, one_n, two_n, inner_n, outer_n],
        [joint, near_x, near_y, far_top, far_bottom],
        out_own,
        out_sent,
    )


def scatter_chips(blocks):
    if len(blocks) != 4:
        return [blocks[0]] + [swap(blocks[k], "dp", 2 * k) for k in range(1, len(blocks))]
    half = blocks[0].shape[0] // 2
    far_top = swap(blocks[3][:half], "dp", 4)
    far_bottom = swap(blocks[3][half:], "dp", 2)
    near_x = swap(
        jnp.concatenate([blocks[1][:half] + far_top, blocks[1][half:]], axis=0), "dp", 2
    )
    near_y = swap(
        jnp.concatenate([blocks[2][:half], blocks[2][half:] + far_bottom], axis=0), "dp", 4
    )
    return [blocks[0], near_x, near_y]


def scatter_tensor(blocks):
    if len(blocks) != 4:
        return [blocks[0]] + [swap(blocks[k], "tensor", k) for k in range(1, len(blocks))]
    outer, inner = outer_pair(blocks[3], False), inner_pair(blocks[3])
    outer, inner = tied(outer, inner)
    two, one = swap(blocks[2] + outer, "tensor", 2), swap(blocks[1], "tensor", 1)
    return [blocks[0], one, inner, two]


def column_start(chip, which, block):
    return pl.multiple_of((chip * 2 + which) * block, 128)


def divide(chip, core, source, keep, send, block):
    for k in range(keep.shape[1] // block):
        columns = slice(k * block, (k + 1) * block)
        keep[:, columns] = source[:, pl.ds(column_start(chip ^ k, core, block), block)]
        send[:, columns] = source[:, pl.ds(column_start(chip ^ k, 1 - core, block), block)]


def divide_kernel(block, place, source, keep, send):
    divide(0, place[1], source, keep, send, block)


def norm_kernel(block, place, tokens, gain, keep, send, normed):
    values = tokens[...].astype(jnp.float32)
    root_mean = jnp.sqrt(jnp.mean(values * values, axis=-1, keepdims=True) + epsilon)
    normed[...] = (values / root_mean * gain[...].astype(jnp.float32)).astype(jnp.bfloat16)
    divide(place[0], place[1], normed, keep, send, block)


def project_kernel(pieces, weights, size, transposed, place, *refs):
    row_refs, weight_refs = refs[:pieces], refs[pieces : pieces + weights]
    keep, send, pair = refs[pieces + weights :]
    rows = row_refs[0].shape[0] // 2
    length = rows * size
    for k in range(size):
        value = row_refs[k][...]
        if pieces > size and k == size - 1:
            middle = jnp.logical_or(place[2] == 1, place[2] == 2)
            value = jnp.where(middle, value, row_refs[k + 1][...])
        pair[k * rows : (k + 1) * rows] = value[:rows]
        pair[length + k * rows : length + (k + 1) * rows] = value[rows:]
    width = keep.shape[1]
    tile = 256 if width % 256 == 0 else width

    def step(columns):
        start, total = 0, None
        for weight in weight_refs:
            depth = weight.shape[1 if transposed else 0]
            left = pair[:, start : start + depth]
            if transposed:
                term = dot(left, weight[columns, :], CONTRACT_LAST)
            else:
                term = dot(left, weight[:, columns])
            total = term if total is None else total + term
            start += depth
        keep[:, columns] = total[:length]
        send[:, columns] = total[length:].astype(jnp.bfloat16)

    if tile == width:
        step(slice(0, width))
    else:

        @pl.loop(0, width // tile)
        def _(number):
            step(pl.ds(pl.multiple_of(number * tile, tile), tile))


def project(place, pieces, weights, transposed, size, keep_pair):
    rows = pieces[0].shape[0] // 2 * size
    half = pieces[0].shape[1]
    width = weights[0].shape[0 if transposed else 1]
    outs = [shaped((rows, width), jnp.float32), shaped((rows, width))]
    pair = shaped((2 * rows, half))
    return call(
        functools.partial(project_kernel, len(pieces), len(weights), size, transposed),
        [*outs, pair] if keep_pair else outs,
        [*pieces, *weights],
        [place],
        () if keep_pair else [pltpu.VMEM(pair.shape, pair.dtype)],
        flops=4 * rows * half * width,
    )


def attention_kernel(rows, heads, place, lengths, out_own, out_sent, own, sent, grads, partial):
    length = out_own.shape[0]
    width = heads * HD
    scale = 1 / math.sqrt(HD)
    tensor_index = place[2]

    def positions_of(dimension):
        order = lax.broadcasted_iota(jnp.int32, (length, length), dimension)
        return ((order // rows) ^ tensor_index) * rows + order % rows

    def labels_of(positions):
        labels, end = jnp.zeros((length, length), jnp.int32), 0
        for document in range(lengths.shape[1]):
            end = end + lengths[0, document]
            labels = labels + (end <= positions).astype(jnp.int32)
        return labels

    key_positions, query_positions = positions_of(0), positions_of(1)
    allowed = jnp.logical_and(
        labels_of(key_positions) == labels_of(query_positions), key_positions <= query_positions
    )

    def joined(first, second, columns):
        return (first[:, columns] + second[:, columns].astype(jnp.float32)).astype(jnp.bfloat16)

    keys = joined(own, sent, slice(width, width + HD))
    values = joined(own, sent, slice(width + HD, width + 2 * HD))
    key_total = value_total = None
    for head in range(heads):
        columns = slice(head * HD, (head + 1) * HD)
        queries = joined(own, sent, columns)
        out_grad = joined(out_own, out_sent, columns)
        scores = jnp.where(allowed, dot(keys, queries, CONTRACT_LAST) * scale, -1e30)
        expo = jnp.exp(scores - jnp.max(scores, axis=0, keepdims=True))
        probs = expo * (1 / jnp.sum(expo, axis=0, keepdims=True))
        prob_grad = dot(values, out_grad, CONTRACT_LAST)
        inner = jnp.sum(probs * prob_grad, axis=0, keepdims=True)
        score_grad = (probs * (prob_grad - inner) * scale).astype(jnp.bfloat16)
        grads[:, columns] = dot(score_grad, keys, CONTRACT_FIRST).astype(jnp.bfloat16)
        key_term = dot(score_grad, queries)
        value_term = dot(probs.astype(jnp.bfloat16), out_grad)
        key_total = key_term if head == 0 else key_total + key_term
        value_total = value_term if head == 0 else value_total + value_term
    if partial is None:
        grads[:, width : width + HD] = key_total.astype(jnp.bfloat16)
        grads[:, width + HD :] = value_total.astype(jnp.bfloat16)
    else:
        partial[:, :HD] = key_total
        partial[:, HD:] = value_total


def attention(place, lengths, out_own, out_sent, own, sent, rows, split):
    length, width = out_own.shape
    outs = [shaped((length, width if split else width + 2 * HD))]
    if split:
        outs.append(shaped((length, 2 * HD), jnp.float32))

    def kernel(*refs):
        attention_kernel(rows, width // HD, *(refs if split else (*refs, None)))

    return call(
        kernel,
        outs,
        [out_own, out_sent, own, sent],
        [place, lengths],
        flops=10 * length * length * width,
    )


def weight_kernel(first, block, pair, own, other, *outs):
    length = own.shape[0]
    tile = min(block, 256)
    for number, out in enumerate(outs):
        for part in range(block // tile):
            start = (first + number) * block + part * tile
            out[part * tile : (part + 1) * tile] = (
                dot(pair[:length, start : start + tile], own[...], CONTRACT_FIRST)
                + dot(pair[length:, start : start + tile], other[...], CONTRACT_FIRST)
            ).astype(jnp.bfloat16)


def weight_terms(pair, own, other, first, count, block):
    return call(
        functools.partial(weight_kernel, first, block),
        [shaped((block, own.shape[1]))] * count,
        [pair, own, other],
        flops=2 * pair.shape[0] * block * count * own.shape[1],
    )


def row_kernel(weights, own, other, *refs):
    weight_refs, outs = refs[:weights], refs[weights:]
    length = own.shape[0]
    rows = length // len(outs)
    start = 0
    for weight in weight_refs:
        tile = min(weight.shape[0], 256)
        for part in range(weight.shape[0] // tile):
            right = weight[part * tile : (part + 1) * tile, :]
            for offset, left in ((0, own), (rows, other)):
                term = dot(left[...], right, CONTRACT_LAST).astype(jnp.bfloat16)
                for k, out in enumerate(outs):
                    out[offset : offset + rows, start : start + tile] = term[
                        k * rows : (k + 1) * rows
                    ]
            start += tile


def row_terms(own, other, weights, size):
    length, width = own.shape
    half = sum(weight.shape[0] for weight in weights)
    return call(
        functools.partial(row_kernel, len(weights)),
        [shaped((2 * length // size, half))] * size,
        [own, other, *weights],
        flops=4 * length * width * half,
    )


def finish_kernel(count, share, *refs):
    total = refs[0][...].astype(jnp.float32)
    for part in refs[1:count]:
        total = total + part[...].astype(jnp.float32)
    total = total * share
    query_out, kv_out = refs[count:]
    width = query_out.shape[1]
    query_out[...] = total[:, :width]
    kv_out[...] = total[:, width:]


def finish(parts, query_width, share):
    block, width = parts[0].shape
    step = min(block, 128)

    def spec(columns):
        return pl.BlockSpec((step, columns), lambda i: (i, 0))

    return pl.pallas_call(
        functools.partial(finish_kernel, len(parts), share),
        grid=(block // step,),
        out_shape=[
            shaped((block, query_width), jnp.float32),
            shaped((block, width - query_width), jnp.float32),
        ],
        in_specs=[spec(width)] * len(parts),
        out_specs=[spec(query_width), spec(width - query_width)],
        compiler_params=pltpu.CompilerParams(vmem_limit_bytes=32 * 2**20),
        cost_estimate=pl.CostEstimate(
            flops=0, bytes_accessed=(2 * len(parts) + 4) * block * width, transcendentals=0
        ),
    )(*parts)


def input_kernel(count, block, place, tokens, gain, grad_out, handed, *refs):
    parts, out, gathered = refs[:count], refs[count], refs[count + 1]
    rows = tokens.shape[0]
    core = place[1]
    total = parts[0][:rows].astype(jnp.float32)
    for part in parts[1:]:
        total = total + part[:rows].astype(jnp.float32)
    for k in range(total.shape[1] // block):
        columns = slice(k * block, (k + 1) * block)
        gathered[:, pl.ds(column_start(place[0] ^ k, core, block), block)] = total[:, columns]
        gathered[:, pl.ds(column_start(place[0] ^ k, 1 - core, block), block)] = handed[
            :, columns
        ].astype(jnp.float32)
    values = tokens[...].astype(jnp.float32)
    root_mean = jnp.sqrt(jnp.mean(values * values, axis=-1, keepdims=True) + epsilon)
    unit = values / root_mean
    scaled = gathered[...] * gain[...].astype(jnp.float32)
    correction = unit * jnp.mean(scaled * unit, axis=-1, keepdims=True)
    out[...] = (grad_out[...].astype(jnp.float32) + (scaled - correction) / root_mean).astype(
        jnp.bfloat16
    )


def local(tokens, norm_gain, query_weight, kv_weight, out_weight, grad_out, doc_lengths):
    tensor_size = lax.axis_size("tensor")
    data_size = lax.axis_size("dp")
    tensor_index = lax.axis_index("tensor")
    data_index = lax.axis_index("dp")
    chips = data_size // 2
    place = jnp.stack([data_index >> 1, data_index & 1, tensor_index]).astype(jnp.int32)
    sharers = tensor_size // KVH
    levels = sharers.bit_length() - 1
    rows, width = tokens.shape
    block = width // data_size
    query_width = query_weight.shape[1]
    gain = norm_gain.reshape(1, width)
    halves = [shaped((rows, width // 2))] * 2

    out_half = gather_outward(out_weight)
    keep, send = call(functools.partial(divide_kernel, block), halves, [grad_out], [place])
    grad_pair = jnp.concatenate([keep, swap(send, "dp", 1)], axis=0)
    grad_pair, joint_parts, inputs = lax.optimization_barrier(
        (grad_pair, (query_weight, kv_weight), (tokens, gain))
    )
    joint = jnp.concatenate(joint_parts, axis=1)

    def normed_pair():
        keep, send = call(
            functools.partial(norm_kernel, block),
            halves,
            inputs,
            [place],
            [pltpu.VMEM((rows, width), jnp.bfloat16)],
        )
        return jnp.concatenate([keep, swap(send, "dp", 1)], axis=0)

    def project_out(blocks):
        own, sent = project(place, blocks, [out_half], True, tensor_size, False)
        return own, swap(sent, "dp", 1)

    if chips == 4 and tensor_size == 4:
        normed_blocks, joint_blocks, out_own, out_sent = staged_gathers(
            grad_pair, normed_pair, joint, project_out
        )
    else:
        out_own, out_sent = project_out(everyone(grad_pair, "tensor", 1))
        normed_blocks = everyone(normed_pair(), "tensor", 1)
        joint_blocks = everyone(joint, "dp", 2)
    own, sent, normed = project(place, normed_blocks, joint_blocks, False, tensor_size, True)
    sent = swap(sent, "dp", 1)
    if levels:
        joined = (own + sent.astype(jnp.float32)).astype(jnp.bfloat16)
        keyvals = joined[:, query_width:]
        for bit_index in range(levels):
            partner = swap(keyvals, "tensor", 2**bit_index)
            upper = tensor_index >> bit_index & 1 == 1
            keyvals = jnp.concatenate(
                [jnp.where(upper, partner, keyvals), jnp.where(upper, keyvals, partner)], axis=1
            )
        own = jnp.concatenate([joined[:, :query_width], keyvals], axis=1).astype(jnp.float32)
        sent = jnp.zeros(own.shape, jnp.bfloat16)
    combined, *partial = attention(
        place, doc_lengths, out_own, out_sent, own, sent, rows, levels > 0
    )
    if levels:
        kv_partial = partial[0]
        for bit_index in reversed(range(levels)):
            half_cols = kv_partial.shape[1] // 2
            upper = tensor_index >> bit_index & 1 == 1
            lower_cols = kv_partial[:, :half_cols]
            higher_cols = kv_partial[:, half_cols:]
            kept = jnp.where(upper, higher_cols, lower_cols)
            handed = jnp.where(upper, lower_cols, higher_cols)
            kv_partial = kept + swap(handed.astype(jnp.bfloat16), "tensor", 2**bit_index).astype(
                jnp.float32
            )
        combined = jnp.concatenate([combined, kv_partial.astype(jnp.bfloat16)], axis=1)
    other = swap(combined, "dp", 1)

    row_blocks = row_terms(combined, other, joint_blocks, tensor_size)
    normed, *row_blocks = tied(normed, *row_blocks)
    far = weight_terms(normed, combined, other, chips - 1, 1, block)
    near = weight_terms(normed, combined, other, 0, chips - 1, block)
    row_parts = scatter_tensor(row_blocks)
    weight_parts = scatter_chips([*near, *far])
    handed = sum(part[rows:].astype(jnp.float32) for part in row_parts).astype(jnp.bfloat16)
    (input_grad,) = call(
        functools.partial(input_kernel, len(row_parts), block),
        [shaped((rows, width))],
        [tokens, gain, grad_out, swap(handed, "dp", 1), *row_parts],
        [place],
        [pltpu.VMEM((rows, width), jnp.float32)],
    )
    query_grad, kv_grad = finish(weight_parts, query_width, 1 / data_size)
    return (input_grad, query_grad, kv_grad)


def solution(mesh):
    placed = (
        P(("dp", "tensor"), None),
        P(),
        P("dp", "tensor"),
        P("dp", "tensor"),
        P("tensor", "dp"),
        P(("dp", "tensor"), None),
        P("dp", None),
    )
    return jax.shard_map(
        local,
        mesh=mesh,
        in_specs=placed,
        out_specs=(P(("dp", "tensor"), None), P("dp", "tensor"), P("dp", "tensor")),
        check_vma=False,
    )
```

```python
import functools
import math

import jax
import jax.numpy as jnp
from jax import lax
from jax.experimental import pallas as pl
from jax.experimental.pallas import tpu as pltpu
from jax.sharding import PartitionSpec as P

KVH = 4
HD = 128

epsilon = 1e-05
CONTRACT_LAST = (((1,), (1,)), ((), ()))
CONTRACT_FIRST = (((0,), (0,)), ((), ()))
WHOLE = pl.BlockSpec(memory_space=pltpu.VMEM)
SCALARS = pl.BlockSpec(memory_space=pltpu.SMEM)


def call(kernel, outs, operands, scalars=(), scratch=(), flops=0, megabytes=32):
    moved = sum(math.prod(a.shape) * a.dtype.itemsize for a in (*operands, *outs))
    return pl.pallas_call(
        kernel,
        out_shape=outs,
        in_specs=[SCALARS] * len(scalars) + [WHOLE] * len(operands),
        out_specs=[WHOLE] * len(outs),
        scratch_shapes=scratch,
        compiler_params=pltpu.CompilerParams(vmem_limit_bytes=megabytes * 2**20),
        cost_estimate=pl.CostEstimate(flops=flops, bytes_accessed=moved, transcendentals=0),
    )(*scalars, *operands)


def shaped(shape, dtype=jnp.bfloat16):
    return jax.ShapeDtypeStruct(shape, dtype)


def dot(left, right, contract=(((1,), (0,)), ((), ()))):
    return lax.dot_general(left, right, contract, preferred_element_type=jnp.float32)


def swap(value, axis, mask):
    pairs = [(source, source ^ mask) for source in range(lax.axis_size(axis))]
    return lax.ppermute(value, axis, pairs)


def tied(*values):
    return lax.optimization_barrier(values)


def everyone(value, axis, unit):
    size = lax.axis_size(axis) // unit
    return [value] + [swap(value, axis, unit * k) for k in range(1, size)]


def gather_chips(value, axis):
    if lax.axis_size("dp") != 8:
        return everyone(value, "dp", 2)
    near_x = swap(value, "dp", 2)
    near_y = swap(value, "dp", 4)
    near_x, near_y = tied(near_x, near_y)
    far_top = swap(jnp.split(near_x, 2, axis)[0], "dp", 4)
    far_bottom = swap(jnp.split(near_y, 2, axis)[1], "dp", 2)
    return [value, near_x, near_y, far_top, far_bottom]


def along(value, pairs):
    return lax.ppermute(value, "tensor", pairs)


def gather_tensor(value):
    if lax.axis_size("tensor") != 4:
        return everyone(value, "tensor", 1)
    right_one = along(value, [(0, 1), (1, 2), (2, 3)])
    left_one = along(value, [(1, 0), (2, 1), (3, 2)])
    right_one, left_one = tied(right_one, left_one)
    right_two = along(right_one, [(1, 2), (2, 3)])
    left_two = along(left_one, [(1, 0), (2, 1)])
    right_two, left_two = tied(right_two, left_two)
    last = along(
        jnp.where(lax.axis_index("tensor") == 1, left_two, right_two), [(1, 0), (2, 3)]
    )
    return [value, right_one, left_one, right_two, left_two, last]


def pick(index, pieces, size, k, rows):
    if len(pieces) == size:
        return pieces[k][rows]
    own, right_one, left_one, right_two, left_two, last = [piece.at[rows] for piece in pieces]
    if k == 0:
        return own[...]
    if k == 1:
        return jnp.where(index % 2 == 1, right_one[...], left_one[...])
    if k == 2:
        return jnp.where(index >= 2, right_two[...], left_two[...])
    near = jnp.where(index == 1, left_one[...], right_one[...])
    return jnp.where(jnp.logical_or(index == 0, index == 3), last[...], near)


def inner_pair(value):
    return along(value, [(1, 2), (2, 1)])


def outer_pair(value):
    return along(value, [(3, 2), (0, 1)])


def scatter_chips(blocks):
    if len(blocks) != 4:
        return [blocks[0]] + [swap(blocks[k], "dp", 2 * k) for k in range(1, len(blocks))]
    half = blocks[0].shape[0] // 2
    far_top = swap(blocks[3][:half], "dp", 4)
    far_bottom = swap(blocks[3][half:], "dp", 2)
    near_x = swap(
        jnp.concatenate([blocks[1][:half] + far_top, blocks[1][half:]], axis=0), "dp", 2
    )
    near_y = swap(
        jnp.concatenate([blocks[2][:half], blocks[2][half:] + far_bottom], axis=0), "dp", 4
    )
    return [blocks[0], near_x, near_y]


def scatter_tensor(blocks):
    if len(blocks) != 4:
        return [blocks[0]] + [swap(blocks[k], "tensor", k) for k in range(1, len(blocks))]
    outer, inner = outer_pair(blocks[3]), inner_pair(blocks[3])
    outer, inner = tied(outer, inner)
    two, one = swap(blocks[2] + outer, "tensor", 2), swap(blocks[1], "tensor", 1)
    return [blocks[0], one, inner, two]


def column_start(place, k, which, block):
    return pl.multiple_of(((place[0] ^ k) * 2 + which) * block, 128)


def prepare_kernel(block, place, grad_out, tokens, gain, keep, send, normed):
    rows, core = tokens.shape[0], place[1]
    values = tokens[...].astype(jnp.float32)
    root_mean = jnp.sqrt(jnp.mean(values * values, axis=-1, keepdims=True) + epsilon)
    normed[...] = (values / root_mean * gain[...].astype(jnp.float32)).astype(jnp.bfloat16)
    for start, source in ((0, grad_out), (rows, normed)):
        for k in range(keep.shape[1] // block):
            place_out = (slice(start, start + rows), slice(k * block, (k + 1) * block))
            keep[place_out] = source[:, pl.ds(column_start(place, k, core, block), block)]
            send[place_out] = source[:, pl.ds(column_start(place, k, 1 - core, block), block)]


def project_kernel(pieces, weights, size, first, transposed, place, *refs):
    row_refs, weight_refs = refs[:pieces], refs[pieces : pieces + weights]
    keep, send, pair = refs[pieces + weights :]
    rows = row_refs[0].shape[0] // 4
    length = rows * size
    for core in range(2):
        start = first + 2 * core * rows
        for k in range(size):
            target = core * length + k * rows
            pair[target : target + rows] = pick(
                place[2], row_refs, size, k, slice(start, start + rows)
            )
    width = keep.shape[1]
    tile = 256 if width % 256 == 0 else width

    def step(columns):
        start, total = 0, None
        for weight in weight_refs:
            depth = weight.shape[1 if transposed else 0]
            left = pair[:, start : start + depth]
            if transposed:
                term = dot(left, weight[columns, :], CONTRACT_LAST)
            else:
                term = dot(left, weight[:, columns])
            total = term if total is None else total + term
            start += depth
        keep[:, columns] = total[:length]
        send[:, columns] = total[length:].astype(jnp.bfloat16)

    if tile == width:
        step(slice(0, width))
    else:

        @pl.loop(0, width // tile)
        def _(number):
            step(pl.ds(pl.multiple_of(number * tile, tile), tile))


def project(place, pieces, weights, first, transposed, size, keep_pair):
    rows = pieces[0].shape[0] // 4 * size
    half = pieces[0].shape[1]
    width = weights[0].shape[0 if transposed else 1]
    outs = [shaped((rows, width), jnp.float32), shaped((rows, width))]
    pair = shaped((2 * rows, half))
    return call(
        functools.partial(project_kernel, len(pieces), len(weights), size, first, transposed),
        [*outs, pair] if keep_pair else outs,
        [*pieces, *weights],
        [place],
        () if keep_pair else [pltpu.VMEM(pair.shape, pair.dtype)],
        flops=4 * rows * half * width,
    )


def attention_kernel(rows, heads, place, lengths, out_own, out_sent, own, sent, grads, partial):
    length = out_own.shape[0]
    width = heads * HD
    scale = 1 / math.sqrt(HD)
    tensor_index = place[2]

    def positions_of(dimension):
        order = lax.broadcasted_iota(jnp.int32, (length, length), dimension)
        return ((order // rows) ^ tensor_index) * rows + order % rows

    def labels_of(positions):
        labels, end = jnp.zeros((length, length), jnp.int32), 0
        for document in range(lengths.shape[1]):
            end = end + lengths[0, document]
            labels = labels + (end <= positions).astype(jnp.int32)
        return labels

    key_positions, query_positions = positions_of(0), positions_of(1)
    allowed = jnp.logical_and(
        labels_of(key_positions) == labels_of(query_positions), key_positions <= query_positions
    )

    def joined(first, second, columns):
        return (first[:, columns] + second[:, columns].astype(jnp.float32)).astype(jnp.bfloat16)

    keys = joined(own, sent, slice(width, width + HD))
    values = joined(own, sent, slice(width + HD, width + 2 * HD))
    key_total = value_total = None
    for head in range(heads):
        columns = slice(head * HD, (head + 1) * HD)
        queries = joined(own, sent, columns)
        out_grad = joined(out_own, out_sent, columns)
        scores = jnp.where(allowed, dot(keys, queries, CONTRACT_LAST) * scale, -1e30)
        expo = jnp.exp(scores - jnp.max(scores, axis=0, keepdims=True))
        probs = expo * (1 / jnp.sum(expo, axis=0, keepdims=True))
        prob_grad = dot(values, out_grad, CONTRACT_LAST)
        inner = jnp.sum(probs * prob_grad, axis=0, keepdims=True)
        score_grad = (probs * (prob_grad - inner) * scale).astype(jnp.bfloat16)
        grads[:, columns] = dot(score_grad, keys, CONTRACT_FIRST).astype(jnp.bfloat16)
        key_term = dot(score_grad, queries)
        value_term = dot(probs.astype(jnp.bfloat16), out_grad)
        key_total = key_term if head == 0 else key_total + key_term
        value_total = value_term if head == 0 else value_total + value_term
    if partial is None:
        grads[:, width : width + HD] = key_total.astype(jnp.bfloat16)
        grads[:, width + HD :] = value_total.astype(jnp.bfloat16)
    else:
        partial[:, :HD] = key_total
        partial[:, HD:] = value_total


def attention(place, lengths, out_own, out_sent, own, sent, rows, split):
    length, width = out_own.shape
    outs = [shaped((length, width if split else width + 2 * HD))]
    if split:
        outs.append(shaped((length, 2 * HD), jnp.float32))

    def kernel(*refs):
        attention_kernel(rows, width // HD, *(refs if split else (*refs, None)))

    return call(
        kernel,
        outs,
        [out_own, out_sent, own, sent],
        [place, lengths],
        flops=10 * length * length * width,
    )


def weight_kernel(first, block, pair, own, other, *outs):
    length = own.shape[0]
    tile = min(block, 256)
    for number, out in enumerate(outs):
        for part in range(block // tile):
            start = (first + number) * block + part * tile
            out[part * tile : (part + 1) * tile] = (
                dot(pair[:length, start : start + tile], own[...], CONTRACT_FIRST)
                + dot(pair[length:, start : start + tile], other[...], CONTRACT_FIRST)
            ).astype(jnp.bfloat16)


def weight_terms(pair, own, other, first, count, block):
    return call(
        functools.partial(weight_kernel, first, block),
        [shaped((block, own.shape[1]))] * count,
        [pair, own, other],
        flops=2 * pair.shape[0] * block * count * own.shape[1],
    )


def row_kernel(weights, own, other, *refs):
    weight_refs, outs = refs[:weights], refs[weights:]
    length = own.shape[0]
    rows = length // len(outs)
    start = 0
    for weight in weight_refs:
        tile = min(weight.shape[0], 256)
        for part in range(weight.shape[0] // tile):
            right = weight[part * tile : (part + 1) * tile, :]
            for offset, left in ((0, own), (rows, other)):
                term = dot(left[...], right, CONTRACT_LAST).astype(jnp.bfloat16)
                for k, out in enumerate(outs):
                    out[offset : offset + rows, start : start + tile] = term[
                        k * rows : (k + 1) * rows
                    ]
            start += tile


def row_terms(own, other, weights, size):
    length, width = own.shape
    half = sum(weight.shape[0] for weight in weights)
    return call(
        functools.partial(row_kernel, len(weights)),
        [shaped((2 * length // size, half))] * size,
        [own, other, *weights],
        flops=4 * length * width * half,
    )


def finish_kernel(count, share, *refs):
    total = refs[0][...].astype(jnp.float32)
    for part in refs[1:count]:
        total = total + part[...].astype(jnp.float32)
    total = total * share
    query_out, kv_out = refs[count:]
    width = query_out.shape[1]
    query_out[...] = total[:, :width]
    kv_out[...] = total[:, width:]


def finish(parts, query_width, share):
    block, width = parts[0].shape
    step = min(block, 128)

    def spec(columns):
        return pl.BlockSpec((step, columns), lambda i: (i, 0))

    return pl.pallas_call(
        functools.partial(finish_kernel, len(parts), share),
        grid=(block // step,),
        out_shape=[
            shaped((block, query_width), jnp.float32),
            shaped((block, width - query_width), jnp.float32),
        ],
        in_specs=[spec(width)] * len(parts),
        out_specs=[spec(query_width), spec(width - query_width)],
        compiler_params=pltpu.CompilerParams(vmem_limit_bytes=32 * 2**20),
        cost_estimate=pl.CostEstimate(
            flops=0, bytes_accessed=(2 * len(parts) + 4) * block * width, transcendentals=0
        ),
    )(*parts)


def input_kernel(count, block, place, tokens, gain, grad_out, handed, *refs):
    parts, out, gathered = refs[:count], refs[count], refs[count + 1]
    rows = tokens.shape[0]
    core = place[1]
    total = parts[0][:rows].astype(jnp.float32)
    for part in parts[1:]:
        total = total + part[:rows].astype(jnp.float32)
    for k in range(total.shape[1] // block):
        columns = slice(k * block, (k + 1) * block)
        gathered[:, pl.ds(column_start(place, k, core, block), block)] = total[:, columns]
        gathered[:, pl.ds(column_start(place, k, 1 - core, block), block)] = handed[
            :, columns
        ].astype(jnp.float32)
    values = tokens[...].astype(jnp.float32)
    root_mean = jnp.sqrt(jnp.mean(values * values, axis=-1, keepdims=True) + epsilon)
    unit = values / root_mean
    scaled = gathered[...] * gain[...].astype(jnp.float32)
    correction = unit * jnp.mean(scaled * unit, axis=-1, keepdims=True)
    out[...] = (grad_out[...].astype(jnp.float32) + (scaled - correction) / root_mean).astype(
        jnp.bfloat16
    )


def local(tokens, norm_gain, query_weight, kv_weight, out_weight, grad_out, doc_lengths):
    tensor_size = lax.axis_size("tensor")
    data_size = lax.axis_size("dp")
    tensor_index = lax.axis_index("tensor")
    data_index = lax.axis_index("dp")
    chips = data_size // 2
    place = jnp.stack([data_index >> 1, data_index & 1, tensor_index]).astype(jnp.int32)
    sharers = tensor_size // KVH
    levels = sharers.bit_length() - 1
    rows, width = tokens.shape
    block = width // data_size
    query_width = query_weight.shape[1]
    gain = norm_gain.reshape(1, width)

    keep, send = call(
        functools.partial(prepare_kernel, block),
        [shaped((2 * rows, width // 2))] * 2,
        [grad_out, tokens, gain],
        [place],
        [pltpu.VMEM((rows, width), jnp.bfloat16)],
    )
    row_pieces = gather_tensor(jnp.concatenate([keep, swap(send, "dp", 1)], axis=0))
    joint_blocks = gather_chips(jnp.concatenate([query_weight, kv_weight], axis=1), 0)
    *joint_blocks, out_weight = tied(*joint_blocks, out_weight)
    out_blocks = gather_chips(out_weight, 1)

    own, sent, normed = project(
        place, row_pieces, joint_blocks, rows, False, tensor_size, True
    )
    sent = swap(sent, "dp", 1)
    out_own, out_sent = project(place, row_pieces, out_blocks, 0, True, tensor_size, False)
    out_sent = swap(out_sent, "dp", 1)
    if levels:
        joined = (own + sent.astype(jnp.float32)).astype(jnp.bfloat16)
        keyvals = joined[:, query_width:]
        for bit_index in range(levels):
            partner = swap(keyvals, "tensor", 2**bit_index)
            upper = tensor_index >> bit_index & 1 == 1
            keyvals = jnp.concatenate(
                [jnp.where(upper, partner, keyvals), jnp.where(upper, keyvals, partner)], axis=1
            )
        own = jnp.concatenate([joined[:, :query_width], keyvals], axis=1).astype(jnp.float32)
        sent = jnp.zeros(own.shape, jnp.bfloat16)
    combined, *partial = attention(
        place, doc_lengths, out_own, out_sent, own, sent, rows, levels > 0
    )
    if levels:
        kv_partial = partial[0]
        for bit_index in reversed(range(levels)):
            half_cols = kv_partial.shape[1] // 2
            upper = tensor_index >> bit_index & 1 == 1
            lower_cols = kv_partial[:, :half_cols]
            higher_cols = kv_partial[:, half_cols:]
            kept = jnp.where(upper, higher_cols, lower_cols)
            handed = jnp.where(upper, lower_cols, higher_cols)
            kv_partial = kept + swap(handed.astype(jnp.bfloat16), "tensor", 2**bit_index).astype(
                jnp.float32
            )
        combined = jnp.concatenate([combined, kv_partial.astype(jnp.bfloat16)], axis=1)
    other = swap(combined, "dp", 1)

    far = weight_terms(normed, combined, other, chips - 1, 1, block)
    near = weight_terms(normed, combined, other, 0, chips - 1, block)
    row_parts = scatter_tensor(row_terms(combined, other, joint_blocks, tensor_size))
    weight_parts = scatter_chips([*near, *far])
    handed = sum(part[rows:].astype(jnp.float32) for part in row_parts).astype(jnp.bfloat16)
    (input_grad,) = call(
        functools.partial(input_kernel, len(row_parts), block),
        [shaped((rows, width))],
        [tokens, gain, grad_out, swap(handed, "dp", 1), *row_parts],
        [place],
        [pltpu.VMEM((rows, width), jnp.float32)],
    )
    query_grad, kv_grad = finish(weight_parts, query_width, 1 / data_size)
    return (input_grad, query_grad, kv_grad)


def solution(mesh):
    placed = (
        P(("dp", "tensor"), None),
        P(),
        P("dp", "tensor"),
        P("dp", "tensor"),
        P("tensor", "dp"),
        P(("dp", "tensor"), None),
        P("dp", None),
    )
    return jax.shard_map(
        local,
        mesh=mesh,
        in_specs=placed,
        out_specs=(P(("dp", "tensor"), None), P("dp", "tensor"), P("dp", "tensor")),
        check_vma=False,
    )
```

```python
import functools
import math

import jax
import jax.numpy as jnp
from jax import lax
from jax.experimental import pallas as pl
from jax.experimental.pallas import tpu as pltpu
from jax.sharding import PartitionSpec as P

KVH = 4
HD = 128

epsilon = 1e-05
CONTRACT_LAST = (((1,), (1,)), ((), ()))
CONTRACT_FIRST = (((0,), (0,)), ((), ()))
WHOLE = pl.BlockSpec(memory_space=pltpu.VMEM)
SCALARS = pl.BlockSpec(memory_space=pltpu.SMEM)


def call(kernel, outs, operands, scalars=(), scratch=(), flops=0, megabytes=24):
    moved = sum(math.prod(a.shape) * a.dtype.itemsize for a in (*operands, *outs))
    return pl.pallas_call(
        kernel,
        out_shape=outs,
        in_specs=[SCALARS] * len(scalars) + [WHOLE] * len(operands),
        out_specs=[WHOLE] * len(outs),
        scratch_shapes=scratch,
        compiler_params=pltpu.CompilerParams(vmem_limit_bytes=megabytes * 2**20),
        cost_estimate=pl.CostEstimate(flops=flops, bytes_accessed=moved, transcendentals=0),
    )(*scalars, *operands)


def shaped(shape, dtype=jnp.bfloat16):
    return jax.ShapeDtypeStruct(shape, dtype)


def dot(left, right, contract=(((1,), (0,)), ((), ()))):
    return lax.dot_general(left, right, contract, preferred_element_type=jnp.float32)


def swap(value, axis, mask):
    pairs = [(source, source ^ mask) for source in range(lax.axis_size(axis))]
    return lax.ppermute(value, axis, pairs)


def tied(*values):
    return lax.optimization_barrier(values)


def everyone(value, axis, unit):
    size = lax.axis_size(axis) // unit
    return [value] + [swap(value, axis, unit * k) for k in range(1, size)]


def gather_chips(value):
    if lax.axis_size("dp") != 8:
        return everyone(value, "dp", 2), []
    half = value.shape[0] // 2
    near_x = swap(value, "dp", 2)
    near_y = swap(value, "dp", 4)
    near_x, near_y = tied(near_x, near_y)
    far_top = swap(near_x[:half], "dp", 4)
    far_bottom = swap(near_y[half:], "dp", 2)
    return [value, near_x, near_y], [far_top, far_bottom]


def along(value, pairs):
    return lax.ppermute(value, "tensor", pairs)


def gather_tensor(value):
    if lax.axis_size("tensor") != 4:
        return everyone(value, "tensor", 1)
    right_one = along(value, [(0, 1), (1, 2), (2, 3)])
    left_one = along(value, [(1, 0), (2, 1), (3, 2)])
    right_one, left_one = tied(right_one, left_one)
    right_two = along(right_one, [(1, 2), (2, 3)])
    left_two = along(left_one, [(1, 0), (2, 1)])
    right_two, left_two = tied(right_two, left_two)
    last = along(
        jnp.where(lax.axis_index("tensor") == 1, left_two, right_two), [(1, 0), (2, 3)]
    )
    return [value, right_one, left_one, right_two, left_two, last]


def pick(index, pieces, size, k, rows):
    if len(pieces) == size:
        return pieces[k][rows]
    own, right_one, left_one, right_two, left_two, last = [piece.at[rows] for piece in pieces]
    if k == 0:
        return own[...]
    if k == 1:
        return jnp.where(index % 2 == 1, right_one[...], left_one[...])
    if k == 2:
        return jnp.where(index >= 2, right_two[...], left_two[...])
    near = jnp.where(index == 1, left_one[...], right_one[...])
    return jnp.where(jnp.logical_or(index == 0, index == 3), last[...], near)


def inner_pair(value):
    return along(value, [(1, 2), (2, 1)])


def outer_pair(value):
    return along(value, [(3, 2), (0, 1)])


def scatter_chips(blocks):
    if len(blocks) != 4:
        return [blocks[0]] + [swap(blocks[k], "dp", 2 * k) for k in range(1, len(blocks))]
    half = blocks[0].shape[0] // 2
    far_top = swap(blocks[3][:half], "dp", 4)
    far_bottom = swap(blocks[3][half:], "dp", 2)
    near_x = swap(
        jnp.concatenate([blocks[1][:half] + far_top, blocks[1][half:]], axis=0), "dp", 2
    )
    near_y = swap(
        jnp.concatenate([blocks[2][:half], blocks[2][half:] + far_bottom], axis=0), "dp", 4
    )
    return [blocks[0], near_x, near_y]


def scatter_tensor(blocks):
    if len(blocks) != 4:
        return [blocks[0]] + [swap(blocks[k], "tensor", k) for k in range(1, len(blocks))]
    outer, inner = outer_pair(blocks[3]), inner_pair(blocks[3])
    outer, inner = tied(outer, inner)
    carried, adjacent = tied(blocks[2] + outer, blocks[1])
    two, one = swap(carried, "tensor", 2), swap(adjacent, "tensor", 1)
    return [blocks[0], one, inner, two]


def column_start(place, k, which, block):
    return pl.multiple_of(((place[0] ^ k) * 2 + which) * block, 128)


def prepare_kernel(block, place, grad_out, tokens, gain, keep, send, normed):
    rows, core = tokens.shape[0], place[1]
    values = tokens[...].astype(jnp.float32)
    root_mean = jnp.sqrt(jnp.mean(values * values, axis=-1, keepdims=True) + epsilon)
    normed[...] = (values / root_mean * gain[...].astype(jnp.float32)).astype(jnp.bfloat16)
    for start, source in ((0, grad_out), (rows, normed)):
        for k in range(keep.shape[1] // block):
            place_out = (slice(start, start + rows), slice(k * block, (k + 1) * block))
            keep[place_out] = source[:, pl.ds(column_start(place, k, core, block), block)]
            send[place_out] = source[:, pl.ds(column_start(place, k, 1 - core, block), block)]


def merge_kernel(out_weight, query_weight, kv_weight, merged):
    block, start = merged.shape[0], 0
    for chunk in range(out_weight.shape[0] // block):
        merged[:, start : start + block] = out_weight[chunk * block : (chunk + 1) * block]
        start += block
    for weight in (query_weight, kv_weight):
        merged[:, start : start + weight.shape[1]] = weight[...]
        start += weight.shape[1]


def products(grads, normed, weights, first, out_width, block, columns):
    chunks = out_width // block
    size = weights[0].shape[0]
    if columns < out_width:
        chunk = columns // block
        for row in range(0, block, min(size, 256)):
            total = None
            if size == block:
                for k, weight in enumerate(weights):
                    right = weight[row : row + min(size, 256), chunk * block : (chunk + 1) * block]
                    left = grads[:, first + k * block : first + (k + 1) * block]
                    term = dot(left, right, CONTRACT_LAST)
                    total = term if total is None else total + term
            else:
                right = weights[row // size][:, chunk * block : (chunk + 1) * block]
                total = dot(grads[:, first : first + block], right, CONTRACT_LAST)
            yield slice(columns + row, columns + row + min(size, 256)), total
    else:
        width = min(256, weights[0].shape[1] - columns)
        total = None
        for k, weight in enumerate(weights):
            left = normed[:, first + k * size : first + (k + 1) * size]
            term = dot(left, weight[:, columns : columns + width])
            total = term if total is None else total + term
        yield slice(columns, columns + width), total


def column_steps(out_width, width, block):
    return [*range(0, out_width, block), *range(out_width, width, 256)]


def early_kernel(pieces, weights, size, out_width, place, *refs):
    row_refs, weight_refs = refs[:pieces], refs[pieces : pieces + weights]
    total, grads, normed = refs[pieces + weights :]
    rows = row_refs[0].shape[0] // 4
    block = weight_refs[0].shape[0]
    for core in range(2):
        for number, pair in enumerate((grads, normed)):
            start = (2 * core + number) * rows
            for k in range(size):
                target = (core * size + k) * rows
                pair[target : target + rows] = pick(
                    place[2], row_refs, size, k, slice(start, start + rows)
                )
    for columns in column_steps(out_width, total.shape[1], block):
        for place_out, value in products(grads, normed, weight_refs, 0, out_width, block, columns):
            total[:, place_out] = value


def late_kernel(first, out_width, block, total, grads, normed, *refs):
    weight_refs, (keep, send) = refs[:-2], refs[-2:]
    length = keep.shape[0]
    if not weight_refs:
        keep[...] = total[:length]
        send[...] = total[length:].astype(jnp.bfloat16)
    for columns in column_steps(out_width, keep.shape[1], block) if weight_refs else []:
        for place_out, value in products(
            grads, normed, weight_refs, first, out_width, block, columns
        ):
            keep[:, place_out] = total[:length, place_out] + value[:length]
            send[:, place_out] = (total[length:, place_out] + value[length:]).astype(jnp.bfloat16)


def project(place, pieces, early, late, size, out_width):
    rows = pieces[0].shape[0] // 4 * size
    half = pieces[0].shape[1]
    block, width = early[0].shape
    first = len(early) * block
    total, grads, normed = call(
        functools.partial(early_kernel, len(pieces), len(early), size, out_width),
        [shaped((2 * rows, width), jnp.float32)] + [shaped((2 * rows, half))] * 2,
        [*pieces, *early],
        [place],
        flops=4 * rows * first * width,
        megabytes=24,
    )
    own, sent = call(
        functools.partial(late_kernel, first, out_width, block),
        [shaped((rows, width), jnp.float32), shaped((rows, width))],
        [total, grads, normed, *late],
        flops=4 * rows * (half - first) * width,
        megabytes=24,
    )
    return own, sent, normed


def attention_kernel(rows, heads, place, lengths, own, sent, grads, partial):
    length = own.shape[0]
    width = heads * HD
    scale = 1 / math.sqrt(HD)
    tensor_index = place[2]

    def positions_of(dimension):
        order = lax.broadcasted_iota(jnp.int32, (length, length), dimension)
        return ((order // rows) ^ tensor_index) * rows + order % rows

    def labels_of(positions):
        labels, end = jnp.zeros((length, length), jnp.int32), 0
        for document in range(lengths.shape[1]):
            end = end + lengths[0, document]
            labels = labels + (end <= positions).astype(jnp.int32)
        return labels

    key_positions, query_positions = positions_of(0), positions_of(1)
    allowed = jnp.logical_and(
        labels_of(key_positions) == labels_of(query_positions), key_positions <= query_positions
    )

    def joined(first, second, columns):
        return (first[:, columns] + second[:, columns].astype(jnp.float32)).astype(jnp.bfloat16)

    keys = joined(own, sent, slice(2 * width, 2 * width + HD))
    values = joined(own, sent, slice(2 * width + HD, 2 * width + 2 * HD))
    key_total = value_total = None
    for head in range(heads):
        columns = slice(head * HD, (head + 1) * HD)
        out_grad = joined(own, sent, columns)
        queries = joined(own, sent, slice(width + head * HD, width + (head + 1) * HD))
        scores = jnp.where(allowed, dot(keys, queries, CONTRACT_LAST) * scale, -1e30)
        expo = jnp.exp(scores - jnp.max(scores, axis=0, keepdims=True))
        probs = expo * (1 / jnp.sum(expo, axis=0, keepdims=True))
        prob_grad = dot(values, out_grad, CONTRACT_LAST)
        inner = jnp.sum(probs * prob_grad, axis=0, keepdims=True)
        score_grad = (probs * (prob_grad - inner) * scale).astype(jnp.bfloat16)
        grads[:, columns] = dot(score_grad, keys, CONTRACT_FIRST).astype(jnp.bfloat16)
        key_term = dot(score_grad, queries)
        value_term = dot(probs.astype(jnp.bfloat16), out_grad)
        key_total = key_term if head == 0 else key_total + key_term
        value_total = value_term if head == 0 else value_total + value_term
    if partial is None:
        grads[:, width : width + HD] = key_total.astype(jnp.bfloat16)
        grads[:, width + HD :] = value_total.astype(jnp.bfloat16)
    else:
        partial[:, :HD] = key_total
        partial[:, HD:] = value_total


def attention(place, lengths, own, sent, rows, width, split):
    length = own.shape[0]
    outs = [shaped((length, width if split else width + 2 * HD))]
    if split:
        outs.append(shaped((length, 2 * HD), jnp.float32))

    def kernel(*refs):
        attention_kernel(rows, width // HD, *(refs if split else (*refs, None)))

    return call(
        kernel,
        outs,
        [own, sent],
        [place, lengths],
        flops=10 * length * length * width,
    )


def weight_kernel(first, block, pair, own, other, *outs):
    length = own.shape[0]
    tile = min(block, 256)
    for number, out in enumerate(outs):
        for part in range(block // tile):
            start = (first + number) * block + part * tile
            out[part * tile : (part + 1) * tile] = (
                dot(pair[:length, start : start + tile], own[...], CONTRACT_FIRST)
                + dot(pair[length:, start : start + tile], other[...], CONTRACT_FIRST)
            ).astype(jnp.bfloat16)


def weight_terms(pair, own, other, first, count, block):
    return call(
        functools.partial(weight_kernel, first, block),
        [shaped((block, own.shape[1]))] * count,
        [pair, own, other],
        flops=2 * pair.shape[0] * block * count * own.shape[1],
    )


def row_kernel(weights, offset_columns, own, other, *refs):
    weight_refs, outs = refs[:weights], refs[weights:]
    length = own.shape[0]
    rows = length // len(outs)
    start = 0
    for weight in weight_refs:
        tile = min(weight.shape[0], 256)
        for part in range(weight.shape[0] // tile):
            right = weight[part * tile : (part + 1) * tile, offset_columns:]
            for offset, left in ((0, own), (rows, other)):
                term = dot(left[...], right, CONTRACT_LAST).astype(jnp.bfloat16)
                for k, out in enumerate(outs):
                    out[offset : offset + rows, start : start + tile] = term[
                        k * rows : (k + 1) * rows
                    ]
            start += tile


def row_terms(own, other, weights, size, out_width):
    length, width = own.shape
    half = sum(weight.shape[0] for weight in weights)
    return call(
        functools.partial(row_kernel, len(weights), out_width),
        [shaped((2 * length // size, half))] * size,
        [own, other, *weights],
        flops=4 * length * width * half,
    )


def finish_kernel(count, share, *refs):
    total = refs[0][...].astype(jnp.float32)
    for part in refs[1:count]:
        total = total + part[...].astype(jnp.float32)
    total = total * share
    query_out, kv_out = refs[count:]
    width = query_out.shape[1]
    query_out[...] = total[:, :width]
    kv_out[...] = total[:, width:]


def finish(parts, query_width, share):
    block, width = parts[0].shape
    step = min(block, 128)

    def spec(columns):
        return pl.BlockSpec((step, columns), lambda i: (i, 0))

    return pl.pallas_call(
        functools.partial(finish_kernel, len(parts), share),
        grid=(block // step,),
        out_shape=[
            shaped((block, query_width), jnp.float32),
            shaped((block, width - query_width), jnp.float32),
        ],
        in_specs=[spec(width)] * len(parts),
        out_specs=[spec(query_width), spec(width - query_width)],
        compiler_params=pltpu.CompilerParams(vmem_limit_bytes=32 * 2**20),
        cost_estimate=pl.CostEstimate(
            flops=0, bytes_accessed=(2 * len(parts) + 4) * block * width, transcendentals=0
        ),
    )(*parts)


def input_kernel(count, block, place, tokens, gain, grad_out, handed, *refs):
    parts, out, gathered = refs[:count], refs[count], refs[count + 1]
    rows = tokens.shape[0]
    core = place[1]
    total = parts[0][:rows].astype(jnp.float32)
    for part in parts[1:]:
        total = total + part[:rows].astype(jnp.float32)
    for k in range(total.shape[1] // block):
        columns = slice(k * block, (k + 1) * block)
        gathered[:, pl.ds(column_start(place, k, core, block), block)] = total[:, columns]
        gathered[:, pl.ds(column_start(place, k, 1 - core, block), block)] = handed[
            :, columns
        ].astype(jnp.float32)
    values = tokens[...].astype(jnp.float32)
    root_mean = jnp.sqrt(jnp.mean(values * values, axis=-1, keepdims=True) + epsilon)
    unit = values / root_mean
    scaled = gathered[...] * gain[...].astype(jnp.float32)
    correction = unit * jnp.mean(scaled * unit, axis=-1, keepdims=True)
    out[...] = (grad_out[...].astype(jnp.float32) + (scaled - correction) / root_mean).astype(
        jnp.bfloat16
    )


def local(tokens, norm_gain, query_weight, kv_weight, out_weight, grad_out, doc_lengths):
    tensor_size = lax.axis_size("tensor")
    data_size = lax.axis_size("dp")
    tensor_index = lax.axis_index("tensor")
    data_index = lax.axis_index("dp")
    chips = data_size // 2
    place = jnp.stack([data_index >> 1, data_index & 1, tensor_index]).astype(jnp.int32)
    sharers = tensor_size // KVH
    levels = sharers.bit_length() - 1
    rows, width = tokens.shape
    block = width // data_size
    query_width = query_weight.shape[1]
    gain = norm_gain.reshape(1, width)

    keep, send = call(
        functools.partial(prepare_kernel, block),
        [shaped((2 * rows, width // 2))] * 2,
        [grad_out, tokens, gain],
        [place],
        [pltpu.VMEM((rows, width), jnp.bfloat16)],
    )
    out_width = out_weight.shape[0]
    send, out_weight, query_weight, kv_weight = tied(send, out_weight, query_weight, kv_weight)
    row_pieces = gather_tensor(jnp.concatenate([keep, swap(send, "dp", 1)], axis=0))
    (merged,) = call(
        merge_kernel,
        [shaped((block, out_width + query_width + kv_weight.shape[1]))],
        [out_weight, query_weight, kv_weight],
    )
    early, late = gather_chips(merged)
    own, sent, normed = project(place, row_pieces, early, late, tensor_size, out_width)
    sent = swap(sent, "dp", 1)
    if levels:
        joined = (own + sent.astype(jnp.float32)).astype(jnp.bfloat16)
        keyvals = joined[:, out_width + query_width :]
        for bit_index in range(levels):
            partner = swap(keyvals, "tensor", 2**bit_index)
            upper = tensor_index >> bit_index & 1 == 1
            keyvals = jnp.concatenate(
                [jnp.where(upper, partner, keyvals), jnp.where(upper, keyvals, partner)], axis=1
            )
        own = jnp.concatenate(
            [joined[:, : out_width + query_width], keyvals], axis=1
        ).astype(jnp.float32)
        sent = jnp.zeros(own.shape, jnp.bfloat16)
    combined, *partial = attention(place, doc_lengths, own, sent, rows, query_width, levels > 0)
    if levels:
        kv_partial = partial[0]
        for bit_index in reversed(range(levels)):
            half_cols = kv_partial.shape[1] // 2
            upper = tensor_index >> bit_index & 1 == 1
            lower_cols = kv_partial[:, :half_cols]
            higher_cols = kv_partial[:, half_cols:]
            kept = jnp.where(upper, higher_cols, lower_cols)
            handed = jnp.where(upper, lower_cols, higher_cols)
            kv_partial = kept + swap(handed.astype(jnp.bfloat16), "tensor", 2**bit_index).astype(
                jnp.float32
            )
        combined = jnp.concatenate([combined, kv_partial.astype(jnp.bfloat16)], axis=1)
    other = swap(combined, "dp", 1)

    far = weight_terms(normed, combined, other, chips - 1, 1, block)
    near = weight_terms(normed, combined, other, 0, chips - 1, block)
    row_parts = scatter_tensor(row_terms(combined, other, early + late, tensor_size, out_width))
    weight_parts = scatter_chips([*near, *far])
    handed = sum(part[rows:].astype(jnp.float32) for part in row_parts).astype(jnp.bfloat16)
    handed = swap(handed, "dp", 1)
    query_grad, kv_grad = finish(weight_parts, query_width, 1 / data_size)
    handed, query_grad, kv_grad = tied(handed, query_grad, kv_grad)
    (input_grad,) = call(
        functools.partial(input_kernel, len(row_parts), block),
        [shaped((rows, width))],
        [tokens, gain, grad_out, handed, *row_parts],
        [place],
        [pltpu.VMEM((rows, width), jnp.float32)],
    )
    return (input_grad, query_grad, kv_grad)


def solution(mesh):
    placed = (
        P(("dp", "tensor"), None),
        P(),
        P("dp", "tensor"),
        P("dp", "tensor"),
        P("tensor", "dp"),
        P(("dp", "tensor"), None),
        P("dp", None),
    )
    return jax.shard_map(
        local,
        mesh=mesh,
        in_specs=placed,
        out_specs=(P(("dp", "tensor"), None), P("dp", "tensor"), P("dp", "tensor")),
        check_vma=False,
    )
```

```python
import functools
import math

import jax
import jax.numpy as jnp
from jax import lax
from jax.experimental import pallas as pl
from jax.experimental.pallas import tpu as pltpu
from jax.sharding import PartitionSpec as P

KVH = 4
HD = 128

epsilon = 1e-05
CONTRACT_LAST = (((1,), (1,)), ((), ()))
CONTRACT_FIRST = (((0,), (0,)), ((), ()))
WHOLE = pl.BlockSpec(memory_space=pltpu.VMEM)
SCALARS = pl.BlockSpec(memory_space=pltpu.SMEM)


def call(kernel, outs, operands, scalars=(), scratch=(), flops=0, megabytes=24):
    moved = sum(math.prod(a.shape) * a.dtype.itemsize for a in (*operands, *outs))
    return pl.pallas_call(
        kernel,
        out_shape=outs,
        in_specs=[SCALARS] * len(scalars) + [WHOLE] * len(operands),
        out_specs=[WHOLE] * len(outs),
        scratch_shapes=scratch,
        compiler_params=pltpu.CompilerParams(vmem_limit_bytes=megabytes * 2**20),
        cost_estimate=pl.CostEstimate(flops=flops, bytes_accessed=moved, transcendentals=0),
    )(*scalars, *operands)


def shaped(shape, dtype=jnp.bfloat16):
    return jax.ShapeDtypeStruct(shape, dtype)


def dot(left, right, contract=(((1,), (0,)), ((), ()))):
    return lax.dot_general(left, right, contract, preferred_element_type=jnp.float32)


def swap(value, axis, mask):
    pairs = [(source, source ^ mask) for source in range(lax.axis_size(axis))]
    return lax.ppermute(value, axis, pairs)


def tied(*values):
    return lax.optimization_barrier(values)


def everyone(value, axis, unit):
    size = lax.axis_size(axis) // unit
    return [value] + [swap(value, axis, unit * k) for k in range(1, size)]


def gather_chips(value):
    if lax.axis_size("dp") != 8:
        return everyone(value, "dp", 2), []
    half = value.shape[0] // 2
    near_x = swap(value, "dp", 2)
    near_y = swap(value, "dp", 4)
    near_x, near_y = tied(near_x, near_y)
    far_top = swap(near_x[:half], "dp", 4)
    far_bottom = swap(near_y[half:], "dp", 2)
    return [value, near_x, near_y], [far_top, far_bottom]


def along(value, pairs):
    return lax.ppermute(value, "tensor", pairs)


def gather_tensor(value):
    if lax.axis_size("tensor") != 4:
        return everyone(value, "tensor", 1)
    right_one = along(value, [(0, 1), (1, 2), (2, 3)])
    left_one = along(value, [(1, 0), (2, 1), (3, 2)])
    right_one, left_one = tied(right_one, left_one)
    right_two = along(right_one, [(1, 2), (2, 3)])
    left_two = along(left_one, [(1, 0), (2, 1)])
    right_two, left_two = tied(right_two, left_two)
    last = along(
        jnp.where(lax.axis_index("tensor") == 1, left_two, right_two), [(1, 0), (2, 3)]
    )
    return [value, right_one, left_one, right_two, left_two, last]


def pick(index, pieces, size, k, rows):
    if len(pieces) == size:
        return pieces[k][rows]
    own, right_one, left_one, right_two, left_two, last = [piece.at[rows] for piece in pieces]
    if k == 0:
        return own[...]
    if k == 1:
        return jnp.where(index % 2 == 1, right_one[...], left_one[...])
    if k == 2:
        return jnp.where(index >= 2, right_two[...], left_two[...])
    near = jnp.where(index == 1, left_one[...], right_one[...])
    return jnp.where(jnp.logical_or(index == 0, index == 3), last[...], near)


def inner_pair(value):
    return along(value, [(1, 2), (2, 1)])


def outer_pair(value):
    return along(value, [(3, 2), (0, 1)])


def scatter_chips(blocks):
    if len(blocks) != 4:
        return [blocks[0]] + [swap(blocks[k], "dp", 2 * k) for k in range(1, len(blocks))]
    half = blocks[0].shape[0] // 2
    far_top = swap(blocks[3][:half], "dp", 4)
    far_bottom = swap(blocks[3][half:], "dp", 2)
    near_x = swap(
        jnp.concatenate([blocks[1][:half] + far_top, blocks[1][half:]], axis=0), "dp", 2
    )
    near_y = swap(
        jnp.concatenate([blocks[2][:half], blocks[2][half:] + far_bottom], axis=0), "dp", 4
    )
    return [blocks[0], near_x, near_y]


def scatter_tensor(blocks):
    if len(blocks) != 4:
        return [blocks[0]] + [swap(blocks[k], "tensor", k) for k in range(1, len(blocks))]
    outer, inner = outer_pair(blocks[3]), inner_pair(blocks[3])
    outer, inner = tied(outer, inner)
    carried, adjacent = tied(blocks[2] + outer, blocks[1])
    two, one = swap(carried, "tensor", 2), swap(adjacent, "tensor", 1)
    return [blocks[0], one, inner, two]


def column_start(place, k, which, block):
    return pl.multiple_of(((place[0] ^ k) * 2 + which) * block, 128)


def prepare_kernel(block, place, grad_out, tokens, gain, grad_keep, normed_keep, send, normed):
    rows, core = tokens.shape[0], place[1]
    values = tokens[...].astype(jnp.float32)
    root_mean = jnp.sqrt(jnp.mean(values * values, axis=-1, keepdims=True) + epsilon)
    normed[...] = (values / root_mean * gain[...].astype(jnp.float32)).astype(jnp.bfloat16)
    for start, source, keep in ((0, grad_out, grad_keep), (rows, normed, normed_keep)):
        for k in range(keep.shape[1] // block):
            columns = slice(k * block, (k + 1) * block)
            keep[:, columns] = source[:, pl.ds(column_start(place, k, core, block), block)]
            send[start : start + rows, columns] = source[
                :, pl.ds(column_start(place, k, 1 - core, block), block)
            ]


def merge_kernel(out_weight, query_weight, kv_weight, merged):
    block, start = merged.shape[0], 0
    for chunk in range(out_weight.shape[0] // block):
        merged[:, start : start + block] = out_weight[chunk * block : (chunk + 1) * block]
        start += block
    for weight in (query_weight, kv_weight):
        merged[:, start : start + weight.shape[1]] = weight[...]
        start += weight.shape[1]


def products(grads, normed, weights, first, out_width, block, columns):
    chunks = out_width // block
    size = weights[0].shape[0]
    if columns < out_width:
        chunk = columns // block
        for row in range(0, block, min(size, 256)):
            total = None
            if size == block:
                for k, weight in enumerate(weights):
                    right = weight[row : row + min(size, 256), chunk * block : (chunk + 1) * block]
                    left = grads[:, first + k * block : first + (k + 1) * block]
                    term = dot(left, right, CONTRACT_LAST)
                    total = term if total is None else total + term
            else:
                right = weights[row // size][:, chunk * block : (chunk + 1) * block]
                total = dot(grads[:, first : first + block], right, CONTRACT_LAST)
            yield slice(columns + row, columns + row + min(size, 256)), total
    else:
        width = min(256, weights[0].shape[1] - columns)
        total = None
        for k, weight in enumerate(weights):
            left = normed[:, first + k * size : first + (k + 1) * size]
            term = dot(left, weight[:, columns : columns + width])
            total = term if total is None else total + term
        yield slice(columns, columns + width), total


def column_steps(out_width, width, block):
    return [*range(0, out_width, block), *range(out_width, width, 256)]


def early_kernel(pieces, weights, size, out_width, place, *refs):
    row_refs, weight_refs = refs[:pieces], refs[pieces : pieces + weights]
    total, grads, normed = refs[pieces + weights :]
    rows = row_refs[0].shape[0] // 2
    block = weight_refs[0].shape[0]
    halves = row_refs[: pieces // 2], row_refs[pieces // 2 :]
    for pair, gathered in zip((grads, normed), halves):
        for core in range(2):
            for k in range(size):
                target = (core * size + k) * rows
                pair[target : target + rows] = pick(
                    place[2], gathered, size, k, slice(core * rows, (core + 1) * rows)
                )
    for columns in column_steps(out_width, total.shape[1], block):
        for place_out, value in products(grads, normed, weight_refs, 0, out_width, block, columns):
            total[:, place_out] = value


def late_kernel(first, out_width, block, total, grads, normed, *refs):
    weight_refs, (keep, send) = refs[:-2], refs[-2:]
    length = keep.shape[0]
    if not weight_refs:
        keep[...] = total[:length]
        send[...] = total[length:].astype(jnp.bfloat16)
    for columns in column_steps(out_width, keep.shape[1], block) if weight_refs else []:
        for place_out, value in products(
            grads, normed, weight_refs, first, out_width, block, columns
        ):
            keep[:, place_out] = total[:length, place_out] + value[:length]
            send[:, place_out] = (total[length:, place_out] + value[length:]).astype(jnp.bfloat16)


def project(place, pieces, early, late, size, out_width):
    rows = pieces[0].shape[0] // 2 * size
    half = pieces[0].shape[1]
    block, width = early[0].shape
    first = len(early) * block
    total, grads, normed = call(
        functools.partial(early_kernel, len(pieces), len(early), size, out_width),
        [shaped((2 * rows, width), jnp.float32)] + [shaped((2 * rows, half))] * 2,
        [*pieces, *early],
        [place],
        flops=4 * rows * first * width,
        megabytes=24,
    )
    own, sent = call(
        functools.partial(late_kernel, first, out_width, block),
        [shaped((rows, width), jnp.float32), shaped((rows, width))],
        [total, grads, normed, *late],
        flops=4 * rows * (half - first) * width,
        megabytes=24,
    )
    return own, sent, normed


def attention_kernel(rows, heads, place, lengths, own, sent, grads, partial):
    length = own.shape[0]
    width = heads * HD
    scale = 1 / math.sqrt(HD)
    tensor_index = place[2]

    def positions_of(dimension):
        order = lax.broadcasted_iota(jnp.int32, (length, length), dimension)
        return ((order // rows) ^ tensor_index) * rows + order % rows

    def labels_of(positions):
        labels, end = jnp.zeros((length, length), jnp.int32), 0
        for document in range(lengths.shape[1]):
            end = end + lengths[0, document]
            labels = labels + (end <= positions).astype(jnp.int32)
        return labels

    key_positions, query_positions = positions_of(0), positions_of(1)
    allowed = jnp.logical_and(
        labels_of(key_positions) == labels_of(query_positions), key_positions <= query_positions
    )

    def joined(first, second, columns):
        return (first[:, columns] + second[:, columns].astype(jnp.float32)).astype(jnp.bfloat16)

    keys = joined(own, sent, slice(2 * width, 2 * width + HD))
    values = joined(own, sent, slice(2 * width + HD, 2 * width + 2 * HD))
    key_total = value_total = None
    for head in range(heads):
        columns = slice(head * HD, (head + 1) * HD)
        out_grad = joined(own, sent, columns)
        queries = joined(own, sent, slice(width + head * HD, width + (head + 1) * HD))
        scores = jnp.where(allowed, dot(keys, queries, CONTRACT_LAST) * scale, -1e30)
        expo = jnp.exp(scores - jnp.max(scores, axis=0, keepdims=True))
        probs = expo * (1 / jnp.sum(expo, axis=0, keepdims=True))
        prob_grad = dot(values, out_grad, CONTRACT_LAST)
        inner = jnp.sum(probs * prob_grad, axis=0, keepdims=True)
        score_grad = (probs * (prob_grad - inner) * scale).astype(jnp.bfloat16)
        grads[:, columns] = dot(score_grad, keys, CONTRACT_FIRST).astype(jnp.bfloat16)
        key_term = dot(score_grad, queries)
        value_term = dot(probs.astype(jnp.bfloat16), out_grad)
        key_total = key_term if head == 0 else key_total + key_term
        value_total = value_term if head == 0 else value_total + value_term
    if partial is None:
        grads[:, width : width + HD] = key_total.astype(jnp.bfloat16)
        grads[:, width + HD :] = value_total.astype(jnp.bfloat16)
    else:
        partial[:, :HD] = key_total
        partial[:, HD:] = value_total


def attention(place, lengths, own, sent, rows, width, split):
    length = own.shape[0]
    outs = [shaped((length, width if split else width + 2 * HD))]
    if split:
        outs.append(shaped((length, 2 * HD), jnp.float32))

    def kernel(*refs):
        attention_kernel(rows, width // HD, *(refs if split else (*refs, None)))

    return call(
        kernel,
        outs,
        [own, sent],
        [place, lengths],
        flops=10 * length * length * width,
    )


def weight_kernel(first, block, pair, own, other, *outs):
    length = own.shape[0]
    tile = min(block, 256)
    for number, out in enumerate(outs):
        for part in range(block // tile):
            start = (first + number) * block + part * tile
            out[part * tile : (part + 1) * tile] = (
                dot(pair[:length, start : start + tile], own[...], CONTRACT_FIRST)
                + dot(pair[length:, start : start + tile], other[...], CONTRACT_FIRST)
            ).astype(jnp.bfloat16)


def weight_terms(pair, own, other, first, count, block):
    return call(
        functools.partial(weight_kernel, first, block),
        [shaped((block, own.shape[1]))] * count,
        [pair, own, other],
        flops=2 * pair.shape[0] * block * count * own.shape[1],
    )


def row_kernel(weights, offset_columns, own, other, *refs):
    weight_refs, outs = refs[:weights], refs[weights:]
    length = own.shape[0]
    rows = length // len(outs)
    start = 0
    for weight in weight_refs:
        tile = min(weight.shape[0], 256)
        for part in range(weight.shape[0] // tile):
            right = weight[part * tile : (part + 1) * tile, offset_columns:]
            for offset, left in ((0, own), (rows, other)):
                term = dot(left[...], right, CONTRACT_LAST).astype(jnp.bfloat16)
                for k, out in enumerate(outs):
                    out[offset : offset + rows, start : start + tile] = term[
                        k * rows : (k + 1) * rows
                    ]
            start += tile


def row_terms(own, other, weights, size, out_width):
    length, width = own.shape
    half = sum(weight.shape[0] for weight in weights)
    return call(
        functools.partial(row_kernel, len(weights), out_width),
        [shaped((2 * length // size, half))] * size,
        [own, other, *weights],
        flops=4 * length * width * half,
    )


def finish_kernel(count, share, *refs):
    total = refs[0][...].astype(jnp.float32)
    for part in refs[1:count]:
        total = total + part[...].astype(jnp.float32)
    total = total * share
    query_out, kv_out = refs[count:]
    width = query_out.shape[1]
    query_out[...] = total[:, :width]
    kv_out[...] = total[:, width:]


def finish(parts, query_width, share):
    block, width = parts[0].shape
    step = min(block, 128)

    def spec(columns):
        return pl.BlockSpec((step, columns), lambda i: (i, 0))

    return pl.pallas_call(
        functools.partial(finish_kernel, len(parts), share),
        grid=(block // step,),
        out_shape=[
            shaped((block, query_width), jnp.float32),
            shaped((block, width - query_width), jnp.float32),
        ],
        in_specs=[spec(width)] * len(parts),
        out_specs=[spec(query_width), spec(width - query_width)],
        compiler_params=pltpu.CompilerParams(vmem_limit_bytes=32 * 2**20),
        cost_estimate=pl.CostEstimate(
            flops=0, bytes_accessed=(2 * len(parts) + 4) * block * width, transcendentals=0
        ),
    )(*parts)


def input_kernel(count, block, place, tokens, gain, grad_out, handed, *refs):
    parts, out, gathered = refs[:count], refs[count], refs[count + 1]
    rows = tokens.shape[0]
    core = place[1]
    total = parts[0][:rows].astype(jnp.float32)
    for part in parts[1:]:
        total = total + part[:rows].astype(jnp.float32)
    for k in range(total.shape[1] // block):
        columns = slice(k * block, (k + 1) * block)
        gathered[:, pl.ds(column_start(place, k, core, block), block)] = total[:, columns]
        gathered[:, pl.ds(column_start(place, k, 1 - core, block), block)] = handed[
            :, columns
        ].astype(jnp.float32)
    values = tokens[...].astype(jnp.float32)
    root_mean = jnp.sqrt(jnp.mean(values * values, axis=-1, keepdims=True) + epsilon)
    unit = values / root_mean
    scaled = gathered[...] * gain[...].astype(jnp.float32)
    correction = unit * jnp.mean(scaled * unit, axis=-1, keepdims=True)
    out[...] = (grad_out[...].astype(jnp.float32) + (scaled - correction) / root_mean).astype(
        jnp.bfloat16
    )


def local(tokens, norm_gain, query_weight, kv_weight, out_weight, grad_out, doc_lengths):
    tensor_size = lax.axis_size("tensor")
    data_size = lax.axis_size("dp")
    tensor_index = lax.axis_index("tensor")
    data_index = lax.axis_index("dp")
    chips = data_size // 2
    place = jnp.stack([data_index >> 1, data_index & 1, tensor_index]).astype(jnp.int32)
    sharers = tensor_size // KVH
    levels = sharers.bit_length() - 1
    rows, width = tokens.shape
    block = width // data_size
    query_width = query_weight.shape[1]
    gain = norm_gain.reshape(1, width)

    grad_keep, normed_keep, send = call(
        functools.partial(prepare_kernel, block),
        [shaped((rows, width // 2))] * 2 + [shaped((2 * rows, width // 2))],
        [grad_out, tokens, gain],
        [place],
        [pltpu.VMEM((rows, width), jnp.bfloat16)],
    )
    out_width = out_weight.shape[0]
    send, out_weight, query_weight, kv_weight = tied(send, out_weight, query_weight, kv_weight)
    sent = swap(send, "dp", 1)
    row_pieces = gather_tensor(jnp.concatenate([grad_keep, sent[:rows]], axis=0))
    row_pieces += gather_tensor(jnp.concatenate([normed_keep, sent[rows:]], axis=0))
    (merged,) = call(
        merge_kernel,
        [shaped((block, out_width + query_width + kv_weight.shape[1]))],
        [out_weight, query_weight, kv_weight],
    )
    early, late = gather_chips(merged)
    own, sent, normed = project(place, row_pieces, early, late, tensor_size, out_width)
    sent = swap(sent, "dp", 1)
    if levels:
        joined = (own + sent.astype(jnp.float32)).astype(jnp.bfloat16)
        keyvals = joined[:, out_width + query_width :]
        for bit_index in range(levels):
            partner = swap(keyvals, "tensor", 2**bit_index)
            upper = tensor_index >> bit_index & 1 == 1
            keyvals = jnp.concatenate(
                [jnp.where(upper, partner, keyvals), jnp.where(upper, keyvals, partner)], axis=1
            )
        own = jnp.concatenate(
            [joined[:, : out_width + query_width], keyvals], axis=1
        ).astype(jnp.float32)
        sent = jnp.zeros(own.shape, jnp.bfloat16)
    combined, *partial = attention(place, doc_lengths, own, sent, rows, query_width, levels > 0)
    if levels:
        kv_partial = partial[0]
        for bit_index in reversed(range(levels)):
            half_cols = kv_partial.shape[1] // 2
            upper = tensor_index >> bit_index & 1 == 1
            lower_cols = kv_partial[:, :half_cols]
            higher_cols = kv_partial[:, half_cols:]
            kept = jnp.where(upper, higher_cols, lower_cols)
            handed = jnp.where(upper, lower_cols, higher_cols)
            kv_partial = kept + swap(handed.astype(jnp.bfloat16), "tensor", 2**bit_index).astype(
                jnp.float32
            )
        combined = jnp.concatenate([combined, kv_partial.astype(jnp.bfloat16)], axis=1)
    other = swap(combined, "dp", 1)

    far = weight_terms(normed, combined, other, chips - 1, 1, block)
    near = weight_terms(normed, combined, other, 0, chips - 1, block)
    row_parts = scatter_tensor(row_terms(combined, other, early + late, tensor_size, out_width))
    weight_parts = scatter_chips([*near, *far])
    handed = sum(part[rows:].astype(jnp.float32) for part in row_parts).astype(jnp.bfloat16)
    handed = swap(handed, "dp", 1)
    query_grad, kv_grad = finish(weight_parts, query_width, 1 / data_size)
    handed, query_grad, kv_grad = tied(handed, query_grad, kv_grad)
    (input_grad,) = call(
        functools.partial(input_kernel, len(row_parts), block),
        [shaped((rows, width))],
        [tokens, gain, grad_out, handed, *row_parts],
        [place],
        [pltpu.VMEM((rows, width), jnp.float32)],
    )
    return (input_grad, query_grad, kv_grad)


def solution(mesh):
    placed = (
        P(("dp", "tensor"), None),
        P(),
        P("dp", "tensor"),
        P("dp", "tensor"),
        P("tensor", "dp"),
        P(("dp", "tensor"), None),
        P("dp", None),
    )
    return jax.shard_map(
        local,
        mesh=mesh,
        in_specs=placed,
        out_specs=(P(("dp", "tensor"), None), P("dp", "tensor"), P("dp", "tensor")),
        check_vma=False,
    )
```

```python
import functools
import math

import jax
import jax.numpy as jnp
from jax import lax
from jax.experimental import pallas as pl
from jax.experimental.pallas import tpu as pltpu
from jax.sharding import PartitionSpec as P

KVH = 4
HD = 128

epsilon = 1e-05
CONTRACT_LAST = (((1,), (1,)), ((), ()))
CONTRACT_FIRST = (((0,), (0,)), ((), ()))
WHOLE = pl.BlockSpec(memory_space=pltpu.VMEM)
SCALARS = pl.BlockSpec(memory_space=pltpu.SMEM)


def call(kernel, outs, operands, scalars=(), scratch=(), flops=0, megabytes=24):
    moved = sum(math.prod(a.shape) * a.dtype.itemsize for a in (*operands, *outs))
    return pl.pallas_call(
        kernel,
        out_shape=outs,
        in_specs=[SCALARS] * len(scalars) + [WHOLE] * len(operands),
        out_specs=[WHOLE] * len(outs),
        scratch_shapes=scratch,
        compiler_params=pltpu.CompilerParams(vmem_limit_bytes=megabytes * 2**20),
        cost_estimate=pl.CostEstimate(flops=flops, bytes_accessed=moved, transcendentals=0),
    )(*scalars, *operands)


def shaped(shape, dtype=jnp.bfloat16):
    return jax.ShapeDtypeStruct(shape, dtype)


def dot(left, right, contract=(((1,), (0,)), ((), ()))):
    return lax.dot_general(left, right, contract, preferred_element_type=jnp.float32)


def swap(value, axis, mask):
    pairs = [(source, source ^ mask) for source in range(lax.axis_size(axis))]
    return lax.ppermute(value, axis, pairs)


def tied(*values):
    return lax.optimization_barrier(values)


def everyone(value, axis, unit):
    size = lax.axis_size(axis) // unit
    return [value] + [swap(value, axis, unit * k) for k in range(1, size)]


def gather_near(value):
    if lax.axis_size("dp") != 8:
        return everyone(value, "dp", 2), []
    half = value.shape[0] // 2
    near_x = swap(value, "dp", 2)
    near_y = swap(value, "dp", 4)
    near_x, near_y = tied(near_x, near_y)
    return [value, near_x, near_y], [near_x[:half], near_y[half:]]


def gather_far(parts):
    return [swap(part, "dp", mask) for part, mask in zip(parts, (4, 2))]


def along(value, pairs):
    return lax.ppermute(value, "tensor", pairs)


def gather_tensor(value, after=()):
    if lax.axis_size("tensor") != 4:
        return everyone(value, "tensor", 1)
    right_one = along(value, [(0, 1), (1, 2), (2, 3)])
    left_one = along(value, [(1, 0), (2, 1), (3, 2)])
    right_two = along(right_one, [(1, 2), (2, 3)])
    left_two = along(left_one, [(1, 0), (2, 1)])
    right_two, left_two, *_ = tied(right_two, left_two, *after)
    last = along(
        jnp.where(lax.axis_index("tensor") == 1, left_two, right_two), [(1, 0), (2, 3)]
    )
    return [value, right_one, left_one, right_two, left_two, last]


def pick(index, pieces, size, k, rows):
    if size != 4:
        return pieces[k][rows]
    own, right_one, left_one, right_two, left_two = [piece.at[rows] for piece in pieces[:5]]
    if k == 0:
        return own[...]
    if k == 1:
        return jnp.where(index % 2 == 1, right_one[...], left_one[...])
    return jnp.where(index >= 2, right_two[...], left_two[...])


def last_slot(index, pieces, rows):
    if len(pieces) == 1:
        return pieces[0][rows]
    right_one, left_one, last = [piece[rows] for piece in pieces]
    near = jnp.where(index == 1, left_one, right_one)
    return jnp.where(jnp.logical_or(index == 0, index == 3), last, near)


def inner_pair(value):
    return along(value, [(1, 2), (2, 1)])


def outer_pair(value):
    return along(value, [(3, 2), (0, 1)])


def scatter_chips(blocks):
    if len(blocks) != 4:
        return [blocks[0]] + [swap(blocks[k], "dp", 2 * k) for k in range(1, len(blocks))]
    half = blocks[0].shape[0] // 2
    far_top = swap(blocks[3][:half], "dp", 4)
    far_bottom = swap(blocks[3][half:], "dp", 2)
    near_x = swap(
        jnp.concatenate([blocks[1][:half] + far_top, blocks[1][half:]], axis=0), "dp", 2
    )
    near_y = swap(
        jnp.concatenate([blocks[2][:half], blocks[2][half:] + far_bottom], axis=0), "dp", 4
    )
    return [blocks[0], near_x, near_y]


def scatter_tensor(blocks):
    if len(blocks) != 4:
        return [blocks[0]] + [swap(blocks[k], "tensor", k) for k in range(1, len(blocks))]
    outer, inner = outer_pair(blocks[3]), inner_pair(blocks[3])
    outer, inner = tied(outer, inner)
    carried, adjacent = tied(blocks[2] + outer, blocks[1])
    two, one = swap(carried, "tensor", 2), swap(adjacent, "tensor", 1)
    return [blocks[0], one, inner, two]


def column_start(place, k, which, block):
    return pl.multiple_of(((place[0] ^ k) * 2 + which) * block, 128)


def prepare_kernel(block, place, grad_out, tokens, gain, grad_keep, normed_keep, send, normed):
    rows, core = tokens.shape[0], place[1]
    values = tokens[...].astype(jnp.float32)
    root_mean = jnp.sqrt(jnp.mean(values * values, axis=-1, keepdims=True) + epsilon)
    normed[...] = (values / root_mean * gain[...].astype(jnp.float32)).astype(jnp.bfloat16)
    for start, source, keep in ((0, grad_out, grad_keep), (rows, normed, normed_keep)):
        for k in range(keep.shape[1] // block):
            columns = slice(k * block, (k + 1) * block)
            keep[:, columns] = source[:, pl.ds(column_start(place, k, core, block), block)]
            send[start : start + rows, columns] = source[
                :, pl.ds(column_start(place, k, 1 - core, block), block)
            ]


def merge_kernel(out_weight, query_weight, kv_weight, merged):
    block, start = merged.shape[0], 0
    for chunk in range(out_weight.shape[0] // block):
        merged[:, start : start + block] = out_weight[chunk * block : (chunk + 1) * block]
        start += block
    for weight in (query_weight, kv_weight):
        merged[:, start : start + weight.shape[1]] = weight[...]
        start += weight.shape[1]


def products(grads, normed, weights, first, out_width, block, columns):
    chunks = out_width // block
    size = weights[0].shape[0]
    if columns < out_width:
        chunk = columns // block
        for row in range(0, block, min(size, 256)):
            total = None
            if size == block:
                for k, weight in enumerate(weights):
                    right = weight[row : row + min(size, 256), chunk * block : (chunk + 1) * block]
                    left = grads[:, first + k * block : first + (k + 1) * block]
                    term = dot(left, right, CONTRACT_LAST)
                    total = term if total is None else total + term
            else:
                right = weights[row // size][:, chunk * block : (chunk + 1) * block]
                total = dot(grads[:, first : first + block], right, CONTRACT_LAST)
            yield slice(columns + row, columns + row + min(size, 256)), total
    else:
        width = min(256, weights[0].shape[1] - columns)
        total = None
        for k, weight in enumerate(weights):
            left = normed[:, first + k * size : first + (k + 1) * size]
            term = dot(left, weight[:, columns : columns + width])
            total = term if total is None else total + term
        yield slice(columns, columns + width), total


def column_steps(out_width, width, block):
    return [*range(0, out_width, block), *range(out_width, width, 256)]


def early_kernel(pieces, weights, size, out_width, place, *refs):
    row_refs, weight_refs = refs[:pieces], refs[pieces : pieces + weights]
    total, grads, normed = refs[pieces + weights :]
    rows = row_refs[0].shape[0] // 2
    block = weight_refs[0].shape[0]
    halves = row_refs[: pieces // 2], row_refs[pieces // 2 :]
    for pair, gathered in zip((grads, normed), halves):
        for core in range(2):
            for k in range(size - 1):
                target = (core * (size - 1) + k) * rows
                pair[target : target + rows] = pick(
                    place[2], gathered, size, k, slice(core * rows, (core + 1) * rows)
                )
    for columns in column_steps(out_width, total.shape[1], block):
        for place_out, value in products(grads, normed, weight_refs, 0, out_width, block, columns):
            total[:, place_out] = value


def late_kernel(pieces, early, late, size, out_width, place, *refs):
    total, grads, normed = refs[:3]
    row_refs, refs = refs[3 : 3 + pieces], refs[3 + pieces :]
    early_refs, late_refs, refs = refs[:early], refs[early : early + late], refs[early + late :]
    keep, send, pair, last_grads, last_normed = refs
    rows = row_refs[0].shape[0] // 2
    block = early_refs[0].shape[0]
    first, most, length = early * block, (size - 1) * rows, size * rows
    halves = row_refs[: pieces // 2], row_refs[pieces // 2 :]
    for target, gathered in zip((last_grads, last_normed), halves):
        for core in range(2):
            some = slice(core * rows, (core + 1) * rows)
            target[some] = last_slot(place[2], gathered, some)
    for core in range(2):
        pair[core * length : core * length + most] = normed[core * most : (core + 1) * most]
        pair[core * length + most : (core + 1) * length] = last_normed[
            core * rows : (core + 1) * rows
        ]
    for columns in column_steps(out_width, keep.shape[1], block):
        arguments = out_width, block, columns
        ends = products(last_grads, last_normed, early_refs, 0, *arguments)
        if late:
            far = products(grads, normed, late_refs, first, *arguments)
            far_ends = products(last_grads, last_normed, late_refs, first, *arguments)
        for place_out, end in ends:
            value = total[:, place_out]
            if late:
                value = value + next(far)[1]
                end = end + next(far_ends)[1]
            keep[:most, place_out] = value[:most]
            keep[most:, place_out] = end[:rows]
            send[:most, place_out] = value[most:].astype(jnp.bfloat16)
            send[most:, place_out] = end[rows:].astype(jnp.bfloat16)


def project(place, grad_pieces, normed_pieces, early, late, size, out_width):
    pair_rows, half = grad_pieces[0].shape
    rows = pair_rows // 2 * size
    block, width = early[0].shape
    most = pair_rows * (size - 1)
    pieces = [*grad_pieces[:-1], *normed_pieces[:-1]]
    total, grads, normed = call(
        functools.partial(early_kernel, len(pieces), len(early), size, out_width),
        [shaped((most, width), jnp.float32)] + [shaped((most, half))] * 2,
        [*pieces, *early],
        [place],
        flops=2 * most * len(early) * block * width,
    )
    needed = (1, 2, 5) if size == 4 else (-1,)
    pieces = [gathered[k] for gathered in (grad_pieces, normed_pieces) for k in needed]
    own, sent, normed = call(
        functools.partial(late_kernel, len(pieces), len(early), len(late), size, out_width),
        [
            shaped((rows, width), jnp.float32),
            shaped((rows, width)),
            shaped((2 * rows, half)),
        ],
        [total, grads, normed, *pieces, *early, *late],
        [place],
        [pltpu.VMEM((pair_rows, half), jnp.bfloat16)] * 2,
        flops=2 * (pair_rows * half + most * block) * width,
    )
    return own, sent, normed


def attention_kernel(rows, heads, place, lengths, own, sent, grads, partial):
    length = own.shape[0]
    width = heads * HD
    scale = 1 / math.sqrt(HD)
    tensor_index = place[2]

    def positions_of(dimension):
        order = lax.broadcasted_iota(jnp.int32, (length, length), dimension)
        return ((order // rows) ^ tensor_index) * rows + order % rows

    def labels_of(positions):
        labels, end = jnp.zeros((length, length), jnp.int32), 0
        for document in range(lengths.shape[1]):
            end = end + lengths[0, document]
            labels = labels + (end <= positions).astype(jnp.int32)
        return labels

    key_positions, query_positions = positions_of(0), positions_of(1)
    allowed = jnp.logical_and(
        labels_of(key_positions) == labels_of(query_positions), key_positions <= query_positions
    )

    def joined(first, second, columns):
        return (first[:, columns] + second[:, columns].astype(jnp.float32)).astype(jnp.bfloat16)

    keys = joined(own, sent, slice(2 * width, 2 * width + HD))
    values = joined(own, sent, slice(2 * width + HD, 2 * width + 2 * HD))
    key_total = value_total = None
    for head in range(heads):
        columns = slice(head * HD, (head + 1) * HD)
        out_grad = joined(own, sent, columns)
        queries = joined(own, sent, slice(width + head * HD, width + (head + 1) * HD))
        scores = jnp.where(allowed, dot(keys, queries, CONTRACT_LAST) * scale, -1e30)
        expo = jnp.exp(scores - jnp.max(scores, axis=0, keepdims=True))
        probs = expo * (1 / jnp.sum(expo, axis=0, keepdims=True))
        prob_grad = dot(values, out_grad, CONTRACT_LAST)
        inner = jnp.sum(probs * prob_grad, axis=0, keepdims=True)
        score_grad = (probs * (prob_grad - inner) * scale).astype(jnp.bfloat16)
        grads[:, columns] = dot(score_grad, keys, CONTRACT_FIRST).astype(jnp.bfloat16)
        key_term = dot(score_grad, queries)
        value_term = dot(probs.astype(jnp.bfloat16), out_grad)
        key_total = key_term if head == 0 else key_total + key_term
        value_total = value_term if head == 0 else value_total + value_term
    if partial is None:
        grads[:, width : width + HD] = key_total.astype(jnp.bfloat16)
        grads[:, width + HD :] = value_total.astype(jnp.bfloat16)
    else:
        partial[:, :HD] = key_total
        partial[:, HD:] = value_total


def attention(place, lengths, own, sent, rows, width, split):
    length = own.shape[0]
    outs = [shaped((length, width if split else width + 2 * HD))]
    if split:
        outs.append(shaped((length, 2 * HD), jnp.float32))

    def kernel(*refs):
        attention_kernel(rows, width // HD, *(refs if split else (*refs, None)))

    return call(
        kernel,
        outs,
        [own, sent],
        [place, lengths],
        flops=10 * length * length * width,
    )


def weight_kernel(first, block, pair, own, other, *outs):
    length = own.shape[0]
    tile = min(block, 256)
    for number, out in enumerate(outs):
        for part in range(block // tile):
            start = (first + number) * block + part * tile
            out[part * tile : (part + 1) * tile] = (
                dot(pair[:length, start : start + tile], own[...], CONTRACT_FIRST)
                + dot(pair[length:, start : start + tile], other[...], CONTRACT_FIRST)
            ).astype(jnp.bfloat16)


def weight_terms(pair, own, other, first, count, block):
    return call(
        functools.partial(weight_kernel, first, block),
        [shaped((block, own.shape[1]))] * count,
        [pair, own, other],
        flops=2 * pair.shape[0] * block * count * own.shape[1],
    )


def row_kernel(weights, offset_columns, blocks, own, other, *refs):
    weight_refs, outs, left = refs[:weights], refs[weights:-1], refs[-1]
    rows = outs[0].shape[0] // 2
    for number, k in enumerate(blocks):
        for start, source in ((2 * number, own), (2 * number + 1, other)):
            left[start * rows : (start + 1) * rows] = source[k * rows : (k + 1) * rows]
    start = 0
    for weight in weight_refs:
        tile = min(weight.shape[0], 256)
        for part in range(weight.shape[0] // tile):
            right = weight[part * tile : (part + 1) * tile, offset_columns:]
            term = dot(left[...], right, CONTRACT_LAST).astype(jnp.bfloat16)
            for number, out in enumerate(outs):
                out[:, start : start + tile] = term[2 * number * rows : 2 * (number + 1) * rows]
            start += tile


def row_terms(own, other, weights, size, out_width, blocks):
    length, width = own.shape
    half = sum(weight.shape[0] for weight in weights)
    pair_rows = 2 * length // size
    return call(
        functools.partial(row_kernel, len(weights), out_width, blocks),
        [shaped((pair_rows, half))] * len(blocks),
        [own, other, *weights],
        (),
        [pltpu.VMEM((pair_rows * len(blocks), width), jnp.bfloat16)],
        flops=2 * pair_rows * len(blocks) * width * half,
    )


def finish_kernel(count, share, *refs):
    total = refs[0][...].astype(jnp.float32)
    for part in refs[1:count]:
        total = total + part[...].astype(jnp.float32)
    total = total * share
    query_out, kv_out = refs[count:]
    width = query_out.shape[1]
    query_out[...] = total[:, :width]
    kv_out[...] = total[:, width:]


def finish(parts, query_width, share):
    block, width = parts[0].shape
    step = min(block, 128)

    def spec(columns):
        return pl.BlockSpec((step, columns), lambda i: (i, 0))

    return pl.pallas_call(
        functools.partial(finish_kernel, len(parts), share),
        grid=(block // step,),
        out_shape=[
            shaped((block, query_width), jnp.float32),
            shaped((block, width - query_width), jnp.float32),
        ],
        in_specs=[spec(width)] * len(parts),
        out_specs=[spec(query_width), spec(width - query_width)],
        compiler_params=pltpu.CompilerParams(vmem_limit_bytes=32 * 2**20),
        cost_estimate=pl.CostEstimate(
            flops=0, bytes_accessed=(2 * len(parts) + 4) * block * width, transcendentals=0
        ),
    )(*parts)


def input_kernel(count, block, place, tokens, gain, grad_out, handed, *refs):
    parts, out, gathered = refs[:count], refs[count], refs[count + 1]
    rows = tokens.shape[0]
    core = place[1]
    total = parts[0][:rows].astype(jnp.float32)
    for part in parts[1:]:
        total = total + part[:rows].astype(jnp.float32)
    for k in range(total.shape[1] // block):
        columns = slice(k * block, (k + 1) * block)
        gathered[:, pl.ds(column_start(place, k, core, block), block)] = total[:, columns]
        gathered[:, pl.ds(column_start(place, k, 1 - core, block), block)] = handed[
            :, columns
        ].astype(jnp.float32)
    values = tokens[...].astype(jnp.float32)
    root_mean = jnp.sqrt(jnp.mean(values * values, axis=-1, keepdims=True) + epsilon)
    unit = values / root_mean
    scaled = gathered[...] * gain[...].astype(jnp.float32)
    correction = unit * jnp.mean(scaled * unit, axis=-1, keepdims=True)
    out[...] = (grad_out[...].astype(jnp.float32) + (scaled - correction) / root_mean).astype(
        jnp.bfloat16
    )


def local(tokens, norm_gain, query_weight, kv_weight, out_weight, grad_out, doc_lengths):
    tensor_size = lax.axis_size("tensor")
    data_size = lax.axis_size("dp")
    tensor_index = lax.axis_index("tensor")
    data_index = lax.axis_index("dp")
    chips = data_size // 2
    place = jnp.stack([data_index >> 1, data_index & 1, tensor_index]).astype(jnp.int32)
    sharers = tensor_size // KVH
    levels = sharers.bit_length() - 1
    rows, width = tokens.shape
    block = width // data_size
    query_width = query_weight.shape[1]
    gain = norm_gain.reshape(1, width)

    grad_keep, normed_keep, send = call(
        functools.partial(prepare_kernel, block),
        [shaped((rows, width // 2))] * 2 + [shaped((2 * rows, width // 2))],
        [grad_out, tokens, gain],
        [place],
        [pltpu.VMEM((rows, width), jnp.bfloat16)],
    )
    out_width = out_weight.shape[0]
    send, out_weight, query_weight, kv_weight = tied(send, out_weight, query_weight, kv_weight)
    sent = swap(send, "dp", 1)
    normed_pieces = gather_tensor(jnp.concatenate([normed_keep, sent[rows:]], axis=0))
    (merged,) = call(
        merge_kernel,
        [shaped((block, out_width + query_width + kv_weight.shape[1]))],
        [out_weight, query_weight, kv_weight],
    )
    early, parts = gather_near(merged)
    late = gather_far(parts)
    grad_pieces = gather_tensor(jnp.concatenate([grad_keep, sent[:rows]], axis=0), parts)
    own, sent, normed = project(
        place, grad_pieces, normed_pieces, early, late, tensor_size, out_width
    )
    sent = swap(sent, "dp", 1)
    if levels:
        joined = (own + sent.astype(jnp.float32)).astype(jnp.bfloat16)
        keyvals = joined[:, out_width + query_width :]
        for bit_index in range(levels):
            partner = swap(keyvals, "tensor", 2**bit_index)
            upper = tensor_index >> bit_index & 1 == 1
            keyvals = jnp.concatenate(
                [jnp.where(upper, partner, keyvals), jnp.where(upper, keyvals, partner)], axis=1
            )
        own = jnp.concatenate(
            [joined[:, : out_width + query_width], keyvals], axis=1
        ).astype(jnp.float32)
        sent = jnp.zeros(own.shape, jnp.bfloat16)
    combined, *partial = attention(place, doc_lengths, own, sent, rows, query_width, levels > 0)
    if levels:
        kv_partial = partial[0]
        for bit_index in reversed(range(levels)):
            half_cols = kv_partial.shape[1] // 2
            upper = tensor_index >> bit_index & 1 == 1
            lower_cols = kv_partial[:, :half_cols]
            higher_cols = kv_partial[:, half_cols:]
            kept = jnp.where(upper, higher_cols, lower_cols)
            handed = jnp.where(upper, lower_cols, higher_cols)
            kv_partial = kept + swap(handed.astype(jnp.bfloat16), "tensor", 2**bit_index).astype(
                jnp.float32
            )
        combined = jnp.concatenate([combined, kv_partial.astype(jnp.bfloat16)], axis=1)
    other = swap(combined, "dp", 1)

    far = weight_terms(normed, combined, other, chips - 1, 1, block)
    near = weight_terms(normed, combined, other, 0, chips - 1, block)
    row_blocks = []
    for blocks in ([tensor_size - 1], list(range(tensor_size - 1))):
        some = row_terms(combined, other, early + late, tensor_size, out_width, blocks)
        row_blocks = [*some, *row_blocks]
    row_parts = scatter_tensor(row_blocks)
    weight_parts = scatter_chips([*near, *far])
    handed = sum(part[rows:].astype(jnp.float32) for part in row_parts).astype(jnp.bfloat16)
    handed = swap(handed, "dp", 1)
    query_grad, kv_grad = finish(weight_parts, query_width, 1 / data_size)
    handed, query_grad, kv_grad = tied(handed, query_grad, kv_grad)
    (input_grad,) = call(
        functools.partial(input_kernel, len(row_parts), block),
        [shaped((rows, width))],
        [tokens, gain, grad_out, handed, *row_parts],
        [place],
        [pltpu.VMEM((rows, width), jnp.float32)],
    )
    return (input_grad, query_grad, kv_grad)


def solution(mesh):
    placed = (
        P(("dp", "tensor"), None),
        P(),
        P("dp", "tensor"),
        P("dp", "tensor"),
        P("tensor", "dp"),
        P(("dp", "tensor"), None),
        P("dp", None),
    )
    return jax.shard_map(
        local,
        mesh=mesh,
        in_specs=placed,
        out_specs=(P(("dp", "tensor"), None), P("dp", "tensor"), P("dp", "tensor")),
        check_vma=False,
    )
```

```python
import functools
import math

import jax
import jax.numpy as jnp
from jax import lax
from jax.experimental import pallas as pl
from jax.experimental.pallas import tpu as pltpu
from jax.sharding import PartitionSpec as P

KVH = 4
HD = 128

epsilon = 1e-05
CONTRACT_LAST = (((1,), (1,)), ((), ()))
CONTRACT_FIRST = (((0,), (0,)), ((), ()))
WHOLE = pl.BlockSpec(memory_space=pltpu.VMEM)
SCALARS = pl.BlockSpec(memory_space=pltpu.SMEM)


def call(kernel, outs, operands, scalars=(), scratch=(), flops=0, megabytes=24):
    moved = sum(math.prod(a.shape) * a.dtype.itemsize for a in (*operands, *outs))
    return pl.pallas_call(
        kernel,
        out_shape=outs,
        in_specs=[SCALARS] * len(scalars) + [WHOLE] * len(operands),
        out_specs=[WHOLE] * len(outs),
        scratch_shapes=scratch,
        compiler_params=pltpu.CompilerParams(vmem_limit_bytes=megabytes * 2**20),
        cost_estimate=pl.CostEstimate(flops=flops, bytes_accessed=moved, transcendentals=0),
    )(*scalars, *operands)


def shaped(shape, dtype=jnp.bfloat16):
    return jax.ShapeDtypeStruct(shape, dtype)


def dot(left, right, contract=(((1,), (0,)), ((), ()))):
    return lax.dot_general(left, right, contract, preferred_element_type=jnp.float32)


def swap(value, axis, mask):
    pairs = [(source, source ^ mask) for source in range(lax.axis_size(axis))]
    return lax.ppermute(value, axis, pairs)


def tied(*values):
    return lax.optimization_barrier(values)


def everyone(value, axis, unit):
    size = lax.axis_size(axis) // unit
    return [value] + [swap(value, axis, unit * k) for k in range(1, size)]


def gather_chips(value):
    if lax.axis_size("dp") != 8:
        return everyone(value, "dp", 2), []
    half = value.shape[0] // 2
    near_x = swap(value, "dp", 2)
    near_y = swap(value, "dp", 4)
    near_x, near_y = tied(near_x, near_y)
    far_top = swap(near_x[:half], "dp", 4)
    far_bottom = swap(near_y[half:], "dp", 2)
    return [value, near_x, near_y], [far_top, far_bottom]


def along(value, pairs):
    return lax.ppermute(value, "tensor", pairs)


def gather_tensor(value):
    if lax.axis_size("tensor") != 4:
        return everyone(value, "tensor", 1)
    right_one = along(value, [(0, 1), (1, 2), (2, 3)])
    left_one = along(value, [(1, 0), (2, 1), (3, 2)])
    right_one, left_one = tied(right_one, left_one)
    right_two = along(right_one, [(1, 2), (2, 3)])
    left_two = along(left_one, [(1, 0), (2, 1)])
    right_two, left_two = tied(right_two, left_two)
    last = along(
        jnp.where(lax.axis_index("tensor") == 1, left_two, right_two), [(1, 0), (2, 3)]
    )
    return [value, right_one, left_one, right_two, left_two, last]


def pick(index, pieces, size, k, rows):
    if len(pieces) == size:
        return pieces[k][rows]
    own, right_one, left_one, right_two, left_two, last = [piece.at[rows] for piece in pieces]
    if k == 0:
        return own[...]
    if k == 1:
        return jnp.where(index % 2 == 1, right_one[...], left_one[...])
    if k == 2:
        return jnp.where(index >= 2, right_two[...], left_two[...])
    near = jnp.where(index == 1, left_one[...], right_one[...])
    return jnp.where(jnp.logical_or(index == 0, index == 3), last[...], near)


def inner_pair(value):
    return along(value, [(1, 2), (2, 1)])


def outer_pair(value):
    return along(value, [(3, 2), (0, 1)])


def scatter_chips(blocks):
    if len(blocks) != 4:
        return [blocks[0]] + [swap(blocks[k], "dp", 2 * k) for k in range(1, len(blocks))]
    half = blocks[0].shape[0] // 2
    far_top = swap(blocks[3][:half], "dp", 4)
    far_bottom = swap(blocks[3][half:], "dp", 2)
    near_x = swap(
        jnp.concatenate([blocks[1][:half] + far_top, blocks[1][half:]], axis=0), "dp", 2
    )
    near_y = swap(
        jnp.concatenate([blocks[2][:half], blocks[2][half:] + far_bottom], axis=0), "dp", 4
    )
    return [blocks[0], near_x, near_y]


def scatter_tensor(blocks):
    if len(blocks) != 4:
        return [blocks[0]] + [swap(blocks[k], "tensor", k) for k in range(1, len(blocks))]
    outer, inner = outer_pair(blocks[3]), inner_pair(blocks[3])
    outer, inner = tied(outer, inner)
    carried, adjacent = tied(blocks[2] + outer, blocks[1])
    two, one = swap(carried, "tensor", 2), swap(adjacent, "tensor", 1)
    return [blocks[0], one, inner, two]


def column_start(place, k, which, block):
    return pl.multiple_of(((place[0] ^ k) * 2 + which) * block, 128)


def prepare_kernel(
    block, place, gain, grad_far, tokens_far, grad_keep, normed_keep, send, normed, grad_out, tokens, arrived
):
    rows, core = tokens.shape[0], place[1]
    copies = [
        pltpu.make_async_copy(tokens_far, tokens, arrived.at[0]),
        pltpu.make_async_copy(grad_far, grad_out, arrived.at[1]),
    ]
    for copy in copies:
        copy.start()
    for copy in copies:
        copy.wait()
    values = tokens[...].astype(jnp.float32)
    root_mean = jnp.sqrt(jnp.mean(values * values, axis=-1, keepdims=True) + epsilon)
    normed[...] = (values / root_mean * gain[...].astype(jnp.float32)).astype(jnp.bfloat16)
    for start, source, keep in ((0, grad_out, grad_keep), (rows, normed, normed_keep)):
        for k in range(keep.shape[1] // block):
            columns = slice(k * block, (k + 1) * block)
            keep[:, columns] = source[:, pl.ds(column_start(place, k, core, block), block)]
            send[start : start + rows, columns] = source[
                :, pl.ds(column_start(place, k, 1 - core, block), block)
            ]


def merge_kernel(count, query_weight, kv_weight, out_weight, merged, arrived):
    block, start, parts = merged.shape[0], 0, [query_weight, kv_weight]
    parts += [out_weight.at[k * block : (k + 1) * block] for k in range(count)]
    copies = []
    for number, part in enumerate(parts):
        width = part.shape[1]
        target = merged.at[:, start : start + width]
        copies.append(pltpu.make_async_copy(part, target, arrived.at[number]))
        copies[-1].start()
        start += width
    for copy in copies:
        copy.wait()


def merge(query_weight, kv_weight, out_weight):
    block = query_weight.shape[0]
    count = out_weight.shape[0] // block
    width = query_weight.shape[1] + kv_weight.shape[1] + out_weight.shape[0]
    if kv_weight.shape[1] % 128:
        chunks = jnp.split(out_weight, count, axis=0)
        return jnp.concatenate([query_weight, kv_weight, *chunks], axis=1)
    return pl.pallas_call(
        functools.partial(merge_kernel, count),
        out_shape=shaped((block, width)),
        in_specs=[pl.BlockSpec(memory_space=pltpu.HBM)] * 3,
        out_specs=WHOLE,
        scratch_shapes=[pltpu.SemaphoreType.DMA((2 + count,))],
        compiler_params=pltpu.CompilerParams(vmem_limit_bytes=58 * 2**20),
        cost_estimate=pl.CostEstimate(flops=0, bytes_accessed=4 * block * width, transcendentals=0),
    )(query_weight, kv_weight, out_weight)


def products(grads, normed, weights, first, joint_width, block, columns):
    size = weights[0].shape[0]
    if columns < joint_width:
        width = min(256, joint_width - columns)
        total = None
        for k, weight in enumerate(weights):
            left = normed[:, first + k * size : first + (k + 1) * size]
            term = dot(left, weight[:, columns : columns + width])
            total = term if total is None else total + term
        yield slice(columns, columns + width), total
        return
    for row in range(0, block, min(size, 256)):
        place_out = slice(columns + row, columns + row + min(size, 256))
        total = None
        if size == block:
            for k, weight in enumerate(weights):
                right = weight[row : row + min(size, 256), columns : columns + block]
                left = grads[:, first + k * block : first + (k + 1) * block]
                term = dot(left, right, CONTRACT_LAST)
                total = term if total is None else total + term
        else:
            right = weights[row // size][:, columns : columns + block]
            total = dot(grads[:, first : first + block], right, CONTRACT_LAST)
        yield place_out, total


def column_steps(joint_width, width, block):
    return [*range(0, joint_width, 256), *range(joint_width, width, block)]


def early_kernel(pieces, weights, size, joint_width, place, *refs):
    row_refs, weight_refs = refs[:pieces], refs[pieces : pieces + weights]
    total, grads, normed = refs[pieces + weights :]
    rows = row_refs[0].shape[0] // 2
    block = weight_refs[0].shape[0]
    halves = row_refs[: pieces // 2], row_refs[pieces // 2 :]
    for pair, gathered in zip((grads, normed), halves):
        for core in range(2):
            for k in range(size):
                target = (core * size + k) * rows
                pair[target : target + rows] = pick(
                    place[2], gathered, size, k, slice(core * rows, (core + 1) * rows)
                )
    for columns in column_steps(joint_width, total.shape[1], block):
        for place_out, value in products(grads, normed, weight_refs, 0, joint_width, block, columns):
            total[:, place_out] = value


def late_kernel(first, joint_width, block, total, grads, normed, *refs):
    weight_refs, (keep, send) = refs[:-2], refs[-2:]
    length = keep.shape[0]
    if not weight_refs:
        keep[...] = total[:length]
        send[...] = total[length:].astype(jnp.bfloat16)
    for columns in column_steps(joint_width, keep.shape[1], block) if weight_refs else []:
        for place_out, value in products(
            grads, normed, weight_refs, first, joint_width, block, columns
        ):
            keep[:, place_out] = total[:length, place_out] + value[:length]
            send[:, place_out] = (total[length:, place_out] + value[length:]).astype(jnp.bfloat16)


def project(place, pieces, early, late, size, joint_width):
    rows = pieces[0].shape[0] // 2 * size
    half = pieces[0].shape[1]
    block, width = early[0].shape
    first = len(early) * block
    total, grads, normed = call(
        functools.partial(early_kernel, len(pieces), len(early), size, joint_width),
        [shaped((2 * rows, width), jnp.float32)] + [shaped((2 * rows, half))] * 2,
        [*pieces, *early],
        [place],
        flops=4 * rows * first * width,
        megabytes=24,
    )
    own, sent = call(
        functools.partial(late_kernel, first, joint_width, block),
        [shaped((rows, width), jnp.float32), shaped((rows, width))],
        [total, grads, normed, *late],
        flops=4 * rows * (half - first) * width,
        megabytes=24,
    )
    return own, sent, normed


def attention_kernel(rows, heads, place, lengths, own, sent, grads, partial):
    length = own.shape[0]
    width = heads * HD
    scale = 1 / math.sqrt(HD)
    tensor_index = place[2]

    def positions_of(dimension):
        order = lax.broadcasted_iota(jnp.int32, (length, length), dimension)
        return ((order // rows) ^ tensor_index) * rows + order % rows

    def labels_of(positions):
        labels, end = jnp.zeros((length, length), jnp.int32), 0
        for document in range(lengths.shape[1]):
            end = end + lengths[0, document]
            labels = labels + (end <= positions).astype(jnp.int32)
        return labels

    key_positions, query_positions = positions_of(0), positions_of(1)
    allowed = jnp.logical_and(
        labels_of(key_positions) == labels_of(query_positions), key_positions <= query_positions
    )

    def joined(first, second, columns):
        return (first[:, columns] + second[:, columns].astype(jnp.float32)).astype(jnp.bfloat16)

    keys = joined(own, sent, slice(width, width + HD))
    values = joined(own, sent, slice(width + HD, width + 2 * HD))
    key_total = value_total = None
    for head in range(heads):
        columns = slice(head * HD, (head + 1) * HD)
        start = width + 2 * HD + head * HD
        queries = joined(own, sent, columns)
        out_grad = joined(own, sent, slice(start, start + HD))
        scores = jnp.where(allowed, dot(keys, queries, CONTRACT_LAST) * scale, -1e30)
        expo = jnp.exp(scores - jnp.max(scores, axis=0, keepdims=True))
        probs = expo * (1 / jnp.sum(expo, axis=0, keepdims=True))
        prob_grad = dot(values, out_grad, CONTRACT_LAST)
        inner = jnp.sum(probs * prob_grad, axis=0, keepdims=True)
        score_grad = (probs * (prob_grad - inner) * scale).astype(jnp.bfloat16)
        grads[:, columns] = dot(score_grad, keys, CONTRACT_FIRST).astype(jnp.bfloat16)
        key_term = dot(score_grad, queries)
        value_term = dot(probs.astype(jnp.bfloat16), out_grad)
        key_total = key_term if head == 0 else key_total + key_term
        value_total = value_term if head == 0 else value_total + value_term
    if partial is None:
        grads[:, width : width + HD] = key_total.astype(jnp.bfloat16)
        grads[:, width + HD :] = value_total.astype(jnp.bfloat16)
    else:
        partial[:, :HD] = key_total
        partial[:, HD:] = value_total


def attention(place, lengths, own, sent, rows, width, split):
    length = own.shape[0]
    outs = [shaped((length, width if split else width + 2 * HD))]
    if split:
        outs.append(shaped((length, 2 * HD), jnp.float32))

    def kernel(*refs):
        attention_kernel(rows, width // HD, *(refs if split else (*refs, None)))

    return call(
        kernel,
        outs,
        [own, sent],
        [place, lengths],
        flops=10 * length * length * width,
    )


def weight_kernel(first, block, pair, own, other, *outs):
    length = own.shape[0]
    tile = min(block, 256)
    for number, out in enumerate(outs):
        for part in range(block // tile):
            start = (first + number) * block + part * tile
            out[part * tile : (part + 1) * tile] = (
                dot(pair[:length, start : start + tile], own[...], CONTRACT_FIRST)
                + dot(pair[length:, start : start + tile], other[...], CONTRACT_FIRST)
            ).astype(jnp.bfloat16)


def weight_terms(pair, own, other, first, count, block):
    return call(
        functools.partial(weight_kernel, first, block),
        [shaped((block, own.shape[1]))] * count,
        [pair, own, other],
        flops=2 * pair.shape[0] * block * count * own.shape[1],
    )


def row_kernel(weights, own, other, *refs):
    weight_refs, outs = refs[:weights], refs[weights:]
    length = own.shape[0]
    rows = length // len(outs)
    start = 0
    for weight in weight_refs:
        tile = min(weight.shape[0], 256)
        for part in range(weight.shape[0] // tile):
            right = weight[part * tile : (part + 1) * tile]
            for offset, left in ((0, own), (rows, other)):
                term = dot(left[...], right, CONTRACT_LAST).astype(jnp.bfloat16)
                for k, out in enumerate(outs):
                    out[offset : offset + rows, start : start + tile] = term[
                        k * rows : (k + 1) * rows
                    ]
            start += tile


def row_terms(own, other, weights, size):
    length, width = own.shape
    half = sum(weight.shape[0] for weight in weights)
    moved = sum(2 * weight.shape[0] * width for weight in weights) + 4 * length * (width + half)
    if width % 128 == 0:
        specs = [pl.BlockSpec((weight.shape[0], width), lambda i: (0, 0)) for weight in weights]
    else:
        weights = [weight[:, :width] for weight in weights]
        specs = [pl.BlockSpec(weight.shape, lambda i: (0, 0)) for weight in weights]
    part = (2 * length // size, half)
    return pl.pallas_call(
        functools.partial(row_kernel, len(weights)),
        grid=(1,),
        out_shape=[shaped(part)] * size,
        in_specs=[pl.BlockSpec(own.shape, lambda i: (0, 0))] * 2 + specs,
        out_specs=[pl.BlockSpec(part, lambda i: (0, 0))] * size,
        compiler_params=pltpu.CompilerParams(vmem_limit_bytes=24 * 2**20),
        cost_estimate=pl.CostEstimate(
            flops=4 * length * width * half, bytes_accessed=moved, transcendentals=0
        ),
    )(own, other, *weights)


def finish_kernel(count, share, *refs):
    total = refs[0][...].astype(jnp.float32)
    for part in refs[1:count]:
        total = total + part[...].astype(jnp.float32)
    total = total * share
    query_out, kv_out = refs[count:]
    width = query_out.shape[1]
    query_out[...] = total[:, :width]
    kv_out[...] = total[:, width:]


def finish(parts, query_width, share):
    block, width = parts[0].shape
    step = min(block, 128)

    def spec(columns):
        return pl.BlockSpec((step, columns), lambda i: (i, 0))

    return pl.pallas_call(
        functools.partial(finish_kernel, len(parts), share),
        grid=(block // step,),
        out_shape=[
            shaped((block, query_width), jnp.float32),
            shaped((block, width - query_width), jnp.float32),
        ],
        in_specs=[spec(width)] * len(parts),
        out_specs=[spec(query_width), spec(width - query_width)],
        compiler_params=pltpu.CompilerParams(vmem_limit_bytes=32 * 2**20),
        cost_estimate=pl.CostEstimate(
            flops=0, bytes_accessed=(2 * len(parts) + 4) * block * width, transcendentals=0
        ),
    )(*parts)


def input_kernel(count, block, place, tokens, gain, grad_out, handed, *refs):
    parts, out, gathered = refs[:count], refs[count], refs[count + 1]
    rows = tokens.shape[0]
    core = place[1]
    total = parts[0][:rows].astype(jnp.float32)
    for part in parts[1:]:
        total = total + part[:rows].astype(jnp.float32)
    for k in range(total.shape[1] // block):
        columns = slice(k * block, (k + 1) * block)
        gathered[:, pl.ds(column_start(place, k, core, block), block)] = total[:, columns]
        gathered[:, pl.ds(column_start(place, k, 1 - core, block), block)] = handed[
            :, columns
        ].astype(jnp.float32)
    values = tokens[...].astype(jnp.float32)
    root_mean = jnp.sqrt(jnp.mean(values * values, axis=-1, keepdims=True) + epsilon)
    unit = values / root_mean
    scaled = gathered[...] * gain[...].astype(jnp.float32)
    correction = unit * jnp.mean(scaled * unit, axis=-1, keepdims=True)
    out[...] = (grad_out[...].astype(jnp.float32) + (scaled - correction) / root_mean).astype(
        jnp.bfloat16
    )


def local(tokens, norm_gain, query_weight, kv_weight, out_weight, grad_out, doc_lengths):
    tensor_size = lax.axis_size("tensor")
    data_size = lax.axis_size("dp")
    tensor_index = lax.axis_index("tensor")
    data_index = lax.axis_index("dp")
    chips = data_size // 2
    place = jnp.stack([data_index >> 1, data_index & 1, tensor_index]).astype(jnp.int32)
    sharers = tensor_size // KVH
    levels = sharers.bit_length() - 1
    rows, width = tokens.shape
    block = width // data_size
    query_width = query_weight.shape[1]
    gain = norm_gain.reshape(1, width)

    merged = merge(query_weight, kv_weight, out_weight)
    merged, early_tokens, early_grads = tied(merged, tokens, grad_out)
    row_block = pltpu.VMEM((rows, width), jnp.bfloat16)
    grad_keep, normed_keep, send = pl.pallas_call(
        functools.partial(prepare_kernel, block),
        out_shape=[shaped((rows, width // 2))] * 2 + [shaped((2 * rows, width // 2))],
        in_specs=[SCALARS, WHOLE] + [pl.BlockSpec(memory_space=pltpu.HBM)] * 2,
        out_specs=[WHOLE] * 3,
        scratch_shapes=[row_block] * 3 + [pltpu.SemaphoreType.DMA((2,))],
        compiler_params=pltpu.CompilerParams(vmem_limit_bytes=56 * 2**20),
        cost_estimate=pl.CostEstimate(
            flops=0, bytes_accessed=8 * rows * width, transcendentals=0
        ),
    )(place, gain, early_grads, early_tokens)
    joint_width = query_width + kv_weight.shape[1]
    sent = swap(send, "dp", 1)
    early, late = gather_chips(merged)
    row_pieces = gather_tensor(jnp.concatenate([grad_keep, sent[:rows]], axis=0))
    row_pieces += gather_tensor(jnp.concatenate([normed_keep, sent[rows:]], axis=0))
    own, sent, normed = project(place, row_pieces, early, late, tensor_size, joint_width)
    sent = swap(sent, "dp", 1)
    if levels:
        joined = (own + sent.astype(jnp.float32)).astype(jnp.bfloat16)
        keyvals = joined[:, query_width:joint_width]
        for bit_index in range(levels):
            partner = swap(keyvals, "tensor", 2**bit_index)
            upper = tensor_index >> bit_index & 1 == 1
            keyvals = jnp.concatenate(
                [jnp.where(upper, partner, keyvals), jnp.where(upper, keyvals, partner)], axis=1
            )
        own = jnp.concatenate(
            [joined[:, :query_width], keyvals, joined[:, joint_width:]], axis=1
        ).astype(jnp.float32)
        sent = jnp.zeros(own.shape, jnp.bfloat16)
    combined, *partial = attention(place, doc_lengths, own, sent, rows, query_width, levels > 0)
    if levels:
        kv_partial = partial[0]
        for bit_index in reversed(range(levels)):
            half_cols = kv_partial.shape[1] // 2
            upper = tensor_index >> bit_index & 1 == 1
            lower_cols = kv_partial[:, :half_cols]
            higher_cols = kv_partial[:, half_cols:]
            kept = jnp.where(upper, higher_cols, lower_cols)
            handed = jnp.where(upper, lower_cols, higher_cols)
            kv_partial = kept + swap(handed.astype(jnp.bfloat16), "tensor", 2**bit_index).astype(
                jnp.float32
            )
        combined = jnp.concatenate([combined, kv_partial.astype(jnp.bfloat16)], axis=1)
    other = swap(combined, "dp", 1)

    far = weight_terms(normed, combined, other, chips - 1, 1, block)
    near = weight_terms(normed, combined, other, 0, chips - 1, block)
    row_parts = scatter_tensor(row_terms(combined, other, early + late, tensor_size))
    weight_parts = scatter_chips([*near, *far])
    handed = sum(part[rows:].astype(jnp.float32) for part in row_parts).astype(jnp.bfloat16)
    handed = swap(handed, "dp", 1)
    query_grad, kv_grad = finish(weight_parts, query_width, 1 / data_size)
    handed, query_grad, kv_grad = tied(handed, query_grad, kv_grad)
    (input_grad,) = call(
        functools.partial(input_kernel, len(row_parts), block),
        [shaped((rows, width))],
        [tokens, gain, grad_out, handed, *row_parts],
        [place],
        [pltpu.VMEM((rows, width), jnp.float32)],
    )
    return (input_grad, query_grad, kv_grad)


def solution(mesh):
    placed = (
        P(("dp", "tensor"), None),
        P(),
        P("dp", "tensor"),
        P("dp", "tensor"),
        P("tensor", "dp"),
        P(("dp", "tensor"), None),
        P("dp", None),
    )
    return jax.shard_map(
        local,
        mesh=mesh,
        in_specs=placed,
        out_specs=(P(("dp", "tensor"), None), P("dp", "tensor"), P("dp", "tensor")),
        check_vma=False,
    )
```

```python
import functools
import math

import jax
import jax.numpy as jnp
from jax import lax
from jax.experimental import pallas as pl
from jax.experimental.pallas import tpu as pltpu
from jax.sharding import PartitionSpec as P

KVH = 4
HD = 128

epsilon = 1e-05
CONTRACT_LAST = (((1,), (1,)), ((), ()))
CONTRACT_FIRST = (((0,), (0,)), ((), ()))
WHOLE = pl.BlockSpec(memory_space=pltpu.VMEM)
SCALARS = pl.BlockSpec(memory_space=pltpu.SMEM)


def call(kernel, outs, operands, scalars=(), scratch=(), flops=0, megabytes=24):
    moved = sum(math.prod(a.shape) * a.dtype.itemsize for a in (*operands, *outs))
    return pl.pallas_call(
        kernel,
        out_shape=outs,
        in_specs=[SCALARS] * len(scalars) + [WHOLE] * len(operands),
        out_specs=[WHOLE] * len(outs),
        scratch_shapes=scratch,
        compiler_params=pltpu.CompilerParams(vmem_limit_bytes=megabytes * 2**20),
        cost_estimate=pl.CostEstimate(flops=flops, bytes_accessed=moved, transcendentals=0),
    )(*scalars, *operands)


def shaped(shape, dtype=jnp.bfloat16):
    return jax.ShapeDtypeStruct(shape, dtype)


def dot(left, right, contract=(((1,), (0,)), ((), ()))):
    return lax.dot_general(left, right, contract, preferred_element_type=jnp.float32)


def swap(value, axis, mask):
    pairs = [(source, source ^ mask) for source in range(lax.axis_size(axis))]
    return lax.ppermute(value, axis, pairs)


def tied(*values):
    return lax.optimization_barrier(values)


def everyone(value, axis, unit):
    size = lax.axis_size(axis) // unit
    return [value] + [swap(value, axis, unit * k) for k in range(1, size)]


def gather_chips(top, bottom, after):
    if lax.axis_size("dp") != 8:
        halves = zip(everyone(top, "dp", 2), everyone(bottom, "dp", 2))
        return [half for pair in halves for half in pair], []
    x_top = swap(top, "dp", 2)
    y_bottom = swap(bottom, "dp", 4)
    later, x_top, *_ = tied(bottom, x_top, *after)
    x_bottom = swap(later, "dp", 2)
    later, y_bottom, *_ = tied(top, y_bottom, *after)
    y_top = swap(later, "dp", 4)
    far_bottom, x_bottom = tied(y_bottom, x_bottom)
    far_bottom = swap(far_bottom, "dp", 2)
    far_top, y_top = tied(x_top, y_top)
    far_top = swap(far_top, "dp", 4)
    return [top, bottom, x_top, x_bottom, y_top, y_bottom], [far_top, far_bottom]


def along(value, pairs):
    return lax.ppermute(value, "tensor", pairs)


def first_hops(value):
    if lax.axis_size("tensor") != 4:
        return []
    right_one = along(value, [(0, 1), (1, 2), (2, 3)])
    left_one = along(value, [(1, 0), (2, 1), (3, 2)])
    return tied(right_one, left_one)


def gather_tensor(value, ones):
    if lax.axis_size("tensor") != 4:
        return everyone(value, "tensor", 1)
    right_one, left_one = ones
    right_two = along(right_one, [(1, 2), (2, 3)])
    left_two = along(left_one, [(1, 0), (2, 1)])
    right_two, left_two = tied(right_two, left_two)
    last = along(
        jnp.where(lax.axis_index("tensor") == 1, left_two, right_two), [(1, 0), (2, 3)]
    )
    return [value, right_one, left_one, right_two, left_two, last]


def pick(index, pieces, size, k, rows):
    if len(pieces) == size:
        return pieces[k][rows]
    own, right_one, left_one, right_two, left_two, last = [piece.at[rows] for piece in pieces]
    if k == 0:
        return own[...]
    if k == 1:
        return jnp.where(index % 2 == 1, right_one[...], left_one[...])
    if k == 2:
        return jnp.where(index >= 2, right_two[...], left_two[...])
    near = jnp.where(index == 1, left_one[...], right_one[...])
    return jnp.where(jnp.logical_or(index == 0, index == 3), last[...], near)


def inner_pair(value):
    return along(value, [(1, 2), (2, 1)])


def outer_pair(value):
    return along(value, [(3, 2), (0, 1)])


def scatter_chips(blocks):
    if len(blocks) != 4:
        return [blocks[0]] + [swap(blocks[k], "dp", 2 * k) for k in range(1, len(blocks))]
    half = blocks[0].shape[0] // 2
    far_top = swap(blocks[3][:half], "dp", 4)
    far_bottom = swap(blocks[3][half:], "dp", 2)
    near_x = swap(
        jnp.concatenate([blocks[1][:half] + far_top, blocks[1][half:]], axis=0), "dp", 2
    )
    near_y = swap(
        jnp.concatenate([blocks[2][:half], blocks[2][half:] + far_bottom], axis=0), "dp", 4
    )
    return [blocks[0], near_x, near_y]


def scatter_tensor(blocks):
    if len(blocks) != 4:
        return [blocks[0]] + [swap(blocks[k], "tensor", k) for k in range(1, len(blocks))]
    outer, inner = outer_pair(blocks[3]), inner_pair(blocks[3])
    outer, inner = tied(outer, inner)
    carried, adjacent = tied(blocks[2] + outer, blocks[1])
    two, one = swap(carried, "tensor", 2), swap(adjacent, "tensor", 1)
    return [blocks[0], one, inner, two]


def column_start(place, k, which, block):
    return pl.multiple_of(((place[0] ^ k) * 2 + which) * block, 128)


def prepare_kernel(block, place, grad_out, tokens, gain, grad_keep, normed_keep, send, normed):
    rows, core = tokens.shape[0], place[1]
    values = tokens[...].astype(jnp.float32)
    root_mean = jnp.sqrt(jnp.mean(values * values, axis=-1, keepdims=True) + epsilon)
    normed[...] = (values / root_mean * gain[...].astype(jnp.float32)).astype(jnp.bfloat16)
    for start, source, keep in ((0, grad_out, grad_keep), (rows, normed, normed_keep)):
        for k in range(keep.shape[1] // block):
            columns = slice(k * block, (k + 1) * block)
            keep[:, columns] = source[:, pl.ds(column_start(place, k, core, block), block)]
            send[start : start + rows, columns] = source[
                :, pl.ds(column_start(place, k, 1 - core, block), block)
            ]


def merge_kernel(query_weight, kv_weight, out_weight, *halves):
    half = halves[0].shape[0]
    for number, merged in enumerate(halves):
        start = 0
        for weight in (query_weight, kv_weight):
            merged[:, start : start + weight.shape[1]] = weight[number * half : (number + 1) * half]
            start += weight.shape[1]
        for chunk in range(0, out_weight.shape[0], 2 * half):
            first = chunk + number * half
            merged[:, start : start + out_weight.shape[1]] = out_weight[first : first + half]
            start += out_weight.shape[1]


def products(grads, normed, weights, first, joint_width, block, columns):
    size = weights[0].shape[0]
    if columns < joint_width:
        width = min(256, joint_width - columns)
        total = None
        for k, weight in enumerate(weights):
            left = normed[:, first + k * size : first + (k + 1) * size]
            term = dot(left, weight[:, columns : columns + width])
            total = term if total is None else total + term
        yield slice(columns, columns + width), total
        return
    for half in range(2):
        total = None
        for k, weight in enumerate(weights[half::2]):
            left = grads[:, first + k * block : first + (k + 1) * block]
            term = dot(left, weight[:, columns : columns + block], CONTRACT_LAST)
            total = term if total is None else total + term
        yield slice(columns + half * size, columns + (half + 1) * size), total


def column_steps(joint_width, width, block):
    return [*range(0, joint_width, 256), *range(joint_width, width, block)]


def early_kernel(pieces, weights, size, joint_width, place, *refs):
    row_refs, weight_refs = refs[:pieces], refs[pieces : pieces + weights]
    total, grads, normed = refs[pieces + weights :]
    rows = row_refs[0].shape[0] // 2
    block = 2 * weight_refs[0].shape[0]
    halves = row_refs[: pieces // 2], row_refs[pieces // 2 :]
    for pair, gathered in zip((grads, normed), halves):
        for core in range(2):
            for k in range(size):
                target = (core * size + k) * rows
                pair[target : target + rows] = pick(
                    place[2], gathered, size, k, slice(core * rows, (core + 1) * rows)
                )
    for columns in column_steps(joint_width, total.shape[1], block):
        for place_out, value in products(grads, normed, weight_refs, 0, joint_width, block, columns):
            total[:, place_out] = value


def late_kernel(first, joint_width, block, total, grads, normed, *refs):
    weight_refs, (keep, send) = refs[:-2], refs[-2:]
    length = keep.shape[0]
    if not weight_refs:
        keep[...] = total[:length]
        send[...] = total[length:].astype(jnp.bfloat16)
    for columns in column_steps(joint_width, keep.shape[1], block) if weight_refs else []:
        for place_out, value in products(
            grads, normed, weight_refs, first, joint_width, block, columns
        ):
            keep[:, place_out] = total[:length, place_out] + value[:length]
            send[:, place_out] = (total[length:, place_out] + value[length:]).astype(jnp.bfloat16)


def project(place, pieces, early, late, size, joint_width):
    rows = pieces[0].shape[0] // 2 * size
    half = pieces[0].shape[1]
    half_block, width = early[0].shape
    block, first = 2 * half_block, len(early) * half_block
    total, grads, normed = call(
        functools.partial(early_kernel, len(pieces), len(early), size, joint_width),
        [shaped((2 * rows, width), jnp.float32)] + [shaped((2 * rows, half))] * 2,
        [*pieces, *early],
        [place],
        flops=4 * rows * first * width,
        megabytes=24,
    )
    own, sent = call(
        functools.partial(late_kernel, first, joint_width, block),
        [shaped((rows, width), jnp.float32), shaped((rows, width))],
        [total, grads, normed, *late],
        flops=4 * rows * (half - first) * width,
        megabytes=24,
    )
    return own, sent, normed


def attention_kernel(rows, heads, place, lengths, own, sent, grads, partial):
    length = own.shape[0]
    width = heads * HD
    scale = 1 / math.sqrt(HD)
    tensor_index = place[2]

    def positions_of(dimension):
        order = lax.broadcasted_iota(jnp.int32, (length, length), dimension)
        return ((order // rows) ^ tensor_index) * rows + order % rows

    def labels_of(positions):
        labels, end = jnp.zeros((length, length), jnp.int32), 0
        for document in range(lengths.shape[1]):
            end = end + lengths[0, document]
            labels = labels + (end <= positions).astype(jnp.int32)
        return labels

    key_positions, query_positions = positions_of(0), positions_of(1)
    allowed = jnp.logical_and(
        labels_of(key_positions) == labels_of(query_positions), key_positions <= query_positions
    )

    def joined(first, second, columns):
        return (first[:, columns] + second[:, columns].astype(jnp.float32)).astype(jnp.bfloat16)

    keys = joined(own, sent, slice(width, width + HD))
    values = joined(own, sent, slice(width + HD, width + 2 * HD))
    key_total = value_total = None
    for head in range(heads):
        columns = slice(head * HD, (head + 1) * HD)
        start = width + 2 * HD + head * HD
        queries = joined(own, sent, columns)
        out_grad = joined(own, sent, slice(start, start + HD))
        scores = jnp.where(allowed, dot(keys, queries, CONTRACT_LAST) * scale, -1e30)
        expo = jnp.exp(scores - jnp.max(scores, axis=0, keepdims=True))
        probs = expo * (1 / jnp.sum(expo, axis=0, keepdims=True))
        prob_grad = dot(values, out_grad, CONTRACT_LAST)
        inner = jnp.sum(probs * prob_grad, axis=0, keepdims=True)
        score_grad = (probs * (prob_grad - inner) * scale).astype(jnp.bfloat16)
        grads[:, columns] = dot(score_grad, keys, CONTRACT_FIRST).astype(jnp.bfloat16)
        key_term = dot(score_grad, queries)
        value_term = dot(probs.astype(jnp.bfloat16), out_grad)
        key_total = key_term if head == 0 else key_total + key_term
        value_total = value_term if head == 0 else value_total + value_term
    if partial is None:
        grads[:, width : width + HD] = key_total.astype(jnp.bfloat16)
        grads[:, width + HD :] = value_total.astype(jnp.bfloat16)
    else:
        partial[:, :HD] = key_total
        partial[:, HD:] = value_total


def attention(place, lengths, own, sent, rows, width, split):
    length = own.shape[0]
    outs = [shaped((length, width if split else width + 2 * HD))]
    if split:
        outs.append(shaped((length, 2 * HD), jnp.float32))

    def kernel(*refs):
        attention_kernel(rows, width // HD, *(refs if split else (*refs, None)))

    return call(
        kernel,
        outs,
        [own, sent],
        [place, lengths],
        flops=10 * length * length * width,
    )


def weight_kernel(first, block, pair, own, other, *outs):
    length = own.shape[0]
    tile = min(block, 256)
    for number, out in enumerate(outs):
        for part in range(block // tile):
            start = (first + number) * block + part * tile
            out[part * tile : (part + 1) * tile] = (
                dot(pair[:length, start : start + tile], own[...], CONTRACT_FIRST)
                + dot(pair[length:, start : start + tile], other[...], CONTRACT_FIRST)
            ).astype(jnp.bfloat16)


def weight_terms(pair, own, other, first, count, block):
    return call(
        functools.partial(weight_kernel, first, block),
        [shaped((block, own.shape[1]))] * count,
        [pair, own, other],
        flops=2 * pair.shape[0] * block * count * own.shape[1],
    )


def row_kernel(weights, own, other, *refs):
    weight_refs, outs = refs[:weights], refs[weights:]
    length = own.shape[0]
    rows = length // len(outs)
    start = 0
    for weight in weight_refs:
        tile = min(weight.shape[0], 256)
        for part in range(weight.shape[0] // tile):
            right = weight[part * tile : (part + 1) * tile]
            for offset, left in ((0, own), (rows, other)):
                term = dot(left[...], right, CONTRACT_LAST).astype(jnp.bfloat16)
                for k, out in enumerate(outs):
                    out[offset : offset + rows, start : start + tile] = term[
                        k * rows : (k + 1) * rows
                    ]
            start += tile


def row_terms(own, other, weights, size):
    length, width = own.shape
    half = sum(weight.shape[0] for weight in weights)
    moved = sum(2 * weight.shape[0] * width for weight in weights) + 4 * length * (width + half)
    if width % 128 == 0:
        specs = [pl.BlockSpec((weight.shape[0], width), lambda i: (0, 0)) for weight in weights]
    else:
        weights = [weight[:, :width] for weight in weights]
        specs = [pl.BlockSpec(weight.shape, lambda i: (0, 0)) for weight in weights]
    part = (2 * length // size, half)
    return pl.pallas_call(
        functools.partial(row_kernel, len(weights)),
        grid=(1,),
        out_shape=[shaped(part)] * size,
        in_specs=[pl.BlockSpec(own.shape, lambda i: (0, 0))] * 2 + specs,
        out_specs=[pl.BlockSpec(part, lambda i: (0, 0))] * size,
        compiler_params=pltpu.CompilerParams(vmem_limit_bytes=24 * 2**20),
        cost_estimate=pl.CostEstimate(
            flops=4 * length * width * half, bytes_accessed=moved, transcendentals=0
        ),
    )(own, other, *weights)


def finish_kernel(count, share, *refs):
    total = refs[0][...].astype(jnp.float32)
    for part in refs[1:count]:
        total = total + part[...].astype(jnp.float32)
    total = total * share
    query_out, kv_out = refs[count:]
    width = query_out.shape[1]
    query_out[...] = total[:, :width]
    kv_out[...] = total[:, width:]


def finish(parts, query_width, share):
    block, width = parts[0].shape
    step = min(block, 128)

    def spec(columns):
        return pl.BlockSpec((step, columns), lambda i: (i, 0))

    return pl.pallas_call(
        functools.partial(finish_kernel, len(parts), share),
        grid=(block // step,),
        out_shape=[
            shaped((block, query_width), jnp.float32),
            shaped((block, width - query_width), jnp.float32),
        ],
        in_specs=[spec(width)] * len(parts),
        out_specs=[spec(query_width), spec(width - query_width)],
        compiler_params=pltpu.CompilerParams(vmem_limit_bytes=32 * 2**20),
        cost_estimate=pl.CostEstimate(
            flops=0, bytes_accessed=(2 * len(parts) + 4) * block * width, transcendentals=0
        ),
    )(*parts)


def input_kernel(count, block, place, tokens, gain, grad_out, handed, *refs):
    parts, out, gathered = refs[:count], refs[count], refs[count + 1]
    rows = tokens.shape[0]
    core = place[1]
    total = parts[0][:rows].astype(jnp.float32)
    for part in parts[1:]:
        total = total + part[:rows].astype(jnp.float32)
    for k in range(total.shape[1] // block):
        columns = slice(k * block, (k + 1) * block)
        gathered[:, pl.ds(column_start(place, k, core, block), block)] = total[:, columns]
        gathered[:, pl.ds(column_start(place, k, 1 - core, block), block)] = handed[
            :, columns
        ].astype(jnp.float32)
    values = tokens[...].astype(jnp.float32)
    root_mean = jnp.sqrt(jnp.mean(values * values, axis=-1, keepdims=True) + epsilon)
    unit = values / root_mean
    scaled = gathered[...] * gain[...].astype(jnp.float32)
    correction = unit * jnp.mean(scaled * unit, axis=-1, keepdims=True)
    out[...] = (grad_out[...].astype(jnp.float32) + (scaled - correction) / root_mean).astype(
        jnp.bfloat16
    )


def local(tokens, norm_gain, query_weight, kv_weight, out_weight, grad_out, doc_lengths):
    tensor_size = lax.axis_size("tensor")
    data_size = lax.axis_size("dp")
    tensor_index = lax.axis_index("tensor")
    data_index = lax.axis_index("dp")
    chips = data_size // 2
    place = jnp.stack([data_index >> 1, data_index & 1, tensor_index]).astype(jnp.int32)
    sharers = tensor_size // KVH
    levels = sharers.bit_length() - 1
    rows, width = tokens.shape
    block = width // data_size
    query_width = query_weight.shape[1]
    gain = norm_gain.reshape(1, width)

    grad_keep, normed_keep, send = call(
        functools.partial(prepare_kernel, block),
        [shaped((rows, width // 2))] * 2 + [shaped((2 * rows, width // 2))],
        [grad_out, tokens, gain],
        [place],
        [pltpu.VMEM((rows, width), jnp.bfloat16)],
    )
    joint_width = query_width + kv_weight.shape[1]
    send, out_weight, query_weight, kv_weight = tied(send, out_weight, query_weight, kv_weight)
    sent = swap(send, "dp", 1)
    merged = call(
        merge_kernel,
        [shaped((block // 2, joint_width + out_weight.shape[0]))] * 2,
        [query_weight, kv_weight, out_weight],
    )
    grad_pair = jnp.concatenate([grad_keep, sent[:rows]], axis=0)
    normed_pair = jnp.concatenate([normed_keep, sent[rows:]], axis=0)
    ones = first_hops(grad_pair)
    early, late = gather_chips(*merged, ones)
    row_pieces = gather_tensor(grad_pair, ones)
    row_pieces += gather_tensor(normed_pair, first_hops(normed_pair))
    own, sent, normed = project(place, row_pieces, early, late, tensor_size, joint_width)
    sent = swap(sent, "dp", 1)
    if levels:
        joined = (own + sent.astype(jnp.float32)).astype(jnp.bfloat16)
        keyvals = joined[:, query_width:joint_width]
        for bit_index in range(levels):
            partner = swap(keyvals, "tensor", 2**bit_index)
            upper = tensor_index >> bit_index & 1 == 1
            keyvals = jnp.concatenate(
                [jnp.where(upper, partner, keyvals), jnp.where(upper, keyvals, partner)], axis=1
            )
        own = jnp.concatenate(
            [joined[:, :query_width], keyvals, joined[:, joint_width:]], axis=1
        ).astype(jnp.float32)
        sent = jnp.zeros(own.shape, jnp.bfloat16)
    combined, *partial = attention(place, doc_lengths, own, sent, rows, query_width, levels > 0)
    if levels:
        kv_partial = partial[0]
        for bit_index in reversed(range(levels)):
            half_cols = kv_partial.shape[1] // 2
            upper = tensor_index >> bit_index & 1 == 1
            lower_cols = kv_partial[:, :half_cols]
            higher_cols = kv_partial[:, half_cols:]
            kept = jnp.where(upper, higher_cols, lower_cols)
            handed = jnp.where(upper, lower_cols, higher_cols)
            kv_partial = kept + swap(handed.astype(jnp.bfloat16), "tensor", 2**bit_index).astype(
                jnp.float32
            )
        combined = jnp.concatenate([combined, kv_partial.astype(jnp.bfloat16)], axis=1)
    other = swap(combined, "dp", 1)

    far = weight_terms(normed, combined, other, chips - 1, 1, block)
    near = weight_terms(normed, combined, other, 0, chips - 1, block)
    row_parts = scatter_tensor(row_terms(combined, other, early + late, tensor_size))
    weight_parts = scatter_chips([*near, *far])
    handed = sum(part[rows:].astype(jnp.float32) for part in row_parts).astype(jnp.bfloat16)
    handed = swap(handed, "dp", 1)
    query_grad, kv_grad = finish(weight_parts, query_width, 1 / data_size)
    handed, query_grad, kv_grad = tied(handed, query_grad, kv_grad)
    (input_grad,) = call(
        functools.partial(input_kernel, len(row_parts), block),
        [shaped((rows, width))],
        [tokens, gain, grad_out, handed, *row_parts],
        [place],
        [pltpu.VMEM((rows, width), jnp.float32)],
    )
    return (input_grad, query_grad, kv_grad)


def solution(mesh):
    placed = (
        P(("dp", "tensor"), None),
        P(),
        P("dp", "tensor"),
        P("dp", "tensor"),
        P("tensor", "dp"),
        P(("dp", "tensor"), None),
        P("dp", None),
    )
    return jax.shard_map(
        local,
        mesh=mesh,
        in_specs=placed,
        out_specs=(P(("dp", "tensor"), None), P("dp", "tensor"), P("dp", "tensor")),
        check_vma=False,
    )
```

```python
import functools
import math

import jax
import jax.numpy as jnp
from jax import lax
from jax.experimental import pallas as pl
from jax.experimental.pallas import tpu as pltpu
from jax.sharding import PartitionSpec as P

KVH = 4
HD = 128

epsilon = 1e-05
CONTRACT_LAST = (((1,), (1,)), ((), ()))
CONTRACT_FIRST = (((0,), (0,)), ((), ()))
WHOLE = pl.BlockSpec(memory_space=pltpu.VMEM)
SCALARS = pl.BlockSpec(memory_space=pltpu.SMEM)


def call(kernel, outs, operands, scalars=(), scratch=(), flops=0, megabytes=24):
    moved = sum(math.prod(a.shape) * a.dtype.itemsize for a in (*operands, *outs))
    return pl.pallas_call(
        kernel,
        out_shape=outs,
        in_specs=[SCALARS] * len(scalars) + [WHOLE] * len(operands),
        out_specs=[WHOLE] * len(outs),
        scratch_shapes=scratch,
        compiler_params=pltpu.CompilerParams(vmem_limit_bytes=megabytes * 2**20),
        cost_estimate=pl.CostEstimate(flops=flops, bytes_accessed=moved, transcendentals=0),
    )(*scalars, *operands)


def shaped(shape, dtype=jnp.bfloat16):
    return jax.ShapeDtypeStruct(shape, dtype)


def dot(left, right, contract=(((1,), (0,)), ((), ()))):
    return lax.dot_general(left, right, contract, preferred_element_type=jnp.float32)


def swap(value, axis, mask):
    pairs = [(source, source ^ mask) for source in range(lax.axis_size(axis))]
    return lax.ppermute(value, axis, pairs)


def tied(*values):
    return lax.optimization_barrier(values)


def everyone(value, axis, unit):
    size = lax.axis_size(axis) // unit
    return [value] + [swap(value, axis, unit * k) for k in range(1, size)]


def gather_chips(value):
    if lax.axis_size("dp") != 8:
        return everyone(value, "dp", 2), []
    half = value.shape[0] // 2
    near_x = swap(value, "dp", 2)
    near_y = swap(value, "dp", 4)
    near_x, near_y = tied(near_x, near_y)
    far_top = swap(near_x[:half], "dp", 4)
    far_bottom = swap(near_y[half:], "dp", 2)
    return [value, near_x, near_y], [far_top, far_bottom]


def along(value, pairs):
    return lax.ppermute(value, "tensor", pairs)


def gather_tensor(value):
    if lax.axis_size("tensor") != 4:
        return everyone(value, "tensor", 1)
    right_one = along(value, [(0, 1), (1, 2), (2, 3)])
    left_one = along(value, [(1, 0), (2, 1), (3, 2)])
    right_one, left_one = tied(right_one, left_one)
    right_two = along(right_one, [(1, 2), (2, 3)])
    left_two = along(left_one, [(1, 0), (2, 1)])
    right_two, left_two = tied(right_two, left_two)
    last = along(
        jnp.where(lax.axis_index("tensor") == 1, left_two, right_two), [(1, 0), (2, 3)]
    )
    return [value, right_one, left_one, right_two, left_two, last]


def pick(index, pieces, size, k, rows):
    if len(pieces) == size:
        return pieces[k][rows]
    own, right_one, left_one, right_two, left_two, last = [piece.at[rows] for piece in pieces]
    if k == 0:
        return own[...]
    if k == 1:
        return jnp.where(index % 2 == 1, right_one[...], left_one[...])
    if k == 2:
        return jnp.where(index >= 2, right_two[...], left_two[...])
    near = jnp.where(index == 1, left_one[...], right_one[...])
    return jnp.where(jnp.logical_or(index == 0, index == 3), last[...], near)


def inner_pair(value):
    return along(value, [(1, 2), (2, 1)])


def outer_pair(value):
    return along(value, [(3, 2), (0, 1)])


def scatter_chips(blocks):
    if len(blocks) != 4:
        return [blocks[0]] + [swap(blocks[k], "dp", 2 * k) for k in range(1, len(blocks))]
    half = blocks[0].shape[0] // 2
    far_top = swap(blocks[3][:half], "dp", 4)
    far_bottom = swap(blocks[3][half:], "dp", 2)
    near_x = swap(
        jnp.concatenate([blocks[1][:half] + far_top, blocks[1][half:]], axis=0), "dp", 2
    )
    near_y = swap(
        jnp.concatenate([blocks[2][:half], blocks[2][half:] + far_bottom], axis=0), "dp", 4
    )
    return [blocks[0], near_x, near_y]


def scatter_tensor(blocks):
    if len(blocks) != 4:
        return [blocks[0]] + [swap(blocks[k], "tensor", k) for k in range(1, len(blocks))]
    outer, inner = outer_pair(blocks[3]), inner_pair(blocks[3])
    outer, inner = tied(outer, inner)
    carried, adjacent = tied(blocks[2] + outer, blocks[1])
    two, one = swap(carried, "tensor", 2), swap(adjacent, "tensor", 1)
    return [blocks[0], one, inner, two]


def column_start(place, k, which, block):
    return pl.multiple_of(((place[0] ^ k) * 2 + which) * block, 128)


def prepare_kernel(block, place, grad_out, tokens, gain, grad_keep, normed_keep, send, normed):
    rows, core = tokens.shape[0], place[1]
    values = tokens[...].astype(jnp.float32)
    root_mean = jnp.sqrt(jnp.mean(values * values, axis=-1, keepdims=True) + epsilon)
    normed[...] = (values / root_mean * gain[...].astype(jnp.float32)).astype(jnp.bfloat16)
    for start, source, keep in ((0, grad_out, grad_keep), (rows, normed, normed_keep)):
        for k in range(keep.shape[1] // block):
            columns = slice(k * block, (k + 1) * block)
            keep[:, columns] = source[:, pl.ds(column_start(place, k, core, block), block)]
            send[start : start + rows, columns] = source[
                :, pl.ds(column_start(place, k, 1 - core, block), block)
            ]


def merge_kernel(query_weight, kv_weight, out_weight, merged):
    block, start = merged.shape[0], 0
    parts = [query_weight, kv_weight]
    parts += [out_weight.at[k : k + block] for k in range(0, out_weight.shape[0], block)]
    for part in parts:
        merged[:, start : start + part.shape[1]] = part[...]
        start += part.shape[1]


def products(grads, normed, weights, first, joint_width, block, columns):
    size = weights[0].shape[0]
    if columns < joint_width:
        width = min(256, joint_width - columns)
        total = None
        for k, weight in enumerate(weights):
            left = normed[:, first + k * size : first + (k + 1) * size]
            term = dot(left, weight[:, columns : columns + width])
            total = term if total is None else total + term
        yield slice(columns, columns + width), total
        return
    for row in range(0, block, min(size, 256)):
        place_out = slice(columns + row, columns + row + min(size, 256))
        total = None
        if size == block:
            for k, weight in enumerate(weights):
                right = weight[row : row + min(size, 256), columns : columns + block]
                left = grads[:, first + k * block : first + (k + 1) * block]
                term = dot(left, right, CONTRACT_LAST)
                total = term if total is None else total + term
        else:
            right = weights[row // size][:, columns : columns + block]
            total = dot(grads[:, first : first + block], right, CONTRACT_LAST)
        yield place_out, total


def column_steps(joint_width, width, block):
    return [*range(0, joint_width, 256), *range(joint_width, width, block)]


def early_kernel(pieces, weights, size, joint_width, place, *refs):
    row_refs, weight_refs = refs[:pieces], refs[pieces : pieces + weights]
    total, grads, normed = refs[pieces + weights :]
    rows = row_refs[0].shape[0] // 2
    block = weight_refs[0].shape[0]
    halves = row_refs[: pieces // 2], row_refs[pieces // 2 :]
    for pair, gathered in zip((grads, normed), halves):
        for core in range(2):
            for k in range(size):
                target = (core * size + k) * rows
                pair[target : target + rows] = pick(
                    place[2], gathered, size, k, slice(core * rows, (core + 1) * rows)
                )
    for columns in column_steps(joint_width, total.shape[1], block):
        for place_out, value in products(grads, normed, weight_refs, 0, joint_width, block, columns):
            total[:, place_out] = value


def late_kernel(first, joint_width, block, total, grads, normed, *refs):
    weight_refs, (keep, send) = refs[:-2], refs[-2:]
    length = keep.shape[0]
    if not weight_refs:
        keep[...] = total[:length]
        send[...] = total[length:].astype(jnp.bfloat16)
    for columns in column_steps(joint_width, keep.shape[1], block) if weight_refs else []:
        for place_out, value in products(
            grads, normed, weight_refs, first, joint_width, block, columns
        ):
            keep[:, place_out] = total[:length, place_out] + value[:length]
            send[:, place_out] = (total[length:, place_out] + value[length:]).astype(jnp.bfloat16)


def project(place, pieces, early, late, size, joint_width):
    rows = pieces[0].shape[0] // 2 * size
    half = pieces[0].shape[1]
    block, width = early[0].shape
    first = len(early) * block
    total, grads, normed = call(
        functools.partial(early_kernel, len(pieces), len(early), size, joint_width),
        [shaped((2 * rows, width), jnp.float32)] + [shaped((2 * rows, half))] * 2,
        [*pieces, *early],
        [place],
        flops=4 * rows * first * width,
        megabytes=24,
    )
    own, sent = call(
        functools.partial(late_kernel, first, joint_width, block),
        [shaped((rows, width), jnp.float32), shaped((rows, width))],
        [total, grads, normed, *late],
        flops=4 * rows * (half - first) * width,
        megabytes=24,
    )
    return own, sent, normed


def attention_kernel(rows, heads, place, lengths, own, sent, grads, partial):
    length = own.shape[0]
    width = heads * HD
    scale = 1 / math.sqrt(HD)
    tensor_index = place[2]

    def positions_of(dimension):
        order = lax.broadcasted_iota(jnp.int32, (length, length), dimension)
        return ((order // rows) ^ tensor_index) * rows + order % rows

    def labels_of(positions):
        labels, end = jnp.zeros((length, length), jnp.int32), 0
        for document in range(lengths.shape[1]):
            end = end + lengths[0, document]
            labels = labels + (end <= positions).astype(jnp.int32)
        return labels

    key_positions, query_positions = positions_of(0), positions_of(1)
    allowed = jnp.logical_and(
        labels_of(key_positions) == labels_of(query_positions), key_positions <= query_positions
    )

    def joined(first, second, columns):
        return (first[:, columns] + second[:, columns].astype(jnp.float32)).astype(jnp.bfloat16)

    keys = joined(own, sent, slice(width, width + HD))
    values = joined(own, sent, slice(width + HD, width + 2 * HD))
    key_total = value_total = None
    for head in range(heads):
        columns = slice(head * HD, (head + 1) * HD)
        start = width + 2 * HD + head * HD
        queries = joined(own, sent, columns)
        out_grad = joined(own, sent, slice(start, start + HD))
        scores = jnp.where(allowed, dot(keys, queries, CONTRACT_LAST) * scale, -1e30)
        expo = jnp.exp(scores - jnp.max(scores, axis=0, keepdims=True))
        probs = expo * (1 / jnp.sum(expo, axis=0, keepdims=True))
        prob_grad = dot(values, out_grad, CONTRACT_LAST)
        inner = jnp.sum(probs * prob_grad, axis=0, keepdims=True)
        score_grad = (probs * (prob_grad - inner) * scale).astype(jnp.bfloat16)
        grads[:, columns] = dot(score_grad, keys, CONTRACT_FIRST).astype(jnp.bfloat16)
        key_term = dot(score_grad, queries)
        value_term = dot(probs.astype(jnp.bfloat16), out_grad)
        key_total = key_term if head == 0 else key_total + key_term
        value_total = value_term if head == 0 else value_total + value_term
    if partial is None:
        grads[:, width : width + HD] = key_total.astype(jnp.bfloat16)
        grads[:, width + HD :] = value_total.astype(jnp.bfloat16)
    else:
        partial[:, :HD] = key_total
        partial[:, HD:] = value_total


def attention(place, lengths, own, sent, rows, width, split):
    length = own.shape[0]
    outs = [shaped((length, width if split else width + 2 * HD))]
    if split:
        outs.append(shaped((length, 2 * HD), jnp.float32))

    def kernel(*refs):
        attention_kernel(rows, width // HD, *(refs if split else (*refs, None)))

    return call(
        kernel,
        outs,
        [own, sent],
        [place, lengths],
        flops=10 * length * length * width,
    )


def weight_kernel(first, block, pair, own, other, *outs):
    length = own.shape[0]
    tile = min(block, 256)
    for number, out in enumerate(outs):
        for part in range(block // tile):
            start = (first + number) * block + part * tile
            out[part * tile : (part + 1) * tile] = (
                dot(pair[:length, start : start + tile], own[...], CONTRACT_FIRST)
                + dot(pair[length:, start : start + tile], other[...], CONTRACT_FIRST)
            ).astype(jnp.bfloat16)


def weight_terms(pair, own, other, first, count, block):
    return call(
        functools.partial(weight_kernel, first, block),
        [shaped((block, own.shape[1]))] * count,
        [pair, own, other],
        flops=2 * pair.shape[0] * block * count * own.shape[1],
    )


def row_kernel(weights, own, other, *refs):
    weight_refs, outs = refs[:weights], refs[weights:]
    length = own.shape[0]
    rows = length // len(outs)
    start = 0
    for weight in weight_refs:
        tile = min(weight.shape[0], 256)
        for part in range(weight.shape[0] // tile):
            right = weight[part * tile : (part + 1) * tile]
            for offset, left in ((0, own), (rows, other)):
                term = dot(left[...], right, CONTRACT_LAST).astype(jnp.bfloat16)
                for k, out in enumerate(outs):
                    out[offset : offset + rows, start : start + tile] = term[
                        k * rows : (k + 1) * rows
                    ]
            start += tile


def row_terms(own, other, weights, size):
    length, width = own.shape
    half = sum(weight.shape[0] for weight in weights)
    moved = sum(2 * weight.shape[0] * width for weight in weights) + 4 * length * (width + half)
    if width % 128 == 0:
        specs = [pl.BlockSpec((weight.shape[0], width), lambda i: (0, 0)) for weight in weights]
    else:
        weights = [weight[:, :width] for weight in weights]
        specs = [pl.BlockSpec(weight.shape, lambda i: (0, 0)) for weight in weights]
    part = (2 * length // size, half)
    return pl.pallas_call(
        functools.partial(row_kernel, len(weights)),
        grid=(1,),
        out_shape=[shaped(part)] * size,
        in_specs=[pl.BlockSpec(own.shape, lambda i: (0, 0))] * 2 + specs,
        out_specs=[pl.BlockSpec(part, lambda i: (0, 0))] * size,
        compiler_params=pltpu.CompilerParams(vmem_limit_bytes=24 * 2**20),
        cost_estimate=pl.CostEstimate(
            flops=4 * length * width * half, bytes_accessed=moved, transcendentals=0
        ),
    )(own, other, *weights)


def finish_kernel(count, share, *refs):
    total = refs[0][...].astype(jnp.float32)
    for part in refs[1:count]:
        total = total + part[...].astype(jnp.float32)
    total = total * share
    query_out, kv_out = refs[count:]
    width = query_out.shape[1]
    query_out[...] = total[:, :width]
    kv_out[...] = total[:, width:]


def finish(parts, query_width, share):
    block, width = parts[0].shape
    step = min(block, 128)

    def spec(columns):
        return pl.BlockSpec((step, columns), lambda i: (i, 0))

    return pl.pallas_call(
        functools.partial(finish_kernel, len(parts), share),
        grid=(block // step,),
        out_shape=[
            shaped((block, query_width), jnp.float32),
            shaped((block, width - query_width), jnp.float32),
        ],
        in_specs=[spec(width)] * len(parts),
        out_specs=[spec(query_width), spec(width - query_width)],
        compiler_params=pltpu.CompilerParams(vmem_limit_bytes=32 * 2**20),
        cost_estimate=pl.CostEstimate(
            flops=0, bytes_accessed=(2 * len(parts) + 4) * block * width, transcendentals=0
        ),
    )(*parts)


def input_kernel(count, block, place, tokens, gain, grad_out, handed, *refs):
    parts, out, gathered = refs[:count], refs[count], refs[count + 1]
    rows = tokens.shape[0]
    core = place[1]
    total = parts[0][:rows].astype(jnp.float32)
    for part in parts[1:]:
        total = total + part[:rows].astype(jnp.float32)
    for k in range(total.shape[1] // block):
        columns = slice(k * block, (k + 1) * block)
        gathered[:, pl.ds(column_start(place, k, core, block), block)] = total[:, columns]
        gathered[:, pl.ds(column_start(place, k, 1 - core, block), block)] = handed[
            :, columns
        ].astype(jnp.float32)
    values = tokens[...].astype(jnp.float32)
    root_mean = jnp.sqrt(jnp.mean(values * values, axis=-1, keepdims=True) + epsilon)
    unit = values / root_mean
    scaled = gathered[...] * gain[...].astype(jnp.float32)
    correction = unit * jnp.mean(scaled * unit, axis=-1, keepdims=True)
    out[...] = (grad_out[...].astype(jnp.float32) + (scaled - correction) / root_mean).astype(
        jnp.bfloat16
    )


def local(tokens, norm_gain, query_weight, kv_weight, out_weight, grad_out, doc_lengths):
    tensor_size = lax.axis_size("tensor")
    data_size = lax.axis_size("dp")
    tensor_index = lax.axis_index("tensor")
    data_index = lax.axis_index("dp")
    chips = data_size // 2
    place = jnp.stack([data_index >> 1, data_index & 1, tensor_index]).astype(jnp.int32)
    sharers = tensor_size // KVH
    levels = sharers.bit_length() - 1
    rows, width = tokens.shape
    block = width // data_size
    query_width = query_weight.shape[1]
    gain = norm_gain.reshape(1, width)

    grad_keep, normed_keep, send = call(
        functools.partial(prepare_kernel, block),
        [shaped((rows, width // 2))] * 2 + [shaped((2 * rows, width // 2))],
        [grad_out, tokens, gain],
        [place],
        [pltpu.VMEM((rows, width), jnp.bfloat16)],
    )
    joint_width = query_width + kv_weight.shape[1]
    send, out_weight, query_weight, kv_weight = tied(send, out_weight, query_weight, kv_weight)
    sent = swap(send, "dp", 1)
    (merged,) = call(
        merge_kernel,
        [shaped((block, joint_width + out_weight.shape[0]))],
        [query_weight, kv_weight, out_weight],
    )
    early, late = gather_chips(merged)
    row_pieces = gather_tensor(jnp.concatenate([grad_keep, sent[:rows]], axis=0))
    row_pieces += gather_tensor(jnp.concatenate([normed_keep, sent[rows:]], axis=0))
    own, sent, normed = project(place, row_pieces, early, late, tensor_size, joint_width)
    sent = swap(sent, "dp", 1)
    if levels:
        joined = (own + sent.astype(jnp.float32)).astype(jnp.bfloat16)
        keyvals = joined[:, query_width:joint_width]
        for bit_index in range(levels):
            partner = swap(keyvals, "tensor", 2**bit_index)
            upper = tensor_index >> bit_index & 1 == 1
            keyvals = jnp.concatenate(
                [jnp.where(upper, partner, keyvals), jnp.where(upper, keyvals, partner)], axis=1
            )
        own = jnp.concatenate(
            [joined[:, :query_width], keyvals, joined[:, joint_width:]], axis=1
        ).astype(jnp.float32)
        sent = jnp.zeros(own.shape, jnp.bfloat16)
    combined, *partial = attention(place, doc_lengths, own, sent, rows, query_width, levels > 0)
    if levels:
        kv_partial = partial[0]
        for bit_index in reversed(range(levels)):
            half_cols = kv_partial.shape[1] // 2
            upper = tensor_index >> bit_index & 1 == 1
            lower_cols = kv_partial[:, :half_cols]
            higher_cols = kv_partial[:, half_cols:]
            kept = jnp.where(upper, higher_cols, lower_cols)
            handed = jnp.where(upper, lower_cols, higher_cols)
            kv_partial = kept + swap(handed.astype(jnp.bfloat16), "tensor", 2**bit_index).astype(
                jnp.float32
            )
        combined = jnp.concatenate([combined, kv_partial.astype(jnp.bfloat16)], axis=1)
    other = swap(combined, "dp", 1)

    far = weight_terms(normed, combined, other, chips - 1, 1, block)
    near = weight_terms(normed, combined, other, 0, chips - 1, block)
    row_parts = scatter_tensor(row_terms(combined, other, early + late, tensor_size))
    weight_parts = scatter_chips([*near, *far])
    handed = sum(part[rows:].astype(jnp.float32) for part in row_parts).astype(jnp.bfloat16)
    handed = swap(handed, "dp", 1)
    query_grad, kv_grad = finish(weight_parts, query_width, 1 / data_size)
    handed, query_grad, kv_grad = tied(handed, query_grad, kv_grad)
    (input_grad,) = call(
        functools.partial(input_kernel, len(row_parts), block),
        [shaped((rows, width))],
        [tokens, gain, grad_out, handed, *row_parts],
        [place],
        [pltpu.VMEM((rows, width), jnp.float32)],
    )
    return (input_grad, query_grad, kv_grad)


def solution(mesh):
    placed = (
        P(("dp", "tensor"), None),
        P(),
        P("dp", "tensor"),
        P("dp", "tensor"),
        P("tensor", "dp"),
        P(("dp", "tensor"), None),
        P("dp", None),
    )
    return jax.shard_map(
        local,
        mesh=mesh,
        in_specs=placed,
        out_specs=(P(("dp", "tensor"), None), P("dp", "tensor"), P("dp", "tensor")),
        check_vma=False,
    )
```

```python
import functools
import math

import jax
import jax.numpy as jnp
from jax import lax
from jax.experimental import pallas as pl
from jax.experimental.pallas import tpu as pltpu
from jax.sharding import PartitionSpec as P

KVH = 4
HD = 128

epsilon = 1e-05
CONTRACT_LAST = (((1,), (1,)), ((), ()))
CONTRACT_FIRST = (((0,), (0,)), ((), ()))
WHOLE = pl.BlockSpec(memory_space=pltpu.VMEM)
SCALARS = pl.BlockSpec(memory_space=pltpu.SMEM)


def call(kernel, outs, operands, scalars=(), scratch=(), flops=0, megabytes=24):
    moved = sum(math.prod(a.shape) * a.dtype.itemsize for a in (*operands, *outs))
    return pl.pallas_call(
        kernel,
        out_shape=outs,
        in_specs=[SCALARS] * len(scalars) + [WHOLE] * len(operands),
        out_specs=[WHOLE] * len(outs),
        scratch_shapes=scratch,
        compiler_params=pltpu.CompilerParams(vmem_limit_bytes=megabytes * 2**20),
        cost_estimate=pl.CostEstimate(flops=flops, bytes_accessed=moved, transcendentals=0),
    )(*scalars, *operands)


def shaped(shape, dtype=jnp.bfloat16):
    return jax.ShapeDtypeStruct(shape, dtype)


def dot(left, right, contract=(((1,), (0,)), ((), ()))):
    return lax.dot_general(left, right, contract, preferred_element_type=jnp.float32)


def swap(value, axis, mask):
    pairs = [(source, source ^ mask) for source in range(lax.axis_size(axis))]
    return lax.ppermute(value, axis, pairs)


def tied(*values):
    return lax.optimization_barrier(values)


def everyone(value, axis, unit):
    size = lax.axis_size(axis) // unit
    return [value] + [swap(value, axis, unit * k) for k in range(1, size)]


def gather_near(value):
    if lax.axis_size("dp") != 8:
        return everyone(value, "dp", 2), []
    half = value.shape[0] // 2
    near_x = swap(value, "dp", 2)
    near_y = swap(value, "dp", 4)
    near_x, near_y = tied(near_x, near_y)
    return [value, near_x, near_y], [near_x[:half], near_y[half:]]


def gather_far(parts):
    return [swap(part, "dp", mask) for part, mask in zip(parts, (4, 2))]


def along(value, pairs):
    return lax.ppermute(value, "tensor", pairs)


def gather_tensor(value, after=()):
    if lax.axis_size("tensor") != 4:
        return everyone(value, "tensor", 1)
    right_one = along(value, [(0, 1), (1, 2), (2, 3)])
    left_one = along(value, [(1, 0), (2, 1), (3, 2)])
    right_one, left_one = tied(right_one, left_one)
    right_two = along(right_one, [(1, 2), (2, 3)])
    left_two = along(left_one, [(1, 0), (2, 1)])
    right_two, left_two, *_ = tied(right_two, left_two, *after)
    last = along(
        jnp.where(lax.axis_index("tensor") == 1, left_two, right_two), [(1, 0), (2, 3)]
    )
    return [value, right_one, left_one, right_two, left_two, last]


def pick(index, pieces, size, k, rows):
    if len(pieces) == size:
        return pieces[k][rows]
    own, right_one, left_one, right_two, left_two, last = [piece.at[rows] for piece in pieces]
    if k == 0:
        return own[...]
    if k == 1:
        return jnp.where(index % 2 == 1, right_one[...], left_one[...])
    if k == 2:
        return jnp.where(index >= 2, right_two[...], left_two[...])
    near = jnp.where(index == 1, left_one[...], right_one[...])
    return jnp.where(jnp.logical_or(index == 0, index == 3), last[...], near)


def inner_pair(value):
    return along(value, [(1, 2), (2, 1)])


def outer_pair(value):
    return along(value, [(3, 2), (0, 1)])


def scatter_chips(blocks):
    if len(blocks) != 4:
        return [blocks[0]] + [swap(blocks[k], "dp", 2 * k) for k in range(1, len(blocks))]
    half = blocks[0].shape[0] // 2
    far_top = swap(blocks[3][:half], "dp", 4)
    far_bottom = swap(blocks[3][half:], "dp", 2)
    near_x = swap(
        jnp.concatenate([blocks[1][:half] + far_top, blocks[1][half:]], axis=0), "dp", 2
    )
    near_y = swap(
        jnp.concatenate([blocks[2][:half], blocks[2][half:] + far_bottom], axis=0), "dp", 4
    )
    return [blocks[0], near_x, near_y]


def scatter_tensor(blocks):
    if len(blocks) != 4:
        return [blocks[0]] + [swap(blocks[k], "tensor", k) for k in range(1, len(blocks))]
    outer, inner = outer_pair(blocks[3]), inner_pair(blocks[3])
    outer, inner = tied(outer, inner)
    carried, adjacent = tied(blocks[2] + outer, blocks[1])
    two, one = swap(carried, "tensor", 2), swap(adjacent, "tensor", 1)
    return [blocks[0], one, inner, two]


def column_start(place, k, which, block):
    return pl.multiple_of(((place[0] ^ k) * 2 + which) * block, 128)


def prepare_kernel(block, place, grad_out, tokens, gain, grad_keep, normed_keep, send, normed):
    rows, core = tokens.shape[0], place[1]
    values = tokens[...].astype(jnp.float32)
    root_mean = jnp.sqrt(jnp.mean(values * values, axis=-1, keepdims=True) + epsilon)
    normed[...] = (values / root_mean * gain[...].astype(jnp.float32)).astype(jnp.bfloat16)
    for start, source, keep in ((0, grad_out, grad_keep), (rows, normed, normed_keep)):
        for k in range(keep.shape[1] // block):
            columns = slice(k * block, (k + 1) * block)
            keep[:, columns] = source[:, pl.ds(column_start(place, k, core, block), block)]
            send[start : start + rows, columns] = source[
                :, pl.ds(column_start(place, k, 1 - core, block), block)
            ]


def merge_kernel(query_weight, kv_weight, out_weight, merged):
    block, start = merged.shape[0], 0
    parts = [query_weight, kv_weight]
    parts += [out_weight.at[k : k + block] for k in range(0, out_weight.shape[0], block)]
    for part in parts:
        merged[:, start : start + part.shape[1]] = part[...]
        start += part.shape[1]


def products(grads, normed, weights, first, joint_width, block, columns):
    size = weights[0].shape[0]
    if columns < joint_width:
        width = min(256, joint_width - columns)
        total = None
        for k, weight in enumerate(weights):
            left = normed[:, first + k * size : first + (k + 1) * size]
            term = dot(left, weight[:, columns : columns + width])
            total = term if total is None else total + term
        yield slice(columns, columns + width), total
        return
    for row in range(0, block, min(size, 256)):
        place_out = slice(columns + row, columns + row + min(size, 256))
        total = None
        if size == block:
            for k, weight in enumerate(weights):
                right = weight[row : row + min(size, 256), columns : columns + block]
                left = grads[:, first + k * block : first + (k + 1) * block]
                term = dot(left, right, CONTRACT_LAST)
                total = term if total is None else total + term
        else:
            right = weights[row // size][:, columns : columns + block]
            total = dot(grads[:, first : first + block], right, CONTRACT_LAST)
        yield place_out, total


def column_steps(joint_width, width, block):
    return [*range(0, joint_width, 256), *range(joint_width, width, block)]


def early_kernel(pieces, weights, size, joint_width, place, *refs):
    row_refs, weight_refs = refs[:pieces], refs[pieces : pieces + weights]
    total, grads, normed = refs[pieces + weights :]
    rows = row_refs[0].shape[0] // 2
    block = weight_refs[0].shape[0]
    halves = row_refs[: pieces // 2], row_refs[pieces // 2 :]
    for pair, gathered in zip((grads, normed), halves):
        for core in range(2):
            for k in range(size):
                target = (core * size + k) * rows
                pair[target : target + rows] = pick(
                    place[2], gathered, size, k, slice(core * rows, (core + 1) * rows)
                )
    for columns in column_steps(joint_width, total.shape[1], block):
        for place_out, value in products(grads, normed, weight_refs, 0, joint_width, block, columns):
            total[:, place_out] = value


def late_kernel(first, joint_width, block, total, grads, normed, *refs):
    weight_refs, (keep, send) = refs[:-2], refs[-2:]
    length = keep.shape[0]
    if not weight_refs:
        keep[...] = total[:length]
        send[...] = total[length:].astype(jnp.bfloat16)
    for columns in column_steps(joint_width, keep.shape[1], block) if weight_refs else []:
        for place_out, value in products(
            grads, normed, weight_refs, first, joint_width, block, columns
        ):
            keep[:, place_out] = total[:length, place_out] + value[:length]
            send[:, place_out] = (total[length:, place_out] + value[length:]).astype(jnp.bfloat16)


def project(place, pieces, early, late, size, joint_width):
    rows = pieces[0].shape[0] // 2 * size
    half = pieces[0].shape[1]
    block, width = early[0].shape
    first = len(early) * block
    total, grads, normed = call(
        functools.partial(early_kernel, len(pieces), len(early), size, joint_width),
        [shaped((2 * rows, width), jnp.float32)] + [shaped((2 * rows, half))] * 2,
        [*pieces, *early],
        [place],
        flops=4 * rows * first * width,
        megabytes=24,
    )
    own, sent = call(
        functools.partial(late_kernel, first, joint_width, block),
        [shaped((rows, width), jnp.float32), shaped((rows, width))],
        [total, grads, normed, *late],
        flops=4 * rows * (half - first) * width,
        megabytes=24,
    )
    return own, sent, normed


def attention_kernel(rows, heads, place, lengths, own, sent, grads, partial):
    length = own.shape[0]
    width = heads * HD
    scale = 1 / math.sqrt(HD)
    tensor_index = place[2]

    def positions_of(dimension):
        order = lax.broadcasted_iota(jnp.int32, (length, length), dimension)
        return ((order // rows) ^ tensor_index) * rows + order % rows

    def labels_of(positions):
        labels, end = jnp.zeros((length, length), jnp.int32), 0
        for document in range(lengths.shape[1]):
            end = end + lengths[0, document]
            labels = labels + (end <= positions).astype(jnp.int32)
        return labels

    key_positions, query_positions = positions_of(0), positions_of(1)
    allowed = jnp.logical_and(
        labels_of(key_positions) == labels_of(query_positions), key_positions <= query_positions
    )

    def joined(first, second, columns):
        return (first[:, columns] + second[:, columns].astype(jnp.float32)).astype(jnp.bfloat16)

    keys = joined(own, sent, slice(width, width + HD))
    values = joined(own, sent, slice(width + HD, width + 2 * HD))
    key_total = value_total = None
    for head in range(heads):
        columns = slice(head * HD, (head + 1) * HD)
        start = width + 2 * HD + head * HD
        queries = joined(own, sent, columns)
        out_grad = joined(own, sent, slice(start, start + HD))
        scores = jnp.where(allowed, dot(keys, queries, CONTRACT_LAST) * scale, -1e30)
        expo = jnp.exp(scores - jnp.max(scores, axis=0, keepdims=True))
        probs = expo * (1 / jnp.sum(expo, axis=0, keepdims=True))
        prob_grad = dot(values, out_grad, CONTRACT_LAST)
        inner = jnp.sum(probs * prob_grad, axis=0, keepdims=True)
        score_grad = (probs * (prob_grad - inner) * scale).astype(jnp.bfloat16)
        grads[:, columns] = dot(score_grad, keys, CONTRACT_FIRST).astype(jnp.bfloat16)
        key_term = dot(score_grad, queries)
        value_term = dot(probs.astype(jnp.bfloat16), out_grad)
        key_total = key_term if head == 0 else key_total + key_term
        value_total = value_term if head == 0 else value_total + value_term
    if partial is None:
        grads[:, width : width + HD] = key_total.astype(jnp.bfloat16)
        grads[:, width + HD :] = value_total.astype(jnp.bfloat16)
    else:
        partial[:, :HD] = key_total
        partial[:, HD:] = value_total


def attention(place, lengths, own, sent, rows, width, split):
    length = own.shape[0]
    outs = [shaped((length, width if split else width + 2 * HD))]
    if split:
        outs.append(shaped((length, 2 * HD), jnp.float32))

    def kernel(*refs):
        attention_kernel(rows, width // HD, *(refs if split else (*refs, None)))

    return call(
        kernel,
        outs,
        [own, sent],
        [place, lengths],
        flops=10 * length * length * width,
    )


def weight_kernel(first, block, pair, own, other, *outs):
    length = own.shape[0]
    tile = min(block, 256)
    for number, out in enumerate(outs):
        for part in range(block // tile):
            start = (first + number) * block + part * tile
            out[part * tile : (part + 1) * tile] = (
                dot(pair[:length, start : start + tile], own[...], CONTRACT_FIRST)
                + dot(pair[length:, start : start + tile], other[...], CONTRACT_FIRST)
            ).astype(jnp.bfloat16)


def weight_terms(pair, own, other, first, count, block):
    return call(
        functools.partial(weight_kernel, first, block),
        [shaped((block, own.shape[1]))] * count,
        [pair, own, other],
        flops=2 * pair.shape[0] * block * count * own.shape[1],
    )


def row_kernel(weights, own, other, *refs):
    weight_refs, outs = refs[:weights], refs[weights:]
    length = own.shape[0]
    rows = length // len(outs)
    start = 0
    for weight in weight_refs:
        tile = min(weight.shape[0], 256)
        for part in range(weight.shape[0] // tile):
            right = weight[part * tile : (part + 1) * tile]
            for offset, left in ((0, own), (rows, other)):
                term = dot(left[...], right, CONTRACT_LAST).astype(jnp.bfloat16)
                for k, out in enumerate(outs):
                    out[offset : offset + rows, start : start + tile] = term[
                        k * rows : (k + 1) * rows
                    ]
            start += tile


def row_terms(own, other, weights, size):
    length, width = own.shape
    half = sum(weight.shape[0] for weight in weights)
    moved = sum(2 * weight.shape[0] * width for weight in weights) + 4 * length * (width + half)
    if width % 128 == 0:
        specs = [pl.BlockSpec((weight.shape[0], width), lambda i: (0, 0)) for weight in weights]
    else:
        weights = [weight[:, :width] for weight in weights]
        specs = [pl.BlockSpec(weight.shape, lambda i: (0, 0)) for weight in weights]
    part = (2 * length // size, half)
    return pl.pallas_call(
        functools.partial(row_kernel, len(weights)),
        grid=(1,),
        out_shape=[shaped(part)] * size,
        in_specs=[pl.BlockSpec(own.shape, lambda i: (0, 0))] * 2 + specs,
        out_specs=[pl.BlockSpec(part, lambda i: (0, 0))] * size,
        compiler_params=pltpu.CompilerParams(vmem_limit_bytes=24 * 2**20),
        cost_estimate=pl.CostEstimate(
            flops=4 * length * width * half, bytes_accessed=moved, transcendentals=0
        ),
    )(own, other, *weights)


def finish_kernel(count, share, *refs):
    total = refs[0][...].astype(jnp.float32)
    for part in refs[1:count]:
        total = total + part[...].astype(jnp.float32)
    total = total * share
    query_out, kv_out = refs[count:]
    width = query_out.shape[1]
    query_out[...] = total[:, :width]
    kv_out[...] = total[:, width:]


def finish(parts, query_width, share):
    block, width = parts[0].shape
    step = min(block, 256)

    def spec(columns):
        return pl.BlockSpec((step, columns), lambda i: (i, 0))

    return pl.pallas_call(
        functools.partial(finish_kernel, len(parts), share),
        grid=(block // step,),
        out_shape=[
            shaped((block, query_width), jnp.float32),
            shaped((block, width - query_width), jnp.float32),
        ],
        in_specs=[spec(width)] * len(parts),
        out_specs=[spec(query_width), spec(width - query_width)],
        compiler_params=pltpu.CompilerParams(vmem_limit_bytes=32 * 2**20),
        cost_estimate=pl.CostEstimate(
            flops=0, bytes_accessed=(2 * len(parts) + 4) * block * width, transcendentals=0
        ),
    )(*parts)


def input_kernel(count, block, place, tokens, gain, grad_out, handed, *refs):
    parts, out, gathered = refs[:count], refs[count], refs[count + 1]
    rows = tokens.shape[0]
    core = place[1]
    total = parts[0][:rows].astype(jnp.float32)
    for part in parts[1:]:
        total = total + part[:rows].astype(jnp.float32)
    for k in range(total.shape[1] // block):
        columns = slice(k * block, (k + 1) * block)
        gathered[:, pl.ds(column_start(place, k, core, block), block)] = total[:, columns]
        gathered[:, pl.ds(column_start(place, k, 1 - core, block), block)] = handed[
            :, columns
        ].astype(jnp.float32)
    values = tokens[...].astype(jnp.float32)
    root_mean = jnp.sqrt(jnp.mean(values * values, axis=-1, keepdims=True) + epsilon)
    unit = values / root_mean
    scaled = gathered[...] * gain[...].astype(jnp.float32)
    correction = unit * jnp.mean(scaled * unit, axis=-1, keepdims=True)
    out[...] = (grad_out[...].astype(jnp.float32) + (scaled - correction) / root_mean).astype(
        jnp.bfloat16
    )


def local(tokens, norm_gain, query_weight, kv_weight, out_weight, grad_out, doc_lengths):
    tensor_size = lax.axis_size("tensor")
    data_size = lax.axis_size("dp")
    tensor_index = lax.axis_index("tensor")
    data_index = lax.axis_index("dp")
    chips = data_size // 2
    place = jnp.stack([data_index >> 1, data_index & 1, tensor_index]).astype(jnp.int32)
    sharers = tensor_size // KVH
    levels = sharers.bit_length() - 1
    rows, width = tokens.shape
    block = width // data_size
    query_width = query_weight.shape[1]
    gain = norm_gain.reshape(1, width)

    grad_keep, normed_keep, send = call(
        functools.partial(prepare_kernel, block),
        [shaped((rows, width // 2))] * 2 + [shaped((2 * rows, width // 2))],
        [grad_out, tokens, gain],
        [place],
        [pltpu.VMEM((rows, width), jnp.bfloat16)],
    )
    joint_width = query_width + kv_weight.shape[1]
    send, out_weight, query_weight, kv_weight = tied(send, out_weight, query_weight, kv_weight)
    sent = swap(send, "dp", 1)
    (merged,) = call(
        merge_kernel,
        [shaped((block, joint_width + out_weight.shape[0]))],
        [query_weight, kv_weight, out_weight],
    )
    early, parts = gather_near(merged)
    late = gather_far(parts)
    row_pieces = gather_tensor(jnp.concatenate([grad_keep, sent[:rows]], axis=0))
    row_pieces += gather_tensor(
        jnp.concatenate([normed_keep, sent[rows:]], axis=0), (*parts, *row_pieces[3:4])
    )
    own, sent, normed = project(place, row_pieces, early, late, tensor_size, joint_width)
    sent = swap(sent, "dp", 1)
    if levels:
        joined = (own + sent.astype(jnp.float32)).astype(jnp.bfloat16)
        keyvals = joined[:, query_width:joint_width]
        for bit_index in range(levels):
            partner = swap(keyvals, "tensor", 2**bit_index)
            upper = tensor_index >> bit_index & 1 == 1
            keyvals = jnp.concatenate(
                [jnp.where(upper, partner, keyvals), jnp.where(upper, keyvals, partner)], axis=1
            )
        own = jnp.concatenate(
            [joined[:, :query_width], keyvals, joined[:, joint_width:]], axis=1
        ).astype(jnp.float32)
        sent = jnp.zeros(own.shape, jnp.bfloat16)
    combined, *partial = attention(place, doc_lengths, own, sent, rows, query_width, levels > 0)
    if levels:
        kv_partial = partial[0]
        for bit_index in reversed(range(levels)):
            half_cols = kv_partial.shape[1] // 2
            upper = tensor_index >> bit_index & 1 == 1
            lower_cols = kv_partial[:, :half_cols]
            higher_cols = kv_partial[:, half_cols:]
            kept = jnp.where(upper, higher_cols, lower_cols)
            handed = jnp.where(upper, lower_cols, higher_cols)
            kv_partial = kept + swap(handed.astype(jnp.bfloat16), "tensor", 2**bit_index).astype(
                jnp.float32
            )
        combined = jnp.concatenate([combined, kv_partial.astype(jnp.bfloat16)], axis=1)
    other = swap(combined, "dp", 1)

    far = weight_terms(normed, combined, other, chips - 1, 1, block)
    near = weight_terms(normed, combined, other, 0, chips - 1, block)
    row_parts = scatter_tensor(row_terms(combined, other, early + late, tensor_size))
    weight_parts = scatter_chips([*near, *far])
    handed = sum(part[rows:].astype(jnp.float32) for part in row_parts).astype(jnp.bfloat16)
    handed = swap(handed, "dp", 1)
    query_grad, kv_grad = finish(weight_parts, query_width, 1 / data_size)
    handed, query_grad, kv_grad = tied(handed, query_grad, kv_grad)
    (input_grad,) = call(
        functools.partial(input_kernel, len(row_parts), block),
        [shaped((rows, width))],
        [tokens, gain, grad_out, handed, *row_parts],
        [place],
        [pltpu.VMEM((rows, width), jnp.float32)],
    )
    return (input_grad, query_grad, kv_grad)


def solution(mesh):
    placed = (
        P(("dp", "tensor"), None),
        P(),
        P("dp", "tensor"),
        P("dp", "tensor"),
        P("tensor", "dp"),
        P(("dp", "tensor"), None),
        P("dp", None),
    )
    return jax.shard_map(
        local,
        mesh=mesh,
        in_specs=placed,
        out_specs=(P(("dp", "tensor"), None), P("dp", "tensor"), P("dp", "tensor")),
        check_vma=False,
    )
```

```python
import functools
import math

import jax
import jax.numpy as jnp
from jax import lax
from jax.experimental import pallas as pl
from jax.experimental.pallas import tpu as pltpu
from jax.sharding import PartitionSpec as P

KVH = 4
HD = 128

epsilon = 1e-05
CONTRACT_LAST = (((1,), (1,)), ((), ()))
CONTRACT_FIRST = (((0,), (0,)), ((), ()))
WHOLE = pl.BlockSpec(memory_space=pltpu.VMEM)
SCALARS = pl.BlockSpec(memory_space=pltpu.SMEM)


def call(kernel, outs, operands, scalars=(), scratch=(), flops=0, megabytes=24):
    moved = sum(math.prod(a.shape) * a.dtype.itemsize for a in (*operands, *outs))
    return pl.pallas_call(
        kernel,
        out_shape=outs,
        in_specs=[SCALARS] * len(scalars) + [WHOLE] * len(operands),
        out_specs=[WHOLE] * len(outs),
        scratch_shapes=scratch,
        compiler_params=pltpu.CompilerParams(vmem_limit_bytes=megabytes * 2**20),
        cost_estimate=pl.CostEstimate(flops=flops, bytes_accessed=moved, transcendentals=0),
    )(*scalars, *operands)


def shaped(shape, dtype=jnp.bfloat16):
    return jax.ShapeDtypeStruct(shape, dtype)


def dot(left, right, contract=(((1,), (0,)), ((), ()))):
    return lax.dot_general(left, right, contract, preferred_element_type=jnp.float32)


def swap(value, axis, mask):
    pairs = [(source, source ^ mask) for source in range(lax.axis_size(axis))]
    return lax.ppermute(value, axis, pairs)


def tied(*values):
    return lax.optimization_barrier(values)


def everyone(value, axis, unit):
    size = lax.axis_size(axis) // unit
    return [value] + [swap(value, axis, unit * k) for k in range(1, size)]


def gather_near(value):
    if lax.axis_size("dp") != 8:
        return everyone(value, "dp", 2), []
    half = value.shape[0] // 2
    near_x = swap(value, "dp", 2)
    near_y = swap(value, "dp", 4)
    near_x, near_y = tied(near_x, near_y)
    return [value, near_x, near_y], [near_x[:half], near_y[half:]]


def gather_far(parts):
    return [swap(part, "dp", mask) for part, mask in zip(parts, (4, 2))]


def along(value, pairs):
    return lax.ppermute(value, "tensor", pairs)


def gather_tensor(value, after=()):
    if lax.axis_size("tensor") != 4:
        return everyone(value, "tensor", 1)
    right_one = along(value, [(0, 1), (1, 2), (2, 3)])
    left_one = along(value, [(1, 0), (2, 1), (3, 2)])
    right_one, left_one = tied(right_one, left_one)
    right_two = along(right_one, [(1, 2), (2, 3)])
    left_two = along(left_one, [(1, 0), (2, 1)])
    right_two, left_two, *_ = tied(right_two, left_two, *after)
    last = along(
        jnp.where(lax.axis_index("tensor") == 1, left_two, right_two), [(1, 0), (2, 3)]
    )
    return [value, right_one, left_one, right_two, left_two, last]


def pick(index, pieces, size, k, rows):
    if len(pieces) == size:
        return pieces[k][rows]
    own, right_one, left_one, right_two, left_two, last = [piece.at[rows] for piece in pieces]
    if k == 0:
        return own[...]
    if k == 1:
        return jnp.where(index % 2 == 1, right_one[...], left_one[...])
    if k == 2:
        return jnp.where(index >= 2, right_two[...], left_two[...])
    near = jnp.where(index == 1, left_one[...], right_one[...])
    return jnp.where(jnp.logical_or(index == 0, index == 3), last[...], near)


def inner_pair(value):
    return along(value, [(1, 2), (2, 1)])


def outer_pair(value):
    return along(value, [(3, 2), (0, 1)])


def scatter_chips(blocks):
    if len(blocks) != 4:
        return [blocks[0]] + [swap(blocks[k], "dp", 2 * k) for k in range(1, len(blocks))]
    half = blocks[0].shape[0] // 2
    far_top = swap(blocks[3][:half], "dp", 4)
    far_bottom = swap(blocks[3][half:], "dp", 2)
    near_x = swap(
        jnp.concatenate([blocks[1][:half] + far_top, blocks[1][half:]], axis=0), "dp", 2
    )
    near_y = swap(
        jnp.concatenate([blocks[2][:half], blocks[2][half:] + far_bottom], axis=0), "dp", 4
    )
    return [blocks[0], near_x, near_y]


def scatter_tensor(blocks):
    if len(blocks) != 4:
        return [blocks[0]] + [swap(blocks[k], "tensor", k) for k in range(1, len(blocks))]
    outer, inner = outer_pair(blocks[3]), inner_pair(blocks[3])
    outer, inner = tied(outer, inner)
    carried, adjacent = tied(blocks[2] + outer, blocks[1])
    two, one = swap(carried, "tensor", 2), swap(adjacent, "tensor", 1)
    return [blocks[0], one, inner, two]


def column_start(place, k, which, block):
    return pl.multiple_of(((place[0] ^ k) * 2 + which) * block, 128)


def prepare_kernel(block, place, grad_out, tokens, gain, grad_keep, normed_keep, send, normed):
    rows, core = tokens.shape[0], place[1]
    values = tokens[...].astype(jnp.float32)
    root_mean = jnp.sqrt(jnp.mean(values * values, axis=-1, keepdims=True) + epsilon)
    normed[...] = (values / root_mean * gain[...].astype(jnp.float32)).astype(jnp.bfloat16)
    for start, source, keep in ((0, grad_out, grad_keep), (rows, normed, normed_keep)):
        for k in range(keep.shape[1] // block):
            columns = slice(k * block, (k + 1) * block)
            keep[:, columns] = source[:, pl.ds(column_start(place, k, core, block), block)]
            send[start : start + rows, columns] = source[
                :, pl.ds(column_start(place, k, 1 - core, block), block)
            ]


def merge_kernel(query_weight, kv_weight, out_weight, merged):
    block, start = merged.shape[0], 0
    parts = [query_weight, kv_weight]
    parts += [out_weight.at[k : k + block] for k in range(0, out_weight.shape[0], block)]
    for part in parts:
        merged[:, start : start + part.shape[1]] = part[...]
        start += part.shape[1]


def products(grads, normed, weights, first, joint_width, block, columns):
    size = weights[0].shape[0]
    if columns < joint_width:
        width = min(256, joint_width - columns)
        total = None
        for k, weight in enumerate(weights):
            left = normed[:, first + k * size : first + (k + 1) * size]
            term = dot(left, weight[:, columns : columns + width])
            total = term if total is None else total + term
        yield slice(columns, columns + width), total
        return
    for row in range(0, block, min(size, 256)):
        place_out = slice(columns + row, columns + row + min(size, 256))
        total = None
        if size == block:
            for k, weight in enumerate(weights):
                right = weight[row : row + min(size, 256), columns : columns + block]
                left = grads[:, first + k * block : first + (k + 1) * block]
                term = dot(left, right, CONTRACT_LAST)
                total = term if total is None else total + term
        else:
            right = weights[row // size][:, columns : columns + block]
            total = dot(grads[:, first : first + block], right, CONTRACT_LAST)
        yield place_out, total


def column_steps(joint_width, width, block):
    return [*range(0, joint_width, 256), *range(joint_width, width, block)]


def early_kernel(pieces, weights, size, joint_width, outward, place, *refs):
    row_refs, weight_refs = refs[:pieces], refs[pieces : pieces + weights]
    total, pair = refs[pieces + weights :]
    rows = row_refs[0].shape[0] // 2
    block, width = weight_refs[0].shape
    for core in range(2):
        for k in range(size):
            target = (core * size + k) * rows
            pair[target : target + rows] = pick(
                place[2], row_refs, size, k, slice(core * rows, (core + 1) * rows)
            )
    base = joint_width if outward else 0
    for columns in range(joint_width, width, block) if outward else range(0, joint_width, 256):
        for place_out, value in products(pair, pair, weight_refs, 0, joint_width, block, columns):
            total[:, place_out.start - base : place_out.stop - base] = value


def late_kernel(first, joint_width, block, joint_total, out_total, grads, normed, *refs):
    weight_refs, (keep, send) = refs[:-2], refs[-2:]
    length = keep.shape[0]
    for total, base in ((joint_total, 0), (out_total, joint_width)):
        if not weight_refs:
            columns = slice(base, base + total.shape[1])
            keep[:, columns] = total[:length]
            send[:, columns] = total[length:].astype(jnp.bfloat16)
    for columns in column_steps(joint_width, keep.shape[1], block) if weight_refs else []:
        total, base = (joint_total, 0) if columns < joint_width else (out_total, joint_width)
        for place_out, value in products(
            grads, normed, weight_refs, first, joint_width, block, columns
        ):
            value = value + total[:, place_out.start - base : place_out.stop - base]
            keep[:, place_out] = value[:length]
            send[:, place_out] = value[length:].astype(jnp.bfloat16)


def project(place, grad_pieces, normed_pieces, early, late, size, joint_width):
    pair_rows, half = grad_pieces[0].shape
    rows = pair_rows // 2 * size
    block, width = early[0].shape
    first = len(early) * block
    totals, pairs = [], []
    for pieces, outward in ((normed_pieces, False), (grad_pieces, True)):
        columns = width - joint_width if outward else joint_width
        total, pair = call(
            functools.partial(
                early_kernel, len(pieces), len(early), size, joint_width, outward
            ),
            [shaped((2 * rows, columns), jnp.float32), shaped((2 * rows, half))],
            [*pieces, *early],
            [place],
            flops=4 * rows * first * columns,
        )
        totals.append(total)
        pairs.append(pair)
    normed, grads = pairs
    own, sent = call(
        functools.partial(late_kernel, first, joint_width, block),
        [shaped((rows, width), jnp.float32), shaped((rows, width))],
        [*totals, grads, normed, *late],
        flops=4 * rows * (half - first) * width,
    )
    return own, sent, normed


def attention_kernel(rows, heads, place, lengths, own, sent, grads, partial):
    length = own.shape[0]
    width = heads * HD
    scale = 1 / math.sqrt(HD)
    tensor_index = place[2]

    def positions_of(dimension):
        order = lax.broadcasted_iota(jnp.int32, (length, length), dimension)
        return ((order // rows) ^ tensor_index) * rows + order % rows

    def labels_of(positions):
        labels, end = jnp.zeros((length, length), jnp.int32), 0
        for document in range(lengths.shape[1]):
            end = end + lengths[0, document]
            labels = labels + (end <= positions).astype(jnp.int32)
        return labels

    key_positions, query_positions = positions_of(0), positions_of(1)
    allowed = jnp.logical_and(
        labels_of(key_positions) == labels_of(query_positions), key_positions <= query_positions
    )

    def joined(first, second, columns):
        return (first[:, columns] + second[:, columns].astype(jnp.float32)).astype(jnp.bfloat16)

    keys = joined(own, sent, slice(width, width + HD))
    values = joined(own, sent, slice(width + HD, width + 2 * HD))
    key_total = value_total = None
    for head in range(heads):
        columns = slice(head * HD, (head + 1) * HD)
        start = width + 2 * HD + head * HD
        queries = joined(own, sent, columns)
        out_grad = joined(own, sent, slice(start, start + HD))
        scores = jnp.where(allowed, dot(keys, queries, CONTRACT_LAST) * scale, -1e30)
        expo = jnp.exp(scores - jnp.max(scores, axis=0, keepdims=True))
        probs = expo * (1 / jnp.sum(expo, axis=0, keepdims=True))
        prob_grad = dot(values, out_grad, CONTRACT_LAST)
        inner = jnp.sum(probs * prob_grad, axis=0, keepdims=True)
        score_grad = (probs * (prob_grad - inner) * scale).astype(jnp.bfloat16)
        grads[:, columns] = dot(score_grad, keys, CONTRACT_FIRST).astype(jnp.bfloat16)
        key_term = dot(score_grad, queries)
        value_term = dot(probs.astype(jnp.bfloat16), out_grad)
        key_total = key_term if head == 0 else key_total + key_term
        value_total = value_term if head == 0 else value_total + value_term
    if partial is None:
        grads[:, width : width + HD] = key_total.astype(jnp.bfloat16)
        grads[:, width + HD :] = value_total.astype(jnp.bfloat16)
    else:
        partial[:, :HD] = key_total
        partial[:, HD:] = value_total


def attention(place, lengths, own, sent, rows, width, split):
    length = own.shape[0]
    outs = [shaped((length, width if split else width + 2 * HD))]
    if split:
        outs.append(shaped((length, 2 * HD), jnp.float32))

    def kernel(*refs):
        attention_kernel(rows, width // HD, *(refs if split else (*refs, None)))

    return call(
        kernel,
        outs,
        [own, sent],
        [place, lengths],
        flops=10 * length * length * width,
    )


def weight_kernel(first, block, pair, own, other, *outs):
    length = own.shape[0]
    tile = min(block, 256)
    for number, out in enumerate(outs):
        for part in range(block // tile):
            start = (first + number) * block + part * tile
            out[part * tile : (part + 1) * tile] = (
                dot(pair[:length, start : start + tile], own[...], CONTRACT_FIRST)
                + dot(pair[length:, start : start + tile], other[...], CONTRACT_FIRST)
            ).astype(jnp.bfloat16)


def weight_terms(pair, own, other, first, count, block):
    return call(
        functools.partial(weight_kernel, first, block),
        [shaped((block, own.shape[1]))] * count,
        [pair, own, other],
        flops=2 * pair.shape[0] * block * count * own.shape[1],
    )


def row_kernel(weights, own, other, *refs):
    weight_refs, outs = refs[:weights], refs[weights:]
    length = own.shape[0]
    rows = length // len(outs)
    start = 0
    for weight in weight_refs:
        tile = min(weight.shape[0], 256)
        for part in range(weight.shape[0] // tile):
            right = weight[part * tile : (part + 1) * tile]
            for offset, left in ((0, own), (rows, other)):
                term = dot(left[...], right, CONTRACT_LAST).astype(jnp.bfloat16)
                for k, out in enumerate(outs):
                    out[offset : offset + rows, start : start + tile] = term[
                        k * rows : (k + 1) * rows
                    ]
            start += tile


def row_terms(own, other, weights, size):
    length, width = own.shape
    half = sum(weight.shape[0] for weight in weights)
    moved = sum(2 * weight.shape[0] * width for weight in weights) + 4 * length * (width + half)
    if width % 128 == 0:
        specs = [pl.BlockSpec((weight.shape[0], width), lambda i: (0, 0)) for weight in weights]
    else:
        weights = [weight[:, :width] for weight in weights]
        specs = [pl.BlockSpec(weight.shape, lambda i: (0, 0)) for weight in weights]
    part = (2 * length // size, half)
    return pl.pallas_call(
        functools.partial(row_kernel, len(weights)),
        grid=(1,),
        out_shape=[shaped(part)] * size,
        in_specs=[pl.BlockSpec(own.shape, lambda i: (0, 0))] * 2 + specs,
        out_specs=[pl.BlockSpec(part, lambda i: (0, 0))] * size,
        compiler_params=pltpu.CompilerParams(vmem_limit_bytes=24 * 2**20),
        cost_estimate=pl.CostEstimate(
            flops=4 * length * width * half, bytes_accessed=moved, transcendentals=0
        ),
    )(own, other, *weights)


def finish_kernel(count, share, *refs):
    total = refs[0][...].astype(jnp.float32)
    for part in refs[1:count]:
        total = total + part[...].astype(jnp.float32)
    total = total * share
    query_out, kv_out = refs[count:]
    width = query_out.shape[1]
    query_out[...] = total[:, :width]
    kv_out[...] = total[:, width:]


def finish(parts, query_width, share):
    block, width = parts[0].shape
    step = min(block, 256)

    def spec(columns):
        return pl.BlockSpec((step, columns), lambda i: (i, 0))

    return pl.pallas_call(
        functools.partial(finish_kernel, len(parts), share),
        grid=(block // step,),
        out_shape=[
            shaped((block, query_width), jnp.float32),
            shaped((block, width - query_width), jnp.float32),
        ],
        in_specs=[spec(width)] * len(parts),
        out_specs=[spec(query_width), spec(width - query_width)],
        compiler_params=pltpu.CompilerParams(vmem_limit_bytes=32 * 2**20),
        cost_estimate=pl.CostEstimate(
            flops=0, bytes_accessed=(2 * len(parts) + 4) * block * width, transcendentals=0
        ),
    )(*parts)


def input_kernel(count, block, place, tokens, gain, grad_out, handed, *refs):
    parts, out, gathered = refs[:count], refs[count], refs[count + 1]
    rows = tokens.shape[0]
    core = place[1]
    total = parts[0][:rows].astype(jnp.float32)
    for part in parts[1:]:
        total = total + part[:rows].astype(jnp.float32)
    for k in range(total.shape[1] // block):
        columns = slice(k * block, (k + 1) * block)
        gathered[:, pl.ds(column_start(place, k, core, block), block)] = total[:, columns]
        gathered[:, pl.ds(column_start(place, k, 1 - core, block), block)] = handed[
            :, columns
        ].astype(jnp.float32)
    values = tokens[...].astype(jnp.float32)
    root_mean = jnp.sqrt(jnp.mean(values * values, axis=-1, keepdims=True) + epsilon)
    unit = values / root_mean
    scaled = gathered[...] * gain[...].astype(jnp.float32)
    correction = unit * jnp.mean(scaled * unit, axis=-1, keepdims=True)
    out[...] = (grad_out[...].astype(jnp.float32) + (scaled - correction) / root_mean).astype(
        jnp.bfloat16
    )


def local(tokens, norm_gain, query_weight, kv_weight, out_weight, grad_out, doc_lengths):
    tensor_size = lax.axis_size("tensor")
    data_size = lax.axis_size("dp")
    tensor_index = lax.axis_index("tensor")
    data_index = lax.axis_index("dp")
    chips = data_size // 2
    place = jnp.stack([data_index >> 1, data_index & 1, tensor_index]).astype(jnp.int32)
    sharers = tensor_size // KVH
    levels = sharers.bit_length() - 1
    rows, width = tokens.shape
    block = width // data_size
    query_width = query_weight.shape[1]
    gain = norm_gain.reshape(1, width)

    grad_keep, normed_keep, send = call(
        functools.partial(prepare_kernel, block),
        [shaped((rows, width // 2))] * 2 + [shaped((2 * rows, width // 2))],
        [grad_out, tokens, gain],
        [place],
        [pltpu.VMEM((rows, width), jnp.bfloat16)],
    )
    joint_width = query_width + kv_weight.shape[1]
    send, out_weight, query_weight, kv_weight = tied(send, out_weight, query_weight, kv_weight)
    sent = swap(send, "dp", 1)
    (merged,) = call(
        merge_kernel,
        [shaped((block, joint_width + out_weight.shape[0]))],
        [query_weight, kv_weight, out_weight],
    )
    early, parts = gather_near(merged)
    late = gather_far(parts)
    grad_pieces = gather_tensor(jnp.concatenate([grad_keep, sent[:rows]], axis=0))
    normed_pieces = gather_tensor(
        jnp.concatenate([normed_keep, sent[rows:]], axis=0), (*parts, *grad_pieces[3:4])
    )
    own, sent, normed = project(
        place, grad_pieces, normed_pieces, early, late, tensor_size, joint_width
    )
    sent = swap(sent, "dp", 1)
    if levels:
        joined = (own + sent.astype(jnp.float32)).astype(jnp.bfloat16)
        keyvals = joined[:, query_width:joint_width]
        for bit_index in range(levels):
            partner = swap(keyvals, "tensor", 2**bit_index)
            upper = tensor_index >> bit_index & 1 == 1
            keyvals = jnp.concatenate(
                [jnp.where(upper, partner, keyvals), jnp.where(upper, keyvals, partner)], axis=1
            )
        own = jnp.concatenate(
            [joined[:, :query_width], keyvals, joined[:, joint_width:]], axis=1
        ).astype(jnp.float32)
        sent = jnp.zeros(own.shape, jnp.bfloat16)
    combined, *partial = attention(place, doc_lengths, own, sent, rows, query_width, levels > 0)
    if levels:
        kv_partial = partial[0]
        for bit_index in reversed(range(levels)):
            half_cols = kv_partial.shape[1] // 2
            upper = tensor_index >> bit_index & 1 == 1
            lower_cols = kv_partial[:, :half_cols]
            higher_cols = kv_partial[:, half_cols:]
            kept = jnp.where(upper, higher_cols, lower_cols)
            handed = jnp.where(upper, lower_cols, higher_cols)
            kv_partial = kept + swap(handed.astype(jnp.bfloat16), "tensor", 2**bit_index).astype(
                jnp.float32
            )
        combined = jnp.concatenate([combined, kv_partial.astype(jnp.bfloat16)], axis=1)
    other = swap(combined, "dp", 1)

    far = weight_terms(normed, combined, other, chips - 1, 1, block)
    near = weight_terms(normed, combined, other, 0, chips - 1, block)
    row_parts = scatter_tensor(row_terms(combined, other, early + late, tensor_size))
    weight_parts = scatter_chips([*near, *far])
    handed = sum(part[rows:].astype(jnp.float32) for part in row_parts).astype(jnp.bfloat16)
    handed = swap(handed, "dp", 1)
    query_grad, kv_grad = finish(weight_parts, query_width, 1 / data_size)
    handed, query_grad, kv_grad = tied(handed, query_grad, kv_grad)
    (input_grad,) = call(
        functools.partial(input_kernel, len(row_parts), block),
        [shaped((rows, width))],
        [tokens, gain, grad_out, handed, *row_parts],
        [place],
        [pltpu.VMEM((rows, width), jnp.float32)],
    )
    return (input_grad, query_grad, kv_grad)


def solution(mesh):
    placed = (
        P(("dp", "tensor"), None),
        P(),
        P("dp", "tensor"),
        P("dp", "tensor"),
        P("tensor", "dp"),
        P(("dp", "tensor"), None),
        P("dp", None),
    )
    return jax.shard_map(
        local,
        mesh=mesh,
        in_specs=placed,
        out_specs=(P(("dp", "tensor"), None), P("dp", "tensor"), P("dp", "tensor")),
        check_vma=False,
    )
```

```python
import functools
import math

import jax
import jax.numpy as jnp
from jax import lax
from jax.experimental import pallas as pl
from jax.experimental.pallas import tpu as pltpu
from jax.sharding import PartitionSpec as P

KVH = 4
HD = 128

epsilon = 1e-05
CONTRACT_LAST = (((1,), (1,)), ((), ()))
CONTRACT_FIRST = (((0,), (0,)), ((), ()))
WHOLE = pl.BlockSpec(memory_space=pltpu.VMEM)
SCALARS = pl.BlockSpec(memory_space=pltpu.SMEM)


def call(kernel, outs, operands, scalars=(), scratch=(), flops=0, megabytes=24):
    moved = sum(math.prod(a.shape) * a.dtype.itemsize for a in (*operands, *outs))
    return pl.pallas_call(
        kernel,
        out_shape=outs,
        in_specs=[SCALARS] * len(scalars) + [WHOLE] * len(operands),
        out_specs=[WHOLE] * len(outs),
        scratch_shapes=scratch,
        compiler_params=pltpu.CompilerParams(vmem_limit_bytes=megabytes * 2**20),
        cost_estimate=pl.CostEstimate(flops=flops, bytes_accessed=moved, transcendentals=0),
    )(*scalars, *operands)


def shaped(shape, dtype=jnp.bfloat16):
    return jax.ShapeDtypeStruct(shape, dtype)


def dot(left, right, contract=(((1,), (0,)), ((), ()))):
    return lax.dot_general(left, right, contract, preferred_element_type=jnp.float32)


def swap(value, axis, mask):
    pairs = [(source, source ^ mask) for source in range(lax.axis_size(axis))]
    return lax.ppermute(value, axis, pairs)


def tied(*values):
    return lax.optimization_barrier(values)


def everyone(value, axis, unit):
    size = lax.axis_size(axis) // unit
    return [value] + [swap(value, axis, unit * k) for k in range(1, size)]


def gather_near(value):
    if lax.axis_size("dp") != 8:
        return everyone(value, "dp", 2), []
    half = value.shape[0] // 2
    near_x = swap(value, "dp", 2)
    near_y = swap(value, "dp", 4)
    near_x, near_y = tied(near_x, near_y)
    return [value, near_x, near_y], [near_x[:half], near_y[half:]]


def gather_far(parts):
    return [swap(part, "dp", mask) for part, mask in zip(parts, (4, 2))]


def along(value, pairs):
    return lax.ppermute(value, "tensor", pairs)


def gather_tensor(value, after=()):
    if lax.axis_size("tensor") != 4:
        return everyone(value, "tensor", 1)
    right_one = along(value, [(0, 1), (1, 2), (2, 3)])
    left_one = along(value, [(1, 0), (2, 1), (3, 2)])
    right_one, left_one = tied(right_one, left_one)
    right_two = along(right_one, [(1, 2), (2, 3)])
    left_two = along(left_one, [(1, 0), (2, 1)])
    right_two, left_two, *_ = tied(right_two, left_two, *after)
    last = along(
        jnp.where(lax.axis_index("tensor") == 1, left_two, right_two), [(1, 0), (2, 3)]
    )
    return [value, right_one, left_one, right_two, left_two, last]


def pick(index, pieces, size, k, rows):
    if len(pieces) == size:
        return pieces[k][rows]
    own, right_one, left_one, right_two, left_two, last = [piece.at[rows] for piece in pieces]
    if k == 0:
        return own[...]
    if k == 1:
        return jnp.where(index % 2 == 1, right_one[...], left_one[...])
    if k == 2:
        return jnp.where(index >= 2, right_two[...], left_two[...])
    near = jnp.where(index == 1, left_one[...], right_one[...])
    return jnp.where(jnp.logical_or(index == 0, index == 3), last[...], near)


def inner_pair(value):
    return along(value, [(1, 2), (2, 1)])


def outer_pair(value):
    return along(value, [(3, 2), (0, 1)])


def scatter_chips(blocks):
    if len(blocks) != 4:
        return [blocks[0]] + [swap(blocks[k], "dp", 2 * k) for k in range(1, len(blocks))]
    half = blocks[0].shape[0] // 2
    far_top = swap(blocks[3][:half], "dp", 4)
    far_bottom = swap(blocks[3][half:], "dp", 2)
    near_x = swap(
        jnp.concatenate([blocks[1][:half] + far_top, blocks[1][half:]], axis=0), "dp", 2
    )
    near_y = swap(
        jnp.concatenate([blocks[2][:half], blocks[2][half:] + far_bottom], axis=0), "dp", 4
    )
    return [blocks[0], near_x, near_y]


def scatter_tensor(blocks):
    if len(blocks) != 4:
        return [blocks[0]] + [swap(blocks[k], "tensor", k) for k in range(1, len(blocks))]
    inner, outer = inner_pair(blocks[3]), outer_pair(blocks[3])
    inner, outer = tied(inner, outer)
    carried, adjacent = tied(blocks[2] + outer, blocks[1])
    two, one = swap(carried, "tensor", 2), swap(adjacent, "tensor", 1)
    return [blocks[0], one, inner, two]


def column_start(place, k, which, block):
    return pl.multiple_of(((place[0] ^ k) * 2 + which) * block, 128)


def prepare_kernel(block, place, grad_out, tokens, gain, grad_keep, normed_keep, send, normed):
    rows, core = tokens.shape[0], place[1]
    values = tokens[...].astype(jnp.float32)
    root_mean = jnp.sqrt(jnp.mean(values * values, axis=-1, keepdims=True) + epsilon)
    normed[...] = (values / root_mean * gain[...].astype(jnp.float32)).astype(jnp.bfloat16)
    for start, source, keep in ((0, grad_out, grad_keep), (rows, normed, normed_keep)):
        for k in range(keep.shape[1] // block):
            columns = slice(k * block, (k + 1) * block)
            keep[:, columns] = source[:, pl.ds(column_start(place, k, core, block), block)]
            send[start : start + rows, columns] = source[
                :, pl.ds(column_start(place, k, 1 - core, block), block)
            ]


def merge_kernel(query_weight, kv_weight, out_weight, merged):
    block, start = merged.shape[0], 0
    parts = [query_weight, kv_weight]
    parts += [out_weight.at[k : k + block] for k in range(0, out_weight.shape[0], block)]
    for part in parts:
        merged[:, start : start + part.shape[1]] = part[...]
        start += part.shape[1]


def products(grads, normed, weights, first, joint_width, block, columns):
    size = weights[0].shape[0]
    if columns < joint_width:
        width = min(256, joint_width - columns)
        total = None
        for k, weight in enumerate(weights):
            left = normed[:, first + k * size : first + (k + 1) * size]
            term = dot(left, weight[:, columns : columns + width])
            total = term if total is None else total + term
        yield slice(columns, columns + width), total
        return
    for row in range(0, block, min(size, 256)):
        place_out = slice(columns + row, columns + row + min(size, 256))
        total = None
        if size == block:
            for k, weight in enumerate(weights):
                right = weight[row : row + min(size, 256), columns : columns + block]
                left = grads[:, first + k * block : first + (k + 1) * block]
                term = dot(left, right, CONTRACT_LAST)
                total = term if total is None else total + term
        else:
            right = weights[row // size][:, columns : columns + block]
            total = dot(grads[:, first : first + block], right, CONTRACT_LAST)
        yield place_out, total


def column_steps(joint_width, width, block):
    return [*range(0, joint_width, 256), *range(joint_width, width, block)]


def early_kernel(pieces, weights, size, joint_width, outward, place, *refs):
    row_refs, weight_refs = refs[:pieces], refs[pieces : pieces + weights]
    total, pair = refs[pieces + weights :]
    rows = row_refs[0].shape[0] // 2
    block, width = weight_refs[0].shape
    for core in range(2):
        for k in range(size):
            target = (core * size + k) * rows
            pair[target : target + rows] = pick(
                place[2], row_refs, size, k, slice(core * rows, (core + 1) * rows)
            )
    base = joint_width if outward else 0
    for columns in range(joint_width, width, block) if outward else range(0, joint_width, 256):
        for place_out, value in products(pair, pair, weight_refs, 0, joint_width, block, columns):
            total[:, place_out.start - base : place_out.stop - base] = value


def late_kernel(first, joint_width, block, joint_total, out_total, grads, normed, *refs):
    weight_refs, (keep, send) = refs[:-2], refs[-2:]
    length = keep.shape[0]
    for total, base in ((joint_total, 0), (out_total, joint_width)):
        if not weight_refs:
            columns = slice(base, base + total.shape[1])
            keep[:, columns] = total[:length]
            send[:, columns] = total[length:].astype(jnp.bfloat16)
    for columns in column_steps(joint_width, keep.shape[1], block) if weight_refs else []:
        total, base = (joint_total, 0) if columns < joint_width else (out_total, joint_width)
        for place_out, value in products(
            grads, normed, weight_refs, first, joint_width, block, columns
        ):
            value = value + total[:, place_out.start - base : place_out.stop - base]
            keep[:, place_out] = value[:length]
            send[:, place_out] = value[length:].astype(jnp.bfloat16)


def project(place, grad_pieces, normed_pieces, early, late, size, joint_width):
    pair_rows, half = grad_pieces[0].shape
    rows = pair_rows // 2 * size
    block, width = early[0].shape
    first = len(early) * block
    totals, pairs = [], []
    for pieces, outward in ((normed_pieces, False), (grad_pieces, True)):
        columns = width - joint_width if outward else joint_width
        total, pair = call(
            functools.partial(
                early_kernel, len(pieces), len(early), size, joint_width, outward
            ),
            [shaped((2 * rows, columns), jnp.float32), shaped((2 * rows, half))],
            [*pieces, *early],
            [place],
            flops=4 * rows * first * columns,
        )
        totals.append(total)
        pairs.append(pair)
    normed, grads = pairs
    own, sent = call(
        functools.partial(late_kernel, first, joint_width, block),
        [shaped((rows, width), jnp.float32), shaped((rows, width))],
        [*totals, grads, normed, *late],
        flops=4 * rows * (half - first) * width,
    )
    return own, sent, normed


def attention_kernel(rows, heads, place, lengths, own, sent, grads, partial):
    length = own.shape[0]
    width = heads * HD
    scale = 1 / math.sqrt(HD)
    tensor_index = place[2]

    def positions_of(dimension):
        order = lax.broadcasted_iota(jnp.int32, (length, length), dimension)
        return ((order // rows) ^ tensor_index) * rows + order % rows

    def labels_of(positions):
        labels, end = jnp.zeros((length, length), jnp.int32), 0
        for document in range(lengths.shape[1]):
            end = end + lengths[0, document]
            labels = labels + (end <= positions).astype(jnp.int32)
        return labels

    key_positions, query_positions = positions_of(0), positions_of(1)
    allowed = jnp.logical_and(
        labels_of(key_positions) == labels_of(query_positions), key_positions <= query_positions
    )

    def joined(first, second, columns):
        return (first[:, columns] + second[:, columns].astype(jnp.float32)).astype(jnp.bfloat16)

    keys = joined(own, sent, slice(width, width + HD))
    values = joined(own, sent, slice(width + HD, width + 2 * HD))
    key_total = value_total = None
    for head in range(heads):
        columns = slice(head * HD, (head + 1) * HD)
        start = width + 2 * HD + head * HD
        queries = joined(own, sent, columns)
        out_grad = joined(own, sent, slice(start, start + HD))
        scores = jnp.where(allowed, dot(keys, queries, CONTRACT_LAST) * scale, -1e30)
        expo = jnp.exp(scores - jnp.max(scores, axis=0, keepdims=True))
        probs = expo * (1 / jnp.sum(expo, axis=0, keepdims=True))
        prob_grad = dot(values, out_grad, CONTRACT_LAST)
        inner = jnp.sum(probs * prob_grad, axis=0, keepdims=True)
        score_grad = (probs * (prob_grad - inner) * scale).astype(jnp.bfloat16)
        grads[:, columns] = dot(score_grad, keys, CONTRACT_FIRST).astype(jnp.bfloat16)
        key_term = dot(score_grad, queries)
        value_term = dot(probs.astype(jnp.bfloat16), out_grad)
        key_total = key_term if head == 0 else key_total + key_term
        value_total = value_term if head == 0 else value_total + value_term
    if partial is None:
        grads[:, width : width + HD] = key_total.astype(jnp.bfloat16)
        grads[:, width + HD :] = value_total.astype(jnp.bfloat16)
    else:
        partial[:, :HD] = key_total
        partial[:, HD:] = value_total


def attention(place, lengths, own, sent, rows, width, split):
    length = own.shape[0]
    outs = [shaped((length, width if split else width + 2 * HD))]
    if split:
        outs.append(shaped((length, 2 * HD), jnp.float32))

    def kernel(*refs):
        attention_kernel(rows, width // HD, *(refs if split else (*refs, None)))

    return call(
        kernel,
        outs,
        [own, sent],
        [place, lengths],
        flops=10 * length * length * width,
    )


def weight_kernel(first, block, pair, own, other, *outs):
    length = own.shape[0]
    tile = min(block, 256)
    for number, out in enumerate(outs):
        for part in range(block // tile):
            start = (first + number) * block + part * tile
            out[part * tile : (part + 1) * tile] = (
                dot(pair[:length, start : start + tile], own[...], CONTRACT_FIRST)
                + dot(pair[length:, start : start + tile], other[...], CONTRACT_FIRST)
            ).astype(jnp.bfloat16)


def weight_terms(pair, own, other, first, count, block):
    return call(
        functools.partial(weight_kernel, first, block),
        [shaped((block, own.shape[1]))] * count,
        [pair, own, other],
        flops=2 * pair.shape[0] * block * count * own.shape[1],
    )


def row_kernel(weights, own, other, *refs):
    weight_refs, outs = refs[:weights], refs[weights:]
    length = own.shape[0]
    rows = length // len(outs)
    start = 0
    for weight in weight_refs:
        tile = min(weight.shape[0], 256)
        for part in range(weight.shape[0] // tile):
            right = weight[part * tile : (part + 1) * tile]
            for offset, left in ((0, own), (rows, other)):
                term = dot(left[...], right, CONTRACT_LAST).astype(jnp.bfloat16)
                for k, out in enumerate(outs):
                    out[offset : offset + rows, start : start + tile] = term[
                        k * rows : (k + 1) * rows
                    ]
            start += tile


def row_terms(own, other, weights, size):
    length, width = own.shape
    half = sum(weight.shape[0] for weight in weights)
    moved = sum(2 * weight.shape[0] * width for weight in weights) + 4 * length * (width + half)
    if width % 128 == 0:
        specs = [pl.BlockSpec((weight.shape[0], width), lambda i: (0, 0)) for weight in weights]
    else:
        weights = [weight[:, :width] for weight in weights]
        specs = [pl.BlockSpec(weight.shape, lambda i: (0, 0)) for weight in weights]
    part = (2 * length // size, half)
    return pl.pallas_call(
        functools.partial(row_kernel, len(weights)),
        grid=(1,),
        out_shape=[shaped(part)] * size,
        in_specs=[pl.BlockSpec(own.shape, lambda i: (0, 0))] * 2 + specs,
        out_specs=[pl.BlockSpec(part, lambda i: (0, 0))] * size,
        compiler_params=pltpu.CompilerParams(vmem_limit_bytes=24 * 2**20),
        cost_estimate=pl.CostEstimate(
            flops=4 * length * width * half, bytes_accessed=moved, transcendentals=0
        ),
    )(own, other, *weights)


def finish_kernel(count, share, *refs):
    total = refs[0][...].astype(jnp.float32)
    for part in refs[1:count]:
        total = total + part[...].astype(jnp.float32)
    total = total * share
    query_out, kv_out = refs[count:]
    width = query_out.shape[1]
    query_out[...] = total[:, :width]
    kv_out[...] = total[:, width:]


def finish(parts, query_width, share):
    block, width = parts[0].shape
    step = min(block, 256)

    def spec(columns):
        return pl.BlockSpec((step, columns), lambda i: (i, 0))

    return pl.pallas_call(
        functools.partial(finish_kernel, len(parts), share),
        grid=(block // step,),
        out_shape=[
            shaped((block, query_width), jnp.float32),
            shaped((block, width - query_width), jnp.float32),
        ],
        in_specs=[spec(width)] * len(parts),
        out_specs=[spec(query_width), spec(width - query_width)],
        compiler_params=pltpu.CompilerParams(vmem_limit_bytes=32 * 2**20),
        cost_estimate=pl.CostEstimate(
            flops=0, bytes_accessed=(2 * len(parts) + 4) * block * width, transcendentals=0
        ),
    )(*parts)


def input_kernel(count, block, place, tokens, gain, grad_out, handed, *refs):
    parts, out, gathered = refs[:count], refs[count], refs[count + 1]
    rows = tokens.shape[0]
    core = place[1]
    total = parts[0][:rows].astype(jnp.float32)
    for part in parts[1:]:
        total = total + part[:rows].astype(jnp.float32)
    for k in range(total.shape[1] // block):
        columns = slice(k * block, (k + 1) * block)
        gathered[:, pl.ds(column_start(place, k, core, block), block)] = total[:, columns]
        gathered[:, pl.ds(column_start(place, k, 1 - core, block), block)] = handed[
            :, columns
        ].astype(jnp.float32)
    values = tokens[...].astype(jnp.float32)
    root_mean = jnp.sqrt(jnp.mean(values * values, axis=-1, keepdims=True) + epsilon)
    unit = values / root_mean
    scaled = gathered[...] * gain[...].astype(jnp.float32)
    correction = unit * jnp.mean(scaled * unit, axis=-1, keepdims=True)
    out[...] = (grad_out[...].astype(jnp.float32) + (scaled - correction) / root_mean).astype(
        jnp.bfloat16
    )


def local(tokens, norm_gain, query_weight, kv_weight, out_weight, grad_out, doc_lengths):
    tensor_size = lax.axis_size("tensor")
    data_size = lax.axis_size("dp")
    tensor_index = lax.axis_index("tensor")
    data_index = lax.axis_index("dp")
    chips = data_size // 2
    place = jnp.stack([data_index >> 1, data_index & 1, tensor_index]).astype(jnp.int32)
    sharers = tensor_size // KVH
    levels = sharers.bit_length() - 1
    rows, width = tokens.shape
    block = width // data_size
    query_width = query_weight.shape[1]
    gain = norm_gain.reshape(1, width)

    grad_keep, normed_keep, send = call(
        functools.partial(prepare_kernel, block),
        [shaped((rows, width // 2))] * 2 + [shaped((2 * rows, width // 2))],
        [grad_out, tokens, gain],
        [place],
        [pltpu.VMEM((rows, width), jnp.bfloat16)],
    )
    joint_width = query_width + kv_weight.shape[1]
    send, out_weight, query_weight, kv_weight = tied(send, out_weight, query_weight, kv_weight)
    sent = swap(send, "dp", 1)
    (merged,) = call(
        merge_kernel,
        [shaped((block, joint_width + out_weight.shape[0]))],
        [query_weight, kv_weight, out_weight],
    )
    early, parts = gather_near(merged)
    late = gather_far(parts)
    grad_pieces = gather_tensor(jnp.concatenate([grad_keep, sent[:rows]], axis=0))
    normed_pieces = gather_tensor(
        jnp.concatenate([normed_keep, sent[rows:]], axis=0), (*parts, *grad_pieces[3:4])
    )
    own, sent, normed = project(
        place, grad_pieces, normed_pieces, early, late, tensor_size, joint_width
    )
    sent = swap(sent, "dp", 1)
    if levels:
        joined = (own + sent.astype(jnp.float32)).astype(jnp.bfloat16)
        keyvals = joined[:, query_width:joint_width]
        for bit_index in range(levels):
            partner = swap(keyvals, "tensor", 2**bit_index)
            upper = tensor_index >> bit_index & 1 == 1
            keyvals = jnp.concatenate(
                [jnp.where(upper, partner, keyvals), jnp.where(upper, keyvals, partner)], axis=1
            )
        own = jnp.concatenate(
            [joined[:, :query_width], keyvals, joined[:, joint_width:]], axis=1
        ).astype(jnp.float32)
        sent = jnp.zeros(own.shape, jnp.bfloat16)
    combined, *partial = attention(place, doc_lengths, own, sent, rows, query_width, levels > 0)
    if levels:
        kv_partial = partial[0]
        for bit_index in reversed(range(levels)):
            half_cols = kv_partial.shape[1] // 2
            upper = tensor_index >> bit_index & 1 == 1
            lower_cols = kv_partial[:, :half_cols]
            higher_cols = kv_partial[:, half_cols:]
            kept = jnp.where(upper, higher_cols, lower_cols)
            handed = jnp.where(upper, lower_cols, higher_cols)
            kv_partial = kept + swap(handed.astype(jnp.bfloat16), "tensor", 2**bit_index).astype(
                jnp.float32
            )
        combined = jnp.concatenate([combined, kv_partial.astype(jnp.bfloat16)], axis=1)
    other = swap(combined, "dp", 1)

    far = weight_terms(normed, combined, other, chips - 1, 1, block)
    near = weight_terms(normed, combined, other, 0, chips - 1, block)
    row_parts = scatter_tensor(row_terms(combined, other, early + late, tensor_size))
    weight_parts = scatter_chips([*near, *far])
    handed = sum(part[rows:].astype(jnp.float32) for part in row_parts).astype(jnp.bfloat16)
    handed = swap(handed, "dp", 1)
    query_grad, kv_grad = finish(weight_parts, query_width, 1 / data_size)
    handed, query_grad, kv_grad = tied(handed, query_grad, kv_grad)
    (input_grad,) = call(
        functools.partial(input_kernel, len(row_parts), block),
        [shaped((rows, width))],
        [tokens, gain, grad_out, handed, *row_parts],
        [place],
        [pltpu.VMEM((rows, width), jnp.float32)],
    )
    return (input_grad, query_grad, kv_grad)


def solution(mesh):
    placed = (
        P(("dp", "tensor"), None),
        P(),
        P("dp", "tensor"),
        P("dp", "tensor"),
        P("tensor", "dp"),
        P(("dp", "tensor"), None),
        P("dp", None),
    )
    return jax.shard_map(
        local,
        mesh=mesh,
        in_specs=placed,
        out_specs=(P(("dp", "tensor"), None), P("dp", "tensor"), P("dp", "tensor")),
        check_vma=False,
    )
```

```python
import functools
import math

import jax
import jax.numpy as jnp
from jax import lax
from jax.experimental import pallas as pl
from jax.experimental.pallas import tpu as pltpu
from jax.sharding import PartitionSpec as P

KVH = 4
HD = 128

epsilon = 1e-05
CONTRACT_LAST = (((1,), (1,)), ((), ()))
CONTRACT_FIRST = (((0,), (0,)), ((), ()))
WHOLE = pl.BlockSpec(memory_space=pltpu.VMEM)
SCALARS = pl.BlockSpec(memory_space=pltpu.SMEM)


def call(kernel, outs, operands, scalars=(), scratch=(), flops=0, megabytes=24):
    moved = sum(math.prod(a.shape) * a.dtype.itemsize for a in (*operands, *outs))
    return pl.pallas_call(
        kernel,
        out_shape=outs,
        in_specs=[SCALARS] * len(scalars) + [WHOLE] * len(operands),
        out_specs=[WHOLE] * len(outs),
        scratch_shapes=scratch,
        compiler_params=pltpu.CompilerParams(vmem_limit_bytes=megabytes * 2**20),
        cost_estimate=pl.CostEstimate(flops=flops, bytes_accessed=moved, transcendentals=0),
    )(*scalars, *operands)


def shaped(shape, dtype=jnp.bfloat16):
    return jax.ShapeDtypeStruct(shape, dtype)


def dot(left, right, contract=(((1,), (0,)), ((), ()))):
    return lax.dot_general(left, right, contract, preferred_element_type=jnp.float32)


def swap(value, axis, mask):
    pairs = [(source, source ^ mask) for source in range(lax.axis_size(axis))]
    return lax.ppermute(value, axis, pairs)


def tied(*values):
    return lax.optimization_barrier(values)


def everyone(value, axis, unit):
    size = lax.axis_size(axis) // unit
    return [value] + [swap(value, axis, unit * k) for k in range(1, size)]


def gather_chips(value):
    if lax.axis_size("dp") != 8:
        return everyone(value, "dp", 2), []
    half = value.shape[0] // 2
    near_x = swap(value, "dp", 2)
    near_y = swap(value, "dp", 4)
    near_x, near_y = tied(near_x, near_y)
    far_top = swap(near_x[:half], "dp", 4)
    far_bottom = swap(near_y[half:], "dp", 2)
    return [value, near_x, near_y], [far_top, far_bottom]


def along(value, pairs):
    return lax.ppermute(value, "tensor", pairs)


def gather_tensor(value):
    if lax.axis_size("tensor") != 4:
        return everyone(value, "tensor", 1)
    right_one = along(value, [(0, 1), (1, 2), (2, 3)])
    left_one = along(value, [(1, 0), (2, 1), (3, 2)])
    right_one, left_one = tied(right_one, left_one)
    right_two = along(right_one, [(1, 2), (2, 3)])
    left_two = along(left_one, [(1, 0), (2, 1)])
    right_two, left_two = tied(right_two, left_two)
    last = along(
        jnp.where(lax.axis_index("tensor") == 1, left_two, right_two), [(1, 0), (2, 3)]
    )
    return [value, right_one, left_one, right_two, left_two, last]


def pick(index, pieces, size, k, rows):
    if len(pieces) == size:
        return pieces[k][rows]
    own, right_one, left_one, right_two, left_two, last = [piece.at[rows] for piece in pieces]
    if k == 0:
        return own[...]
    if k == 1:
        return jnp.where(index % 2 == 1, right_one[...], left_one[...])
    if k == 2:
        return jnp.where(index >= 2, right_two[...], left_two[...])
    near = jnp.where(index == 1, left_one[...], right_one[...])
    return jnp.where(jnp.logical_or(index == 0, index == 3), last[...], near)


def inner_pair(value):
    return along(value, [(1, 2), (2, 1)])


def outer_pair(value):
    return along(value, [(3, 2), (0, 1)])


def scatter_chips(blocks):
    if len(blocks) != 4:
        return [blocks[0]] + [swap(blocks[k], "dp", 2 * k) for k in range(1, len(blocks))]
    half = blocks[0].shape[0] // 2
    far_top = swap(blocks[3][:half], "dp", 4)
    far_bottom = swap(blocks[3][half:], "dp", 2)
    near_x = swap(
        jnp.concatenate([blocks[1][:half] + far_top, blocks[1][half:]], axis=0), "dp", 2
    )
    near_y = swap(
        jnp.concatenate([blocks[2][:half], blocks[2][half:] + far_bottom], axis=0), "dp", 4
    )
    return [blocks[0], near_x, near_y]


def scatter_tensor(blocks):
    if len(blocks) != 4:
        return [blocks[0]] + [swap(blocks[k], "tensor", k) for k in range(1, len(blocks))]
    outer, inner = outer_pair(blocks[3]), inner_pair(blocks[3])
    outer, inner = tied(outer, inner)
    carried, adjacent = tied(blocks[2] + outer, blocks[1])
    two, one = swap(carried, "tensor", 2), swap(adjacent, "tensor", 1)
    return [blocks[0], one, inner, two]


def column_start(place, k, which, block):
    return pl.multiple_of(((place[0] ^ k) * 2 + which) * block, 128)


def prepare_kernel(block, place, grad_out, tokens, gain, grad_keep, normed_keep, send, normed):
    rows, core = tokens.shape[0], place[1]
    values = tokens[...].astype(jnp.float32)
    root_mean = jnp.sqrt(jnp.mean(values * values, axis=-1, keepdims=True) + epsilon)
    normed[...] = (values / root_mean * gain[...].astype(jnp.float32)).astype(jnp.bfloat16)
    for start, source, keep in ((0, grad_out, grad_keep), (rows, normed, normed_keep)):
        for k in range(keep.shape[1] // block):
            columns = slice(k * block, (k + 1) * block)
            keep[:, columns] = source[:, pl.ds(column_start(place, k, core, block), block)]
            send[start : start + rows, columns] = source[
                :, pl.ds(column_start(place, k, 1 - core, block), block)
            ]


def merge_kernel(query_weight, kv_weight, out_weight, merged):
    block, start = merged.shape[0], 0
    parts = [query_weight, kv_weight]
    parts += [out_weight.at[k : k + block] for k in range(0, out_weight.shape[0], block)]
    for part in parts:
        merged[:, start : start + part.shape[1]] = part[...]
        start += part.shape[1]


def products(grads, normed, weights, first, joint_width, block, columns):
    size = weights[0].shape[0]
    if columns < joint_width:
        width = min(256, joint_width - columns)
        total = None
        for k, weight in enumerate(weights):
            left = normed[:, first + k * size : first + (k + 1) * size]
            term = dot(left, weight[:, columns : columns + width])
            total = term if total is None else total + term
        yield slice(columns, columns + width), total
        return
    for row in range(0, block, min(size, 256)):
        place_out = slice(columns + row, columns + row + min(size, 256))
        total = None
        if size == block:
            for k, weight in enumerate(weights):
                right = weight[row : row + min(size, 256), columns : columns + block]
                left = grads[:, first + k * block : first + (k + 1) * block]
                term = dot(left, right, CONTRACT_LAST)
                total = term if total is None else total + term
        else:
            right = weights[row // size][:, columns : columns + block]
            total = dot(grads[:, first : first + block], right, CONTRACT_LAST)
        yield place_out, total


def column_steps(joint_width, width, block):
    return [*range(0, joint_width, 256), *range(joint_width, width, block)]


def early_kernel(pieces, weights, size, joint_width, place, *refs):
    row_refs, weight_refs = refs[:pieces], refs[pieces : pieces + weights]
    total, grads, normed = refs[pieces + weights :]
    rows = row_refs[0].shape[0] // 2
    block = weight_refs[0].shape[0]
    halves = row_refs[: pieces // 2], row_refs[pieces // 2 :]
    for pair, gathered in zip((grads, normed), halves):
        for core in range(2):
            for k in range(size):
                target = (core * size + k) * rows
                pair[target : target + rows] = pick(
                    place[2], gathered, size, k, slice(core * rows, (core + 1) * rows)
                )
    for columns in column_steps(joint_width, total.shape[1], block):
        for place_out, value in products(grads, normed, weight_refs, 0, joint_width, block, columns):
            total[:, place_out] = value


def late_kernel(first, joint_width, block, total, grads, normed, *refs):
    weight_refs, (keep, send) = refs[:-2], refs[-2:]
    length = keep.shape[0]
    if not weight_refs:
        keep[...] = total[:length]
        send[...] = total[length:].astype(jnp.bfloat16)
    for columns in column_steps(joint_width, keep.shape[1], block) if weight_refs else []:
        for place_out, value in products(
            grads, normed, weight_refs, first, joint_width, block, columns
        ):
            keep[:, place_out] = total[:length, place_out] + value[:length]
            send[:, place_out] = (total[length:, place_out] + value[length:]).astype(jnp.bfloat16)


def project(place, pieces, early, late, size, joint_width):
    rows = pieces[0].shape[0] // 2 * size
    half = pieces[0].shape[1]
    block, width = early[0].shape
    first = len(early) * block
    total, grads, normed = call(
        functools.partial(early_kernel, len(pieces), len(early), size, joint_width),
        [shaped((2 * rows, width), jnp.float32)] + [shaped((2 * rows, half))] * 2,
        [*pieces, *early],
        [place],
        flops=4 * rows * first * width,
        megabytes=24,
    )
    own, sent = call(
        functools.partial(late_kernel, first, joint_width, block),
        [shaped((rows, width), jnp.float32), shaped((rows, width))],
        [total, grads, normed, *late],
        flops=4 * rows * (half - first) * width,
        megabytes=24,
    )
    return own, sent, normed


def attention_kernel(rows, heads, place, lengths, own, sent, grads, partial):
    length = own.shape[0]
    width = heads * HD
    scale = 1 / math.sqrt(HD)
    tensor_index = place[2]

    def positions_of(dimension):
        order = lax.broadcasted_iota(jnp.int32, (length, length), dimension)
        return ((order // rows) ^ tensor_index) * rows + order % rows

    def labels_of(positions):
        labels, end = jnp.zeros((length, length), jnp.int32), 0
        for document in range(lengths.shape[1]):
            end = end + lengths[0, document]
            labels = labels + (end <= positions).astype(jnp.int32)
        return labels

    key_positions, query_positions = positions_of(0), positions_of(1)
    allowed = jnp.logical_and(
        labels_of(key_positions) == labels_of(query_positions), key_positions <= query_positions
    )

    def joined(first, second, columns):
        return (first[:, columns] + second[:, columns].astype(jnp.float32)).astype(jnp.bfloat16)

    keys = joined(own, sent, slice(width, width + HD))
    values = joined(own, sent, slice(width + HD, width + 2 * HD))
    key_total = value_total = None
    for head in range(heads):
        columns = slice(head * HD, (head + 1) * HD)
        start = width + 2 * HD + head * HD
        queries = joined(own, sent, columns)
        out_grad = joined(own, sent, slice(start, start + HD))
        scores = jnp.where(allowed, dot(keys, queries, CONTRACT_LAST) * scale, -1e30)
        expo = jnp.exp(scores - jnp.max(scores, axis=0, keepdims=True))
        probs = expo * (1 / jnp.sum(expo, axis=0, keepdims=True))
        prob_grad = dot(values, out_grad, CONTRACT_LAST)
        inner = jnp.sum(probs * prob_grad, axis=0, keepdims=True)
        score_grad = (probs * (prob_grad - inner) * scale).astype(jnp.bfloat16)
        grads[:, columns] = dot(score_grad, keys, CONTRACT_FIRST).astype(jnp.bfloat16)
        key_term = dot(score_grad, queries)
        value_term = dot(probs.astype(jnp.bfloat16), out_grad)
        key_total = key_term if head == 0 else key_total + key_term
        value_total = value_term if head == 0 else value_total + value_term
    if partial is None:
        grads[:, width : width + HD] = key_total.astype(jnp.bfloat16)
        grads[:, width + HD :] = value_total.astype(jnp.bfloat16)
    else:
        partial[:, :HD] = key_total
        partial[:, HD:] = value_total


def attention(place, lengths, own, sent, rows, width, split):
    length = own.shape[0]
    outs = [shaped((length, width if split else width + 2 * HD))]
    if split:
        outs.append(shaped((length, 2 * HD), jnp.float32))

    def kernel(*refs):
        attention_kernel(rows, width // HD, *(refs if split else (*refs, None)))

    return call(
        kernel,
        outs,
        [own, sent],
        [place, lengths],
        flops=10 * length * length * width,
    )


def weight_kernel(first, block, pair, own, other, *outs):
    length = own.shape[0]
    tile = min(block, 256)
    for number, out in enumerate(outs):
        for part in range(block // tile):
            start = (first + number) * block + part * tile
            out[part * tile : (part + 1) * tile] = (
                dot(pair[:length, start : start + tile], own[...], CONTRACT_FIRST)
                + dot(pair[length:, start : start + tile], other[...], CONTRACT_FIRST)
            ).astype(jnp.bfloat16)


def weight_terms(pair, own, other, first, count, block):
    return call(
        functools.partial(weight_kernel, first, block),
        [shaped((block, own.shape[1]))] * count,
        [pair, own, other],
        flops=2 * pair.shape[0] * block * count * own.shape[1],
    )


def row_kernel(weights, own, other, *refs):
    weight_refs, outs = refs[:weights], refs[weights:]
    length = own.shape[0]
    rows = length // len(outs)
    start = 0
    for weight in weight_refs:
        tile = min(weight.shape[0], 256)
        for part in range(weight.shape[0] // tile):
            right = weight[part * tile : (part + 1) * tile]
            for offset, left in ((0, own), (rows, other)):
                term = dot(left[...], right, CONTRACT_LAST).astype(jnp.bfloat16)
                for k, out in enumerate(outs):
                    out[offset : offset + rows, start : start + tile] = term[
                        k * rows : (k + 1) * rows
                    ]
            start += tile


def row_terms(own, other, weights, size):
    length, width = own.shape
    half = sum(weight.shape[0] for weight in weights)
    moved = sum(2 * weight.shape[0] * width for weight in weights) + 4 * length * (width + half)
    if width % 128 == 0:
        specs = [pl.BlockSpec((weight.shape[0], width), lambda i: (0, 0)) for weight in weights]
    else:
        weights = [weight[:, :width] for weight in weights]
        specs = [pl.BlockSpec(weight.shape, lambda i: (0, 0)) for weight in weights]
    part = (2 * length // size, half)
    return pl.pallas_call(
        functools.partial(row_kernel, len(weights)),
        grid=(1,),
        out_shape=[shaped(part)] * size,
        in_specs=[pl.BlockSpec(own.shape, lambda i: (0, 0))] * 2 + specs,
        out_specs=[pl.BlockSpec(part, lambda i: (0, 0))] * size,
        compiler_params=pltpu.CompilerParams(vmem_limit_bytes=24 * 2**20),
        cost_estimate=pl.CostEstimate(
            flops=4 * length * width * half, bytes_accessed=moved, transcendentals=0
        ),
    )(own, other, *weights)


def finish_kernel(count, share, *refs):
    total = refs[0][...].astype(jnp.float32)
    for part in refs[1:count]:
        total = total + part[...].astype(jnp.float32)
    total = total * share
    query_out, kv_out = refs[count:]
    width = query_out.shape[1]
    query_out[...] = total[:, :width]
    kv_out[...] = total[:, width:]


def finish(parts, query_width, share):
    block, width = parts[0].shape
    step = min(block, 256)

    def spec(columns):
        return pl.BlockSpec((step, columns), lambda i: (i, 0))

    return pl.pallas_call(
        functools.partial(finish_kernel, len(parts), share),
        grid=(block // step,),
        out_shape=[
            shaped((block, query_width), jnp.float32),
            shaped((block, width - query_width), jnp.float32),
        ],
        in_specs=[spec(width)] * len(parts),
        out_specs=[spec(query_width), spec(width - query_width)],
        compiler_params=pltpu.CompilerParams(vmem_limit_bytes=32 * 2**20),
        cost_estimate=pl.CostEstimate(
            flops=0, bytes_accessed=(2 * len(parts) + 4) * block * width, transcendentals=0
        ),
    )(*parts)


def input_kernel(count, block, place, tokens, gain, grad_out, handed, *refs):
    parts, out, gathered = refs[:count], refs[count], refs[count + 1]
    rows = tokens.shape[0]
    core = place[1]
    total = parts[0][:rows].astype(jnp.float32)
    for part in parts[1:]:
        total = total + part[:rows].astype(jnp.float32)
    for k in range(total.shape[1] // block):
        columns = slice(k * block, (k + 1) * block)
        gathered[:, pl.ds(column_start(place, k, core, block), block)] = total[:, columns]
        gathered[:, pl.ds(column_start(place, k, 1 - core, block), block)] = handed[
            :, columns
        ].astype(jnp.float32)
    values = tokens[...].astype(jnp.float32)
    root_mean = jnp.sqrt(jnp.mean(values * values, axis=-1, keepdims=True) + epsilon)
    unit = values / root_mean
    scaled = gathered[...] * gain[...].astype(jnp.float32)
    correction = unit * jnp.mean(scaled * unit, axis=-1, keepdims=True)
    out[...] = (grad_out[...].astype(jnp.float32) + (scaled - correction) / root_mean).astype(
        jnp.bfloat16
    )


def local(tokens, norm_gain, query_weight, kv_weight, out_weight, grad_out, doc_lengths):
    tensor_size = lax.axis_size("tensor")
    data_size = lax.axis_size("dp")
    tensor_index = lax.axis_index("tensor")
    data_index = lax.axis_index("dp")
    chips = data_size // 2
    place = jnp.stack([data_index >> 1, data_index & 1, tensor_index]).astype(jnp.int32)
    sharers = tensor_size // KVH
    levels = sharers.bit_length() - 1
    rows, width = tokens.shape
    block = width // data_size
    query_width = query_weight.shape[1]
    gain = norm_gain.reshape(1, width)

    grad_keep, normed_keep, send = call(
        functools.partial(prepare_kernel, block),
        [shaped((rows, width // 2))] * 2 + [shaped((2 * rows, width // 2))],
        [grad_out, tokens, gain],
        [place],
        [pltpu.VMEM((rows, width), jnp.bfloat16)],
    )
    joint_width = query_width + kv_weight.shape[1]
    send, out_weight, query_weight, kv_weight = tied(send, out_weight, query_weight, kv_weight)
    sent = swap(send, "dp", 1)
    (merged,) = call(
        merge_kernel,
        [shaped((block, joint_width + out_weight.shape[0]))],
        [query_weight, kv_weight, out_weight],
    )
    early, late = gather_chips(merged)
    row_pieces = gather_tensor(jnp.concatenate([grad_keep, sent[:rows]], axis=0))
    row_pieces += gather_tensor(jnp.concatenate([normed_keep, sent[rows:]], axis=0))
    own, sent, normed = project(place, row_pieces, early, late, tensor_size, joint_width)
    sent = swap(sent, "dp", 1)
    if levels:
        joined = (own + sent.astype(jnp.float32)).astype(jnp.bfloat16)
        keyvals = joined[:, query_width:joint_width]
        for bit_index in range(levels):
            partner = swap(keyvals, "tensor", 2**bit_index)
            upper = tensor_index >> bit_index & 1 == 1
            keyvals = jnp.concatenate(
                [jnp.where(upper, partner, keyvals), jnp.where(upper, keyvals, partner)], axis=1
            )
        own = jnp.concatenate(
            [joined[:, :query_width], keyvals, joined[:, joint_width:]], axis=1
        ).astype(jnp.float32)
        sent = jnp.zeros(own.shape, jnp.bfloat16)
    combined, *partial = attention(place, doc_lengths, own, sent, rows, query_width, levels > 0)
    if levels:
        kv_partial = partial[0]
        for bit_index in reversed(range(levels)):
            half_cols = kv_partial.shape[1] // 2
            upper = tensor_index >> bit_index & 1 == 1
            lower_cols = kv_partial[:, :half_cols]
            higher_cols = kv_partial[:, half_cols:]
            kept = jnp.where(upper, higher_cols, lower_cols)
            handed = jnp.where(upper, lower_cols, higher_cols)
            kv_partial = kept + swap(handed.astype(jnp.bfloat16), "tensor", 2**bit_index).astype(
                jnp.float32
            )
        combined = jnp.concatenate([combined, kv_partial.astype(jnp.bfloat16)], axis=1)
    other = swap(combined, "dp", 1)

    far = weight_terms(normed, combined, other, chips - 1, 1, block)
    near = weight_terms(normed, combined, other, 0, chips - 1, block)
    row_parts = scatter_tensor(row_terms(combined, other, early + late, tensor_size))
    weight_parts = scatter_chips([*near, *far])
    handed = sum(part[rows:].astype(jnp.float32) for part in row_parts).astype(jnp.bfloat16)
    handed = swap(handed, "dp", 1)
    query_grad, kv_grad = finish(weight_parts, query_width, 1 / data_size)
    handed, query_grad, kv_grad = tied(handed, query_grad, kv_grad)
    (input_grad,) = call(
        functools.partial(input_kernel, len(row_parts), block),
        [shaped((rows, width))],
        [tokens, gain, grad_out, handed, *row_parts],
        [place],
        [pltpu.VMEM((rows, width), jnp.float32)],
    )
    return (input_grad, query_grad, kv_grad)


def solution(mesh):
    placed = (
        P(("dp", "tensor"), None),
        P(),
        P("dp", "tensor"),
        P("dp", "tensor"),
        P("tensor", "dp"),
        P(("dp", "tensor"), None),
        P("dp", None),
    )
    return jax.shard_map(
        local,
        mesh=mesh,
        in_specs=placed,
        out_specs=(P(("dp", "tensor"), None), P("dp", "tensor"), P("dp", "tensor")),
        check_vma=False,
    )
```
